32 devices in a mesh: dp: 8 (over y, x, core), tensor: 4 (over z).
Axes of the slice: x: 2, y: 2, z: 4, core: 2. Of those that a mesh axis runs over, the one named last changes fastest.
Arguments:
- tokens: bfloat16 [5120, 2048], P('dp'), may hold values from -6 to 6
- w_query: bfloat16 [2048, 2048], P(None, 'tensor'), may hold values from -0.125 to 0.125
- w_key: bfloat16 [2048, 2048], P(None, 'tensor'), may hold values from -0.125 to 0.125
- w_value: bfloat16 [2048, 2048], P(None, 'tensor'), may hold values from -0.125 to 0.125
- w_out: bfloat16 [2048, 2048], P('tensor'), may hold values from -2 to 2
- w_gate: bfloat16 [2048, 8192], P(None, 'tensor'), may hold values from -0.125 to 0.125
- w_up: bfloat16 [2048, 8192], P(None, 'tensor'), may hold values from -0.125 to 0.125
- w_down: bfloat16 [8192, 2048], P('tensor'), may hold values from -0.125 to 0.125
- cotangent: bfloat16 [5120, 2048], P('dp'), may hold values from -6 to 6
- slot_parent: int32 [40], replicated, may hold values from -1 to 39, as said below
Outputs:
- output: bfloat16 [5120, 2048], P('dp')
- grad_tokens: bfloat16 [5120, 2048], P('dp')
- grad_query: float32 [2048, 2048], P('dp', 'tensor')
- grad_key: float32 [2048, 2048], P('dp', 'tensor')
- grad_value: float32 [2048, 2048], P('dp', 'tensor')
- grad_out: float32 [2048, 2048], P('tensor', 'dp')
- grad_gate: float32 [2048, 8192], P('dp', 'tensor')
- grad_up: float32 [2048, 8192], P('dp', 'tensor')
- grad_down: float32 [8192, 2048], P('tensor', 'dp')
The draws below stay inside these ranges and needn't reach their ends.
Inputs may be any that keep to these rules, and one draw needn't show every extreme that they name: `slot_parent`: the pack holds 2 trees of 8 + 4 * (3) blocks: a trunk of 8 blocks in a chain (its first block's entry is -1, each later one names the one before), 4 branch blocks whose parent is the trunk's last block, and 2 leaf blocks under each branch. Every slot holds one block; slot s lies on index s // 5 of dp.
All inputs are finite; a program needn't handle non-finite values.
Results may differ from the reference program's by a relative error of at most 0.024.
Values may be sent and summed in bfloat16 or wider, within the bound.
No kernel may reach another device: no remote copies, remote signals or barrier semaphores. Data moves between devices by JAX's collectives and lax.ppermute only.
A program may use at most 256 MiB of HBM per device.

```python
import math
import jax
import jax.numpy as jnp
from jax import lax

D = 2048
HEADS = 16
HEAD = 128
FF = 8192
BLOCK = 128
TRUNK_BLOCKS = 8
BRANCHES = 4
LEAVES = 2
SLOTS = 5
NBLK = 40
TOKENS = 5120
TREES = 2


def draw_slot_parent(key, part):
    key = jax.random.fold_in(key, 7)
    tree_size = TRUNK_BLOCKS + BRANCHES * (1 + LEAVES)
    placing = jax.random.permutation(key, NBLK).astype(jnp.int32)
    chosen = jax.random.randint(jax.random.fold_in(key, 1), (), 0, TREES).astype(jnp.int32)
    tree_start = chosen * tree_size
    targets = [(tree_start + TRUNK_BLOCKS + BRANCHES, 0), (tree_start + tree_size - 1, NBLK - 1), (tree_start + TRUNK_BLOCKS + 1, NBLK // SLOTS // 2 * SLOTS)]
    for block_id, target_slot in targets:
        holder = jnp.argmax(placing == target_slot).astype(jnp.int32)
        previous = placing[block_id]
        placing = placing.at[holder].set(previous)
        placing = placing.at[block_id].set(target_slot)
    block_ids = jnp.arange(NBLK, dtype=jnp.int32)
    within = block_ids % tree_size
    first_of_tree = block_ids - within
    parent_within = jnp.where(within < TRUNK_BLOCKS, within - 1, jnp.where(within < TRUNK_BLOCKS + BRANCHES, TRUNK_BLOCKS - 1, TRUNK_BLOCKS + (within - TRUNK_BLOCKS - BRANCHES) // LEAVES))
    parent_block = jnp.clip(first_of_tree + parent_within, 0, NBLK - 1)
    parent_place = jnp.where(parent_within >= 0, placing[parent_block], -1).astype(jnp.int32)
    return jnp.zeros((NBLK,), jnp.int32).at[placing].set(parent_place)


def levels(own_key, extent, split, smallest, top_value):
    factor_of, own = 1.0, jax.random.fold_in(own_key, 6)
    for axis_at, parts in split:
        heights = jnp.exp(jax.random.uniform(jax.random.fold_in(own, axis_at), (parts,), jnp.float32, smallest / len(split), top_value / len(split)))
        factor_of = factor_of * jnp.repeat(heights, extent[axis_at] // parts).reshape([-1 if axis == axis_at else 1 for axis in range(len(extent))])
    return factor_of


def bell_draw(key, dims, scale, reach, cuts=(), held_as=jnp.bfloat16):
    entries = jax.random.normal(key, dims, jnp.float32) * scale
    if len(cuts) > 0:
        entries = levels(key, dims, cuts, -0.22, 0.18) * entries
    return jnp.clip(entries, min=-reach, max=reach).astype(held_as)


def setup_inputs(seed: int = 0) -> dict:
    seeds = jax.random.split(jax.random.key(seed), 11)
    tokens = bell_draw(seeds[0], (TOKENS, D), 1.0, 6.0, ((0, 8),))
    w_query = bell_draw(seeds[1], (D, HEADS * HEAD), D ** -0.5, 0.125, ((1, 4),))
    w_key = bell_draw(seeds[2], (D, HEADS * HEAD), D ** -0.5, 0.125, ((1, 4),))
    w_value = bell_draw(seeds[3], (D, HEADS * HEAD), D ** -0.5, 0.125, ((1, 4),))
    w_out = bell_draw(seeds[4], (HEADS * HEAD, D), (HEADS * HEAD * 4 // (TRUNK_BLOCKS * BLOCK)) ** -0.5, 2.0, ((0, 4),))
    w_gate = bell_draw(seeds[5], (D, FF), D ** -0.5, 0.125, ((1, 4),))
    w_up = bell_draw(seeds[6], (D, FF), D ** -0.5, 0.125, ((1, 4),))
    w_down = bell_draw(seeds[7], (FF, D), (FF // 4) ** -0.5, 0.125, ((0, 4),))
    cotangent = bell_draw(seeds[8], (TOKENS, D), 1.0, 6.0, ((0, 8),))
    slot_parent = draw_slot_parent(jax.random.fold_in(seeds[10], 71), 0)
    return dict(tokens=tokens, w_query=w_query, w_key=w_key, w_value=w_value, w_out=w_out, w_gate=w_gate, w_up=w_up, w_down=w_down, cotangent=cotangent, slot_parent=slot_parent)


@jax.custom_vjp
def low(v):
    return lax.optimization_barrier(v.astype(jnp.bfloat16)).astype(jnp.float32)

@jax.custom_vjp
def low_back(v):
    return v

def low_keep(v):
    return (low(v), None)

def low_pass(kept, grad):
    return (grad,)

def back_keep(v):
    return (v, None)

def back_low(kept, grad):
    return (low(grad),)
low.defvjp(low_keep, low_pass)
low_back.defvjp(back_keep, back_low)
EPSILON = 1e-05
NEGATIVE = -1e+30
HIGH = lax.Precision.HIGHEST

def layer_norm(values):
    centered = values - lax.optimization_barrier(jnp.mean(values, axis=-1, keepdims=True))
    variance = lax.optimization_barrier(jnp.mean(centered * centered, axis=-1, keepdims=True))
    return centered * lax.rsqrt(variance + EPSILON)

def ancestry_matrix(slot_parent):
    block_count = slot_parent.shape[0]
    block_ids = jnp.arange(block_count, dtype=jnp.int32)
    current = slot_parent.astype(jnp.int32)
    reaches = jnp.zeros((block_count, block_count), jnp.float32)
    for rounds in range(TRUNK_BLOCKS + 2):
        reaches = reaches + (current[:, None] == block_ids[None, :]).astype(jnp.float32)
        safe_index = jnp.clip(current, 0, block_count - 1).astype(jnp.int32)
        current = jnp.where(current >= 0, slot_parent[safe_index], -1).astype(jnp.int32)
    return reaches

def rope_tables(positions):
    frequency = jnp.exp(jnp.arange(HEAD // 2, dtype=jnp.float32) * (-2.0 * math.log(10000.0) / HEAD))
    angle_grid = positions[:, None] * frequency[None, :]
    return (jnp.cos(angle_grid), jnp.sin(angle_grid))

def rotate(values, cosine_table, sine_table):
    shaped = values.reshape(values.shape[0], -1, 2, HEAD // 2)
    first_half = shaped[:, :, 0, :]
    second = shaped[:, :, 1, :]
    cosine_wide = cosine_table[:, None, :]
    sine_wide = sine_table[:, None, :]
    turned = jnp.stack([first_half * cosine_wide - second * sine_wide, second * cosine_wide + first_half * sine_wide], axis=2)
    return turned.reshape(values.shape)

def forward(tokens, w_query, w_key, w_value, w_out, w_gate, w_up, w_down, reaches, cosine_table, sine_table):
    row_count = tokens.shape[0]
    normed_one = low(layer_norm(tokens))
    queries = low(rotate(low_back(jnp.dot(normed_one, w_query, precision=HIGH)), cosine_table, sine_table))
    key_rows = low(rotate(low_back(jnp.dot(normed_one, w_key, precision=HIGH)), cosine_table, sine_table))
    value_rows = low(low_back(jnp.dot(normed_one, w_value, precision=HIGH)))
    key_heads = key_rows.reshape(row_count, HEADS, HEAD)
    value_heads = value_rows.reshape(row_count, HEADS, HEAD)
    group_rows = 4 * BLOCK
    group_count = row_count // group_rows
    key_index = jnp.arange(row_count, dtype=jnp.int32)
    key_block = key_index // BLOCK

    def attend_group(group_index):
        group_index = group_index.astype(jnp.int32)
        query_part = lax.dynamic_slice_in_dim(queries, group_index * group_rows, group_rows, 0).reshape(group_rows, HEADS, HEAD)
        reach_rows = lax.dynamic_slice_in_dim(reaches, group_index * 4, 4, 0)
        ancestor = jnp.repeat(jnp.repeat(reach_rows, BLOCK, axis=0), BLOCK, axis=1) > 0.5
        query_index = group_index * group_rows + jnp.arange(group_rows, dtype=jnp.int32)
        same_block = (query_index[:, None] // BLOCK == key_block[None, :]) & (key_index[None, :] <= query_index[:, None])
        allowed = ancestor | same_block
        scores = jnp.einsum('qhd,khd->hqk', query_part, key_heads, precision=HIGH) * HEAD ** (-0.5)
        scores = jnp.where(allowed[None, :, :], low_back(scores), NEGATIVE)
        probability = low(jax.nn.softmax(scores, axis=-1))
        mixed = jnp.einsum('hqk,khd->qhd', probability, value_heads, precision=HIGH)
        return mixed.reshape(group_rows, HEADS * HEAD)
    attended = lax.map(jax.checkpoint(attend_group), jnp.arange(group_count, dtype=jnp.int32))
    attended = low_back(low(attended.reshape(row_count, HEADS * HEAD)))
    branch = low_back(jnp.dot(attended, w_out, precision=HIGH))
    middle = tokens + branch
    normed_two = low(layer_norm(middle))
    gate_proj = low_back(jnp.dot(normed_two, w_gate, precision=HIGH))
    up_proj = low_back(jnp.dot(normed_two, w_up, precision=HIGH))
    hidden = low(jax.nn.silu(gate_proj) * up_proj)
    return middle + jnp.dot(hidden, w_down, precision=HIGH)

def reference(tokens, w_query, w_key, w_value, w_out, w_gate, w_up, w_down, cotangent, slot_parent):
    reaches = ancestry_matrix(slot_parent)
    depths = lax.optimization_barrier(jnp.sum(reaches, axis=1))
    positions = (depths[:, None] * BLOCK + jnp.arange(BLOCK, dtype=jnp.float32)[None, :]).reshape(-1)
    cosine_table, sine_table = rope_tables(positions)
    inputs = tuple((array.astype(jnp.float32) for array in (tokens, w_query, w_key, w_value, w_out, w_gate, w_up, w_down)))

    def wrapped(*arrays):
        return forward(*arrays, reaches, cosine_table, sine_table)
    result, pullback = jax.vjp(wrapped, *inputs)
    gradients = pullback(cotangent.astype(jnp.float32))
    return (result.astype(jnp.bfloat16), gradients[0].astype(jnp.bfloat16), gradients[1], gradients[2], gradients[3], gradients[4], gradients[5], gradients[6], gradients[7])
```

```python
import functools
import math

import jax
import jax.numpy as jnp
import numpy as np
from jax import lax
from jax.experimental import pallas as pl
from jax.experimental.pallas import tpu as pltpu
from jax.sharding import PartitionSpec as P

HEAD = 128
BLOCK = 128
TRUNK_BLOCKS = 8
CHAIN = TRUNK_BLOCKS + 2
EPSILON = 1e-05
NEGATIVE = -1e30
SCALE = HEAD ** (-0.5)
LOW = jnp.bfloat16
F32 = jnp.float32
MIB = 1024 * 1024
NT = (((1,), (1,)), ((), ()))
TN = (((0,), (0,)), ((), ()))


def dot(a, b):
    return jnp.dot(a, b, preferred_element_type=F32)


def dot_nt(a, b):
    return lax.dot_general(a, b, NT, preferred_element_type=F32)


def dot_tn(a, b):
    return lax.dot_general(a, b, TN, preferred_element_type=F32)


def shape(dims, dtype):
    return jax.ShapeDtypeStruct(dims, dtype)


def params(mib):
    return pltpu.CompilerParams(vmem_limit_bytes=mib * MIB)


def layer_norm(values):
    centered = values - jnp.mean(values, axis=-1, keepdims=True)
    variance = jnp.mean(centered * centered, axis=-1, keepdims=True)
    inverse = lax.rsqrt(variance + EPSILON)
    return (centered * inverse, inverse)


def norm_back(gradient, normed, inverse):
    return inverse * (
        gradient
        - jnp.mean(gradient, axis=-1, keepdims=True)
        - normed * jnp.mean(gradient * normed, axis=-1, keepdims=True)
    )


def rope_tables():
    frequency = np.exp(
        np.arange(HEAD // 2, dtype=np.float32) * np.float32(-2.0 * math.log(10000.0) / HEAD)
    ).astype(np.float32)
    angle = np.arange(CHAIN * BLOCK, dtype=np.float32)[:, None] * frequency[None, :]
    cosine, sine = np.cos(angle), np.sin(angle)
    return (
        np.concatenate([cosine, cosine], axis=1).astype(np.float32),
        np.concatenate([-sine, sine], axis=1).astype(np.float32),
    )


def depth_of(parent_ref, slot):
    def up(_, carry):
        at, depth = carry
        parent = jnp.where(at >= 0, parent_ref[jnp.maximum(at, 0)], -1)
        return parent, depth + jnp.where(parent >= 0, 1, 0).astype(jnp.int32)

    return lax.fori_loop(0, CHAIN - 1, up, (slot, jnp.int32(0)))[1]


def xor_pairs(count, mask):
    return [(index, index ^ mask) for index in range(count)]


class Plan:
    def __init__(self, mesh, rows, width, heads, ff):
        self.dp = mesh.shape["dp"]
        self.tensor = mesh.shape["tensor"]
        self.rows, self.width, self.heads, self.ff = rows, width, heads, ff
        self.slots = rows // BLOCK
        self.spread = heads
        self.rest = self.dp // heads
        self.bits = self.dp.bit_length() - 1
        self.piece = width // self.dp
        self.own = rows // self.tensor


def qkv_kernel(plan, parent, place, x, wq, wk, wv, cosine, sine, n_rel, *rest):
    outs, normed, stage = rest[: plan.spread], rest[-2], rest[-1]
    me = place[0]
    part = me // plan.rest
    depth = depth_of(parent, me * plan.slots + pl.program_id(0))
    rows = pl.ds(pl.multiple_of(depth * BLOCK, BLOCK), BLOCK)
    cos, sin = cosine[rows, :], sine[rows, :]
    low = layer_norm(x[...].astype(F32))[0].astype(LOW)
    normed[...] = low
    for kind, w in enumerate((wq, wk, wv)):
        y = dot(low, w[...])
        for head in range(plan.heads):
            yh = y[:, head * HEAD : (head + 1) * HEAD]
            if kind < 2:
                yh = yh * cos + pltpu.roll(yh, HEAD // 2, 1) * sin
            stage[head, kind] = yh.astype(LOW)
    for d in range(plan.spread):
        outs[d][...] = stage[part ^ d]
    store_relative(plan, me, normed, n_rel)


def relative_order(plan):
    return [
        sum(((at >> bit) & 1) << (plan.bits - 1 - bit) for bit in range(plan.bits))
        for at in range(plan.dp)
    ]


def kept_orders(plan):
    up = relative_order(plan)[: plan.dp // 2]
    down = [2 * at for at in range(plan.dp // 2)]
    return up, down


def store_relative(plan, me, source, target):
    up, down = kept_orders(plan)
    order = relative_order(plan) + down
    for at, relative in enumerate(order):
        columns = pl.ds(pl.multiple_of((me ^ relative) * plan.piece, plan.piece), plan.piece)
        target[:, at * plan.piece : (at + 1) * plan.piece] = source[:, columns]


def project_qkv(plan, slot_parent, place, tokens, wq, wk, wv, cosine, sine):
    whole = lambda i, *_: (0, 0)
    once = pl.Buffered(buffer_count=1)
    wide = plan.heads * HEAD
    return pl.pallas_call(
        functools.partial(qkv_kernel, plan),
        grid_spec=pltpu.PrefetchScalarGridSpec(
            num_scalar_prefetch=2,
            grid=(plan.slots,),
            in_specs=[pl.BlockSpec((BLOCK, plan.width), lambda i, *_: (i, 0))]
            + [pl.BlockSpec((plan.width, wide), whole, pipeline_mode=once)] * 3
            + [pl.BlockSpec((CHAIN * BLOCK, HEAD), whole, pipeline_mode=once)] * 2,
            out_specs=[pl.BlockSpec((BLOCK, plan.width * 3 // 2), lambda i, *_: (i, 0))]
            + [pl.BlockSpec((3, BLOCK, HEAD), lambda i, *_: (0, i, 0))] * plan.spread,
            scratch_shapes=[
                pltpu.VMEM((BLOCK, plan.width), LOW),
                pltpu.VMEM((plan.heads, 3, BLOCK, HEAD), LOW),
            ],
        ),
        out_shape=[shape((plan.rows, plan.width * 3 // 2), LOW)]
        + [shape((3, plan.rows, HEAD), LOW)] * plan.spread,
        compiler_params=params(48),
        cost_estimate=pl.CostEstimate(
            flops=6 * plan.rows * plan.width * wide, bytes_accessed=16 * MIB, transcendentals=0
        ),
        name="project_qkv",
    )(slot_parent, place, tokens, wq, wk, wv, cosine, sine)


def relative_kernel(plan, place, source, target):
    store_relative(plan, place[0], source, target)


def relative_columns(plan, place, values):
    return pl.pallas_call(
        functools.partial(relative_kernel, plan),
        grid_spec=pltpu.PrefetchScalarGridSpec(
            num_scalar_prefetch=1,
            grid=(plan.slots,),
            in_specs=[pl.BlockSpec((BLOCK, plan.width), lambda i, *_: (i, 0))],
            out_specs=pl.BlockSpec((BLOCK, plan.width * 3 // 2), lambda i, *_: (i, 0)),
        ),
        out_shape=shape((plan.rows, plan.width * 3 // 2), LOW),
        cost_estimate=pl.CostEstimate(
            flops=0, bytes_accessed=5 * plan.rows * plan.width, transcendentals=0
        ),
        name="relative_columns",
    )(place, values)


def gather_chain(plan, parent, me, slot, kv, keys, values, places=None):
    count = jnp.int32(0)
    at = slot
    for step in range(CHAIN):
        here = jnp.maximum(at, 0)
        relative = (here // plan.slots) ^ me
        block = (
            (relative % plan.rest) * plan.spread + relative // plan.rest
        ) * 2 * plan.slots + here % plan.slots
        keys[step * BLOCK : (step + 1) * BLOCK, :] = kv[block]
        values[step * BLOCK : (step + 1) * BLOCK, :] = kv[block + plan.slots]
        if places is not None:
            places.append(block)
        valid = at >= 0
        count = count + jnp.where(valid, 1, 0).astype(jnp.int32)
        at = jnp.where(valid, parent[here], -1)
    return count


def attend_kernel(plan, parent, place, *refs):
    n = plan.spread
    q_refs, kv, o_refs, keys, values = refs[:n], refs[n], refs[n + 1 : 2 * n + 1], refs[-2], refs[-1]
    me = place[0]
    for d in range(n):

        def one(i, carry, d=d):
            slot = (me ^ (d * plan.rest)) * plan.slots + i
            count = gather_chain(plan, parent, me, slot, kv, keys, values)
            rows = pl.ds(pl.multiple_of(i * BLOCK, BLOCK), BLOCK)
            q = q_refs[d][0, rows, :]
            scores = dot_nt(q, keys[...]) * SCALE
            column = lax.broadcasted_iota(jnp.int32, scores.shape, 1)
            row = lax.broadcasted_iota(jnp.int32, scores.shape, 0)
            allowed = (column < count * BLOCK) & ((column >= BLOCK) | (column <= row))
            scores = jnp.where(allowed, scores, NEGATIVE)
            raised = jnp.exp(scores - jnp.max(scores, axis=1, keepdims=True))
            total = jnp.sum(raised, axis=1, keepdims=True)
            prob = (raised * (1.0 / total)).astype(LOW)
            o_refs[d][rows, :] = dot(prob, values[...]).astype(LOW)
            return carry

        lax.fori_loop(0, plan.slots, one, 0)


def attend(plan, slot_parent, place, parts, kv):
    n = plan.spread
    blocks = plan.dp * 2 * plan.slots
    return pl.pallas_call(
        functools.partial(attend_kernel, plan),
        grid_spec=pltpu.PrefetchScalarGridSpec(
            num_scalar_prefetch=2,
            grid=(1,),
            in_specs=[pl.BlockSpec((1, plan.rows, HEAD), lambda i, *_: (0, 0, 0))] * n
            + [pl.BlockSpec((blocks, BLOCK, HEAD), lambda i, *_: (0, 0, 0))],
            out_specs=[pl.BlockSpec((plan.rows, HEAD), lambda i, *_: (0, 0))] * n,
            scratch_shapes=[pltpu.VMEM((CHAIN * BLOCK, HEAD), LOW)] * 2,
        ),
        out_shape=[shape((plan.rows, HEAD), LOW)] * n,
        compiler_params=params(40),
        cost_estimate=pl.CostEstimate(
            flops=4 * n * plan.rows * CHAIN * BLOCK * HEAD,
            bytes_accessed=8 * MIB,
            transcendentals=n * plan.rows * CHAIN * BLOCK,
        ),
        name="attend",
    )(slot_parent, place, *parts, kv)


def attend_back_kernel(plan, parent, place, *refs):
    n = plan.spread
    q_refs, kv, g_refs = refs[:n], refs[n], refs[n + 1 : 2 * n + 1]
    dq_refs = refs[2 * n + 1 : 3 * n + 1]
    near, far, keys, values, total = refs[3 * n + 1 :]
    me = place[0]
    total[...] = jnp.zeros_like(total)
    for d in range(n):

        def one(i, carry, d=d):
            slot = (me ^ (d * plan.rest)) * plan.slots + i
            places = []
            count = gather_chain(plan, parent, me, slot, kv, keys, values, places)
            rows = pl.ds(pl.multiple_of(i * BLOCK, BLOCK), BLOCK)
            q = q_refs[d][0, rows, :]
            g = g_refs[d][rows, :]
            k = keys[...]
            scores = dot_nt(k, q) * SCALE
            key_at = lax.broadcasted_iota(jnp.int32, scores.shape, 0)
            query_at = lax.broadcasted_iota(jnp.int32, scores.shape, 1)
            allowed = (key_at < count * BLOCK) & ((key_at >= BLOCK) | (key_at <= query_at))
            scores = jnp.where(allowed, scores, NEGATIVE)
            raised = jnp.exp(scores - jnp.max(scores, axis=0, keepdims=True))
            prob = raised * (1.0 / jnp.sum(raised, axis=0, keepdims=True))
            grad_prob = dot_nt(values[...], g)
            inner = jnp.sum(grad_prob * prob, axis=0, keepdims=True)
            grad_scores = (prob * (grad_prob - inner)).astype(LOW)
            dv = dot(prob.astype(LOW), g)
            dk = dot(grad_scores, q) * SCALE
            dq_refs[d][rows, :] = (dot_tn(grad_scores, k) * SCALE).astype(LOW)
            for step, block in enumerate(places):
                span = slice(step * BLOCK, (step + 1) * BLOCK)
                total[block] = total[block] + dk[span]
                total[block + plan.slots] = total[block + plan.slots] + dv[span]
            return carry

        lax.fori_loop(0, plan.slots, one, 0)
    half = near.shape[0]
    near[...] = total[:half]
    far[...] = total[half:].astype(LOW)


def attend_back(plan, slot_parent, place, parts, kv, grads):
    n = plan.spread
    blocks = plan.dp * 2 * plan.slots
    near = n * 2 * plan.slots
    return pl.pallas_call(
        functools.partial(attend_back_kernel, plan),
        grid_spec=pltpu.PrefetchScalarGridSpec(
            num_scalar_prefetch=2,
            grid=(1,),
            in_specs=[pl.BlockSpec((1, plan.rows, HEAD), lambda i, *_: (0, 0, 0))] * n
            + [pl.BlockSpec((blocks, BLOCK, HEAD), lambda i, *_: (0, 0, 0))]
            + [pl.BlockSpec((plan.rows, HEAD), lambda i, *_: (0, 0))] * n,
            out_specs=[pl.BlockSpec((plan.rows, HEAD), lambda i, *_: (0, 0))] * n
            + [
                pl.BlockSpec((near, BLOCK, HEAD), lambda i, *_: (0, 0, 0)),
                pl.BlockSpec((blocks - near, BLOCK, HEAD), lambda i, *_: (0, 0, 0)),
            ],
            scratch_shapes=[pltpu.VMEM((CHAIN * BLOCK, HEAD), LOW)] * 2
            + [pltpu.VMEM((blocks, BLOCK, HEAD), F32)],
        ),
        out_shape=[shape((plan.rows, HEAD), LOW)] * n
        + [shape((near, BLOCK, HEAD), F32), shape((blocks - near, BLOCK, HEAD), LOW)],
        compiler_params=params(56),
        cost_estimate=pl.CostEstimate(
            flops=10 * n * plan.rows * CHAIN * BLOCK * HEAD,
            bytes_accessed=16 * MIB,
            transcendentals=n * plan.rows * CHAIN * BLOCK,
        ),
        name="attend_back",
    )(slot_parent, place, *parts, kv, *grads)


def heads_kernel(plan, place, *refs):
    part = place[0] // plan.rest
    out = refs[-1]
    for d in range(plan.spread):
        head = pl.ds(pl.multiple_of((part ^ d) * HEAD, HEAD), HEAD)
        out[:, head] = refs[d][...]


def gather_heads(plan, place, parts):
    return pl.pallas_call(
        functools.partial(heads_kernel, plan),
        grid_spec=pltpu.PrefetchScalarGridSpec(
            num_scalar_prefetch=1,
            grid=(1,),
            in_specs=[pl.BlockSpec((plan.rows, HEAD), lambda i, *_: (0, 0))] * plan.spread,
            out_specs=pl.BlockSpec((plan.rows, plan.heads * HEAD), lambda i, *_: (0, 0)),
        ),
        out_shape=shape((plan.rows, plan.heads * HEAD), LOW),
        name="gather_heads",
    )(place, *parts)


def scatter_kernel(plan, place, *refs):
    part, z = place[0] // plan.rest, place[1]
    sources, outs = refs[: plan.tensor], refs[plan.tensor :]
    for shift in range(plan.tensor):
        origin = lax.rem(z - shift + plan.tensor, plan.tensor)
        rows = pl.ds(pl.multiple_of(origin * plan.own, 16), plan.own)
        for d in range(plan.spread):
            head = pl.ds(pl.multiple_of((part ^ d) * HEAD, HEAD), HEAD)
            outs[d][rows, :] = sources[shift][:, head]


def scatter_heads(plan, place, sources):
    return pl.pallas_call(
        functools.partial(scatter_kernel, plan),
        grid_spec=pltpu.PrefetchScalarGridSpec(
            num_scalar_prefetch=1,
            grid=(1,),
            in_specs=[pl.BlockSpec((plan.own, plan.heads * HEAD), lambda i, *_: (0, 0))]
            * plan.tensor,
            out_specs=[pl.BlockSpec((plan.rows, HEAD), lambda i, *_: (0, 0))] * plan.spread,
        ),
        out_shape=[shape((plan.rows, HEAD), LOW)] * plan.spread,
        name="scatter_heads",
    )(place, *sources)


def turn_back_kernel(plan, parent, place, cosine, sine, *refs):
    me = place[0]
    part = me // plan.rest
    out = refs[-1]
    depth = depth_of(parent, me * plan.slots + pl.program_id(0))
    rows = pl.ds(pl.multiple_of(depth * BLOCK, BLOCK), BLOCK)
    cos, sin = cosine[rows, :], sine[rows, :]
    for d in range(plan.spread):
        for kind in range(3):
            value = refs[d][kind]
            if kind < 2:
                value = value.astype(F32)
                value = (value * cos - pltpu.roll(value, HEAD // 2, 1) * sin).astype(LOW)
            at = pl.multiple_of((kind * plan.heads + (part ^ d)) * HEAD, HEAD)
            out[:, pl.ds(at, HEAD)] = value


def turn_back(plan, slot_parent, place, cosine, sine, parts):
    whole = lambda i, *_: (0, 0)
    wide = 3 * plan.heads * HEAD
    return pl.pallas_call(
        functools.partial(turn_back_kernel, plan),
        grid_spec=pltpu.PrefetchScalarGridSpec(
            num_scalar_prefetch=2,
            grid=(plan.slots,),
            in_specs=[pl.BlockSpec((CHAIN * BLOCK, HEAD), whole)] * 2
            + [pl.BlockSpec((3, BLOCK, HEAD), lambda i, *_: (0, i, 0))] * plan.spread,
            out_specs=pl.BlockSpec((BLOCK, wide), lambda i, *_: (i, 0)),
        ),
        out_shape=shape((plan.rows, wide), LOW),
        name="turn_back",
    )(slot_parent, place, cosine, sine, *parts)


def out_kernel(plan, place, x, att, near, far, middle, normed):
    half = plan.heads * HEAD // 2
    core = place[0] % 2
    total = x[...].astype(F32)
    for z in range(plan.tensor):
        for side, w in ((core, near), (1 - core, far)):
            columns = pl.ds(pl.multiple_of(side * half, half), half)
            total = total + dot(att[z, :, columns], w[z])
    middle[...] = total
    normed[...] = layer_norm(total)[0].astype(LOW)


def project_out(plan, place, tokens, att, near, far):
    half = plan.heads * HEAD // 2
    once = pl.Buffered(buffer_count=1)
    weights = pl.BlockSpec(
        (plan.tensor, half, plan.width), lambda i, *_: (0, 0, 0), pipeline_mode=once
    )
    rows = pl.BlockSpec((BLOCK, plan.width), lambda i, *_: (i, 0))
    return pl.pallas_call(
        functools.partial(out_kernel, plan),
        grid_spec=pltpu.PrefetchScalarGridSpec(
            num_scalar_prefetch=1,
            grid=(plan.slots,),
            in_specs=[
                rows,
                pl.BlockSpec((plan.tensor, BLOCK, 2 * half), lambda i, *_: (0, i, 0)),
                weights,
                weights,
            ],
            out_specs=[rows, rows],
        ),
        out_shape=[shape((plan.rows, plan.width), F32), shape((plan.rows, plan.width), LOW)],
        compiler_params=params(48),
        cost_estimate=pl.CostEstimate(
            flops=2 * plan.rows * plan.width * plan.width,
            bytes_accessed=20 * MIB,
            transcendentals=0,
        ),
        name="project_out",
    )(place, tokens, att, near, far)


def ff_kernel(rows_each, normed, cot, wg, wu, wd, hidden, grad_gate, grad_up, back, total):
    step = pl.program_id(0)
    for start in range(0, normed.shape[0], rows_each):
        rows = slice(start, start + rows_each)
        n = normed[rows, :]
        gate = dot(n, wg[...])
        up = dot(n, wu[...])
        grad_hidden = dot_nt(cot[rows, :], wd[...])
        s = 1.0 / (1.0 + jnp.exp(-gate))
        active = gate * s
        hidden[rows, :] = (active * up).astype(LOW)
        gu = (grad_hidden * active).astype(LOW)
        gg = (grad_hidden * up * s * (1.0 + gate * (1.0 - s))).astype(LOW)
        grad_up[rows, :] = gu
        grad_gate[rows, :] = gg
        part = dot_nt(gg, wg[...]) + dot_nt(gu, wu[...])

        @pl.when(step == 0)
        def _():
            total[rows, :] = part

        @pl.when(step > 0)
        def _():
            total[rows, :] += part

    @pl.when(step == pl.num_programs(0) - 1)
    def _():
        back[...] = total[...].astype(LOW)


def feed_forward(normed, cot, wg, wu, wd):
    rows, width = normed.shape
    ff = wg.shape[1]
    tile = min(512, ff)
    whole = pl.BlockSpec((rows, width), lambda i: (0, 0), pipeline_mode=pl.Buffered(buffer_count=1))
    across = pl.BlockSpec((width, tile), lambda i: (0, i))
    out = pl.BlockSpec((rows, tile), lambda i: (0, i))
    return pl.pallas_call(
        functools.partial(ff_kernel, rows // 2),
        grid=(ff // tile,),
        in_specs=[whole, whole, across, across, pl.BlockSpec((tile, width), lambda i: (i, 0))],
        out_specs=[out, out, out, pl.BlockSpec((rows, width), lambda i: (0, 0))],
        out_shape=[shape((rows, ff), LOW)] * 3 + [shape((rows, width), LOW)],
        scratch_shapes=[pltpu.VMEM((rows, width), F32)],
        compiler_params=params(60),
        cost_estimate=pl.CostEstimate(
            flops=10 * rows * width * ff, bytes_accessed=40 * MIB, transcendentals=rows * ff
        ),
        name="feed_forward",
    )(normed, cot, wg, wu, wd)


def weight_gradient(plan, lhs, rhs):
    half, piece = plan.dp // 2, plan.piece
    columns = rhs.shape[1]
    kept = half * piece
    pairs = lambda bit: xor_pairs(plan.dp, 1 << bit)
    send = dot_tn(lhs[:, kept : 2 * kept], rhs).astype(LOW)
    recv = lax.ppermute(send, "dp", pairs(0))
    up, down = kept_orders(plan)
    results = []
    for way in range(2):
        cols = slice(way * columns // 2, (way + 1) * columns // 2)
        order = up if way == 0 else down
        base = 0 if way == 0 else 2 * kept
        bits = list(range(1, plan.bits))
        if way == 1:
            bits = bits[::-1]
        size = half // 2
        parts = []
        for side in range(2):
            at = base + side * size * piece
            product = dot_tn(lhs[:, at : at + size * piece], rhs[:, cols])
            arrived = [
                recv[up.index(rel) * piece : (up.index(rel) + 1) * piece, cols]
                for rel in order[side * size : (side + 1) * size]
            ]
            parts.append((product + jnp.concatenate(arrived, 0).astype(F32)).astype(LOW))
        keep, away = parts
        for number, bit in enumerate(bits):
            got = lax.ppermute(away, "dp", pairs(bit))
            total = keep.astype(F32) + got.astype(F32)
            if number == len(bits) - 1:
                results.append(total)
            else:
                size = total.shape[0] // 2
                keep = total[:size].astype(LOW)
                away = total[size:].astype(LOW)
    return jnp.concatenate(results, axis=1)


def body(mesh, tokens, w_query, w_key, w_value, w_out, w_gate, w_up, w_down, cotangent, slot_parent):
    plan = Plan(mesh, tokens.shape[0], tokens.shape[1], w_query.shape[1] // HEAD, w_gate.shape[1])
    me = lax.axis_index("dp")
    z = lax.axis_index("tensor")
    place = jnp.stack([me, z]).astype(jnp.int32)
    cosine, sine = (jnp.asarray(table) for table in rope_tables())
    n = plan.spread

    def swap(array, mask):
        return lax.ppermute(array, "dp", xor_pairs(plan.dp, mask))

    def exchange(parts):
        return [parts[0]] + [swap(parts[d], d * plan.rest) for d in range(1, n)]

    half = w_out.shape[0] // 2
    mine = lax.dynamic_slice_in_dim(w_out, (me % 2) * half, half, 0)
    near = lax.all_gather(mine, "tensor", axis=0, tiled=False)
    far = swap(near, 1)

    normed_one, *sends = project_qkv(
        plan, slot_parent, place, tokens, w_query, w_key, w_value, cosine, sine
    )
    parts = exchange(sends)
    kv = jnp.stack([part[1:] for part in parts])[None]
    mask = 1
    while mask < plan.rest:
        kv = jnp.concatenate([kv, swap(kv, mask)], axis=0)
        mask *= 2
    kv = kv.reshape(plan.dp * 2 * plan.slots, BLOCK, HEAD)
    attended_parts = exchange(attend(plan, slot_parent, place, parts, kv))
    attended = gather_heads(plan, place, attended_parts)
    everyone = lax.all_gather(attended, "tensor", axis=0, tiled=False)
    middle, normed_two = project_out(plan, place, tokens, everyone, near, far)

    hidden, grad_gate_proj, grad_up_proj, partial_two = feed_forward(
        normed_two, cotangent, w_gate, w_up, w_down
    )
    mine_rows = lambda array: lax.dynamic_slice_in_dim(array, z * plan.own, plan.own, 0)
    grad_normed_two = lax.psum_scatter(
        partial_two, "tensor", scatter_dimension=0, tiled=True
    ).astype(F32)
    branch_out = dot(hidden, w_down).astype(LOW)
    middle_own = mine_rows(middle)
    norm_two, inverse_two = layer_norm(middle_own)
    grad_middle = mine_rows(cotangent).astype(F32) + norm_back(grad_normed_two, norm_two, inverse_two)
    grad_branch = grad_middle.astype(LOW)

    ga_near = jnp.einsum("td,zcd->ztc", grad_branch, near, preferred_element_type=F32).astype(LOW)
    ga_far = jnp.einsum("td,zcd->ztc", grad_branch, far, preferred_element_type=F32).astype(LOW)
    even = me % 2 == 0
    ga = jnp.concatenate(
        [jnp.where(even, ga_near, ga_far), jnp.where(even, ga_far, ga_near)], axis=2
    )
    sources = []
    for shift in range(plan.tensor):
        chunk = lax.dynamic_index_in_dim(ga, (z + shift) % plan.tensor, 0, keepdims=False)
        if shift:
            chunk = lax.ppermute(
                chunk, "tensor", [(i, (i + shift) % plan.tensor) for i in range(plan.tensor)]
            )
        sources.append(chunk)
    grads = exchange(scatter_heads(plan, place, sources))
    *grad_queries, grad_near, grad_far = attend_back(plan, slot_parent, place, parts, kv, grads)

    grad_far = grad_far.reshape(plan.rest - 1, n, 2, plan.rows, HEAD)
    grad_near = grad_near.reshape(1, n, 2, plan.rows, HEAD)
    mask = plan.rest // 2
    while mask >= 1:
        got = swap(grad_far[mask - 1 : 2 * mask - 1], mask).astype(F32)
        grad_near = grad_near + got[:1]
        if mask > 1:
            grad_far = (grad_far[: mask - 1].astype(F32) + got[1:]).astype(LOW)
        mask //= 2
    backs = exchange(
        [
            jnp.concatenate([grad_queries[d][None], grad_near[0, d].astype(LOW)], axis=0)
            for d in range(n)
        ]
    )
    turned = turn_back(plan, slot_parent, place, cosine, sine, backs)
    wide = n * HEAD
    partial_one = sum(
        dot_nt(turned[:, kind * wide : (kind + 1) * wide], w)
        for kind, w in enumerate((w_query, w_key, w_value))
    ).astype(LOW)
    grad_normed_one = lax.psum_scatter(
        partial_one, "tensor", scatter_dimension=0, tiled=True
    ).astype(F32)
    norm_one, inverse_one = layer_norm(mine_rows(tokens).astype(F32))
    grad_tokens_own = (grad_middle + norm_back(grad_normed_one, norm_one, inverse_one)).astype(LOW)
    grad_tokens = lax.all_gather(grad_tokens_own, "tensor", axis=0, tiled=True)

    output_own = (
        middle_own
        + lax.psum_scatter(branch_out, "tensor", scatter_dimension=0, tiled=True).astype(F32)
    ).astype(LOW)
    output = lax.all_gather(output_own, "tensor", axis=0, tiled=True)

    cot_relative = relative_columns(plan, place, cotangent)
    two_relative = relative_columns(plan, place, normed_two)
    grad_down = weight_gradient(plan, cot_relative, hidden).T
    grad_gate = weight_gradient(plan, two_relative, grad_gate_proj)
    grad_up = weight_gradient(plan, two_relative, grad_up_proj)
    branch_all = lax.all_gather(grad_branch, "tensor", axis=0, tiled=True)
    grad_out = weight_gradient(plan, relative_columns(plan, place, branch_all), attended).T
    grad_qkv = weight_gradient(plan, normed_one, turned)
    return (
        output,
        grad_tokens,
        grad_qkv[:, :wide],
        grad_qkv[:, wide : 2 * wide],
        grad_qkv[:, 2 * wide :],
        grad_out,
        grad_gate,
        grad_up,
        grad_down,
    )


def solution(mesh):
    in_specs = (
        P("dp", None),
        P(None, "tensor"),
        P(None, "tensor"),
        P(None, "tensor"),
        P("tensor", None),
        P(None, "tensor"),
        P(None, "tensor"),
        P("tensor", None),
        P("dp", None),
        P(),
    )
    out_specs = (
        P("dp", None),
        P("dp", None),
        P("dp", "tensor"),
        P("dp", "tensor"),
        P("dp", "tensor"),
        P("tensor", "dp"),
        P("dp", "tensor"),
        P("dp", "tensor"),
        P("tensor", "dp"),
    )
    return jax.shard_map(
        functools.partial(body, mesh),
        mesh=mesh,
        in_specs=in_specs,
        out_specs=out_specs,
        check_vma=False,
    )
```

```python
import functools
import math

import jax
import jax.numpy as jnp
import numpy as np
from jax import lax
from jax.experimental import pallas as pl
from jax.experimental.pallas import tpu as pltpu
from jax.sharding import PartitionSpec as P

HEAD = 128
BLOCK = 128
TRUNK_BLOCKS = 8
CHAIN = TRUNK_BLOCKS + 2
EPSILON = 1e-05
NEGATIVE = -1e30
SCALE = HEAD ** (-0.5)
LOW = jnp.bfloat16
F32 = jnp.float32
MIB = 1024 * 1024
PER_MICROSECOND = 100e9
NT = (((1,), (1,)), ((), ()))
TN = (((0,), (0,)), ((), ()))


def dot(a, b):
    return jnp.dot(a, b, preferred_element_type=F32)


def dot_nt(a, b):
    return lax.dot_general(a, b, NT, preferred_element_type=F32)


def dot_tn(a, b):
    return lax.dot_general(a, b, TN, preferred_element_type=F32)


def shape(dims, dtype):
    return jax.ShapeDtypeStruct(dims, dtype)


def about(microseconds):
    return pl.CostEstimate(
        flops=int(microseconds * PER_MICROSECOND), bytes_accessed=1, transcendentals=0
    )


def params(mib):
    return pltpu.CompilerParams(vmem_limit_bytes=mib * MIB)


def layer_norm(values):
    centered = values - jnp.mean(values, axis=-1, keepdims=True)
    variance = jnp.mean(centered * centered, axis=-1, keepdims=True)
    inverse = lax.rsqrt(variance + EPSILON)
    return (centered * inverse, inverse)


def norm_back(gradient, normed, inverse):
    return inverse * (
        gradient
        - jnp.mean(gradient, axis=-1, keepdims=True)
        - normed * jnp.mean(gradient * normed, axis=-1, keepdims=True)
    )


def rope_tables():
    frequency = np.exp(
        np.arange(HEAD // 2, dtype=np.float32) * np.float32(-2.0 * math.log(10000.0) / HEAD)
    ).astype(np.float32)
    angle = np.arange(CHAIN * BLOCK, dtype=np.float32)[:, None] * frequency[None, :]
    cosine, sine = np.cos(angle), np.sin(angle)
    return (
        np.concatenate([cosine, cosine], axis=1).astype(np.float32),
        np.concatenate([-sine, sine], axis=1).astype(np.float32),
    )


def depth_of(parent_ref, slot):
    def up(_, carry):
        at, depth = carry
        parent = jnp.where(at >= 0, parent_ref[jnp.maximum(at, 0)], -1)
        return parent, depth + jnp.where(parent >= 0, 1, 0).astype(jnp.int32)

    return lax.fori_loop(0, CHAIN - 1, up, (slot, jnp.int32(0)))[1]


def xor_pairs(count, mask):
    return [(index, index ^ mask) for index in range(count)]


class Plan:
    def __init__(self, mesh, rows, width, heads, ff):
        self.dp = mesh.shape["dp"]
        self.tensor = mesh.shape["tensor"]
        self.rows, self.width, self.heads, self.ff = rows, width, heads, ff
        self.slots = rows // BLOCK
        self.spread = heads
        self.rest = self.dp // heads
        self.bits = self.dp.bit_length() - 1
        self.piece = width // self.dp
        self.own = rows // self.tensor


def fetch(weights, held, sems, kind):
    copies = [
        pltpu.make_async_copy(w, held.at[index], sems.at[index]) for index, w in enumerate(weights)
    ]

    @pl.when(kind == 0)
    def _():
        for copy in copies:
            copy.start()

    def wait():
        for index, copy in enumerate(copies):

            @pl.when(kind == index)
            def _():
                copy.wait()

    return wait


def qkv_kernel(plan, parent, place, x, wq, wk, wv, cosine, sine, normed, *rest):
    outs, stage = rest[: plan.spread], rest[-1]
    me = place[0]
    part = me // plan.rest
    depth = depth_of(parent, me * plan.slots + pl.program_id(0))
    rows = pl.ds(pl.multiple_of(depth * BLOCK, BLOCK), BLOCK)
    cos, sin = cosine[rows, :], sine[rows, :]
    low = layer_norm(x[...].astype(F32))[0].astype(LOW)
    normed[...] = low
    for kind, w in enumerate((wq, wk, wv)):
        y = dot(low, w[...])
        for head in range(plan.heads):
            yh = y[:, head * HEAD : (head + 1) * HEAD]
            if kind < 2:
                yh = yh * cos + pltpu.roll(yh, HEAD // 2, 1) * sin
            stage[head, kind] = yh.astype(LOW)
    for d in range(plan.spread):
        outs[d][...] = stage[part ^ d]


def kept_order(plan):
    return [
        sum(((at >> bit) & 1) << (plan.bits - 1 - bit) for bit in range(plan.bits - 1))
        for at in range(plan.dp // 2)
    ]


def project_qkv(plan, slot_parent, place, tokens, wq, wk, wv, cosine, sine):
    whole = lambda i, *_: (0, 0)
    once = pl.Buffered(buffer_count=1)
    wide = plan.heads * HEAD
    return pl.pallas_call(
        functools.partial(qkv_kernel, plan),
        grid_spec=pltpu.PrefetchScalarGridSpec(
            num_scalar_prefetch=2,
            grid=(plan.slots,),
            in_specs=[pl.BlockSpec((BLOCK, plan.width), lambda i, *_: (i, 0))]
            + [pl.BlockSpec((plan.width, wide), whole, pipeline_mode=once)] * 3
            + [pl.BlockSpec((CHAIN * BLOCK, HEAD), whole, pipeline_mode=once)] * 2,
            out_specs=[pl.BlockSpec((BLOCK, plan.width), lambda i, *_: (i, 0))]
            + [pl.BlockSpec((3, BLOCK, HEAD), lambda i, *_: (0, i, 0))] * plan.spread,
            scratch_shapes=[
                pltpu.VMEM((plan.heads, 3, BLOCK, HEAD), LOW),
            ],
        ),
        out_shape=[shape((plan.rows, plan.width), LOW)]
        + [shape((3, plan.rows, HEAD), LOW)] * plan.spread,
        compiler_params=params(60),
        cost_estimate=about(0),
        name="project_qkv",
    )(slot_parent, place, tokens, wq, wk, wv, cosine, sine)


def gather_chain(plan, parent, me, slot, kv, keys, values):
    count = jnp.int32(0)
    at = slot
    places = []
    for step in range(CHAIN):
        here = jnp.maximum(at, 0)
        relative = (here // plan.slots) ^ me
        block = (
            (relative % plan.rest) * plan.spread + relative // plan.rest
        ) * 2 * plan.slots + here % plan.slots
        keys[step * BLOCK : (step + 1) * BLOCK, :] = kv[block]
        values[step * BLOCK : (step + 1) * BLOCK, :] = kv[block + plan.slots]
        places.append(block)
        valid = at >= 0
        count = count + jnp.where(valid, 1, 0).astype(jnp.int32)
        at = jnp.where(valid, parent[here], -1)
    return count, places


def chain_weights(queries, keys, counts):
    scores = [dot_nt(k, q) * SCALE for q, k in zip(queries, keys)]
    key_at = lax.broadcasted_iota(jnp.int32, scores[0].shape, 0)
    query_at = lax.broadcasted_iota(jnp.int32, scores[0].shape, 1)
    own = (key_at >= BLOCK) | (key_at <= query_at)
    probs = []
    for score, count in zip(scores, counts):
        score = jnp.where(own & (key_at < count * BLOCK), score, NEGATIVE)
        raised = jnp.exp(score - jnp.max(score, axis=0, keepdims=True))
        probs.append(raised * (1.0 / jnp.sum(raised, axis=0, keepdims=True)))
    return probs


def attend_kernel(plan, parent, place, *refs):
    n = plan.spread
    q_refs, kv, o_refs, keys, values = refs[:n], refs[n], refs[n + 1 : 2 * n + 1], refs[-2], refs[-1]
    me = place[0]

    def one(i, carry):
        rows = pl.ds(pl.multiple_of(i * BLOCK, BLOCK), BLOCK)
        slots = [(me ^ (d * plan.rest)) * plan.slots + i for d in range(n)]
        counts = [
            gather_chain(plan, parent, me, slots[d], kv, keys.at[d], values.at[d])[0]
            for d in range(n)
        ]
        queries = [q_refs[d][0, rows, :] for d in range(n)]
        probs = chain_weights(queries, [keys[d] for d in range(n)], counts)
        for d in range(n):
            o_refs[d][rows, :] = dot_tn(probs[d].astype(LOW), values[d]).astype(LOW)
        return carry

    lax.fori_loop(0, plan.slots, one, 0)


def attend(plan, slot_parent, place, parts, kv):
    n = plan.spread
    blocks = plan.dp * 2 * plan.slots
    return pl.pallas_call(
        functools.partial(attend_kernel, plan),
        grid_spec=pltpu.PrefetchScalarGridSpec(
            num_scalar_prefetch=2,
            grid=(1,),
            in_specs=[pl.BlockSpec((1, plan.rows, HEAD), lambda i, *_: (0, 0, 0))] * n
            + [pl.BlockSpec((blocks, BLOCK, HEAD), lambda i, *_: (0, 0, 0))],
            out_specs=[pl.BlockSpec((plan.rows, HEAD), lambda i, *_: (0, 0))] * n,
            scratch_shapes=[pltpu.VMEM((n, CHAIN * BLOCK, HEAD), LOW)] * 2,
        ),
        out_shape=[shape((plan.rows, HEAD), LOW)] * n,
        compiler_params=params(60),
        cost_estimate=about(0),
        name="attend",
    )(slot_parent, place, *parts, kv)


def attend_back_kernel(plan, parent, place, *refs):
    n = plan.spread
    q_refs, kv, g_refs = refs[:n], refs[n], refs[n + 1 : 2 * n + 1]
    dq_refs = refs[2 * n + 1 : 3 * n + 1]
    near, far, keys, values, total = refs[3 * n + 1 :]
    me = place[0]
    total[...] = jnp.zeros_like(total)

    def one(i, carry):
        rows = pl.ds(pl.multiple_of(i * BLOCK, BLOCK), BLOCK)
        slots = [(me ^ (d * plan.rest)) * plan.slots + i for d in range(n)]
        chains = [
            gather_chain(plan, parent, me, slots[d], kv, keys.at[d], values.at[d])
            for d in range(n)
        ]
        queries = [q_refs[d][0, rows, :] for d in range(n)]
        grads = [g_refs[d][rows, :] for d in range(n)]
        probs = chain_weights(queries, [keys[d] for d in range(n)], [chain[0] for chain in chains])
        for d in range(n):
            grad_prob = dot_nt(values[d], grads[d])
            inner = jnp.sum(grad_prob * probs[d], axis=0, keepdims=True)
            grad_scores = (probs[d] * (grad_prob - inner)).astype(LOW)
            dv = dot(probs[d].astype(LOW), grads[d])
            dk = dot(grad_scores, queries[d]) * SCALE
            dq_refs[d][rows, :] = (dot_tn(grad_scores, keys[d]) * SCALE).astype(LOW)
            for step, block in enumerate(chains[d][1]):
                span = slice(step * BLOCK, (step + 1) * BLOCK)
                total[block] = total[block] + dk[span]
                total[block + plan.slots] = total[block + plan.slots] + dv[span]
        return carry

    lax.fori_loop(0, plan.slots, one, 0)
    half = near.shape[0]
    near[...] = total[:half]
    far[...] = total[half:].astype(LOW)


def attend_back(plan, slot_parent, place, parts, kv, grads):
    n = plan.spread
    blocks = plan.dp * 2 * plan.slots
    near = n * 2 * plan.slots
    return pl.pallas_call(
        functools.partial(attend_back_kernel, plan),
        grid_spec=pltpu.PrefetchScalarGridSpec(
            num_scalar_prefetch=2,
            grid=(1,),
            in_specs=[pl.BlockSpec((1, plan.rows, HEAD), lambda i, *_: (0, 0, 0))] * n
            + [pl.BlockSpec((blocks, BLOCK, HEAD), lambda i, *_: (0, 0, 0))]
            + [pl.BlockSpec((plan.rows, HEAD), lambda i, *_: (0, 0))] * n,
            out_specs=[pl.BlockSpec((plan.rows, HEAD), lambda i, *_: (0, 0))] * n
            + [
                pl.BlockSpec((near, BLOCK, HEAD), lambda i, *_: (0, 0, 0)),
                pl.BlockSpec((blocks - near, BLOCK, HEAD), lambda i, *_: (0, 0, 0)),
            ],
            scratch_shapes=[pltpu.VMEM((n, CHAIN * BLOCK, HEAD), LOW)] * 2
            + [pltpu.VMEM((blocks, BLOCK, HEAD), F32)],
        ),
        out_shape=[shape((plan.rows, HEAD), LOW)] * n
        + [shape((near, BLOCK, HEAD), F32), shape((blocks - near, BLOCK, HEAD), LOW)],
        compiler_params=params(60),
        cost_estimate=about(23),
        name="attend_back",
    )(slot_parent, place, *parts, kv, *grads)


def heads_kernel(plan, place, *refs):
    part = place[0] // plan.rest
    out = refs[-1]
    for d in range(plan.spread):
        head = pl.ds(pl.multiple_of((part ^ d) * HEAD, HEAD), HEAD)
        out[:, head] = refs[d][...]


def gather_heads(plan, place, parts):
    return pl.pallas_call(
        functools.partial(heads_kernel, plan),
        grid_spec=pltpu.PrefetchScalarGridSpec(
            num_scalar_prefetch=1,
            grid=(1,),
            in_specs=[pl.BlockSpec((plan.rows, HEAD), lambda i, *_: (0, 0))] * plan.spread,
            out_specs=pl.BlockSpec((plan.rows, plan.heads * HEAD), lambda i, *_: (0, 0)),
        ),
        out_shape=shape((plan.rows, plan.heads * HEAD), LOW),
        name="gather_heads",
    )(place, *parts)


def scatter_kernel(plan, place, *refs):
    part, z = place[0] // plan.rest, place[1]
    sources, outs = refs[: plan.tensor], refs[plan.tensor :]
    for shift in range(plan.tensor):
        origin = lax.rem(z - shift + plan.tensor, plan.tensor)
        rows = pl.ds(pl.multiple_of(origin * plan.own, 16), plan.own)
        for d in range(plan.spread):
            head = pl.ds(pl.multiple_of((part ^ d) * HEAD, HEAD), HEAD)
            outs[d][rows, :] = sources[shift][:, head]


def scatter_heads(plan, place, sources):
    return pl.pallas_call(
        functools.partial(scatter_kernel, plan),
        grid_spec=pltpu.PrefetchScalarGridSpec(
            num_scalar_prefetch=1,
            grid=(1,),
            in_specs=[pl.BlockSpec((plan.own, plan.heads * HEAD), lambda i, *_: (0, 0))]
            * plan.tensor,
            out_specs=[pl.BlockSpec((plan.rows, HEAD), lambda i, *_: (0, 0))] * plan.spread,
        ),
        out_shape=[shape((plan.rows, HEAD), LOW)] * plan.spread,
        name="scatter_heads",
    )(place, *sources)


def turn_back_kernel(plan, parent, place, cosine, sine, wq, wk, wv, *refs):
    parts, refs = refs[: plan.spread], refs[plan.spread :]
    back, out, total, held, sems = refs
    me = place[0]
    part = me // plan.rest
    kind = pl.program_id(0)
    wait = fetch((wq, wk, wv), held, sems, kind)

    @pl.when(kind < 2)
    def _():
        for slot in range(plan.slots):
            depth = depth_of(parent, me * plan.slots + slot)
            table = pl.ds(pl.multiple_of(depth * BLOCK, BLOCK), BLOCK)
            cos, sin = cosine[table, :], sine[table, :]
            rows = slice(slot * BLOCK, (slot + 1) * BLOCK)
            for d in range(plan.spread):
                value = parts[d][0, rows, :].astype(F32)
                value = value * cos - pltpu.roll(value, HEAD // 2, 1) * sin
                columns = pl.ds(pl.multiple_of((part ^ d) * HEAD, HEAD), HEAD)
                out[rows, columns] = value.astype(LOW)

    @pl.when(kind == 2)
    def _():
        for d in range(plan.spread):
            columns = pl.ds(pl.multiple_of((part ^ d) * HEAD, HEAD), HEAD)
            out[:, columns] = parts[d][0]

    wait()
    product = dot_nt(out[...], held[kind])

    @pl.when(kind == 0)
    def _():
        total[...] = product

    @pl.when(kind == 1)
    def _():
        total[...] += product

    @pl.when(kind == 2)
    def _():
        back[...] = (total[...] + product).astype(LOW)


def turn_back(plan, slot_parent, place, cosine, sine, weights, parts):
    whole = lambda i, *_: (0, 0)
    wide = plan.heads * HEAD
    return pl.pallas_call(
        functools.partial(turn_back_kernel, plan),
        grid_spec=pltpu.PrefetchScalarGridSpec(
            num_scalar_prefetch=2,
            grid=(3,),
            in_specs=[pl.BlockSpec((CHAIN * BLOCK, HEAD), whole)] * 2
            + [pl.BlockSpec(memory_space=pl.ANY)] * 3
            + [pl.BlockSpec((1, plan.rows, HEAD), lambda i, *_: (i, 0, 0))] * plan.spread,
            out_specs=[
                pl.BlockSpec((plan.rows, plan.width), whole),
                pl.BlockSpec((plan.rows, wide), lambda i, *_: (0, i)),
            ],
            scratch_shapes=[
                pltpu.VMEM((plan.rows, plan.width), F32),
                pltpu.VMEM((3, plan.width, wide), LOW),
                pltpu.SemaphoreType.DMA((3,)),
            ],
        ),
        out_shape=[shape((plan.rows, plan.width), LOW), shape((plan.rows, 3 * wide), LOW)],
        compiler_params=params(60),
        cost_estimate=about(13),
        name="turn_back",
    )(slot_parent, place, cosine, sine, *weights, *parts)


def out_kernel(plan, place, x, att, near, far, middle, normed):
    half = plan.heads * HEAD // 2
    core = place[0] % 2
    total = x[...].astype(F32)
    for z in range(plan.tensor):
        for side, w in ((core, near), (1 - core, far)):
            columns = pl.ds(pl.multiple_of(side * half, half), half)
            total = total + dot(att[z, :, columns], w[z])
    middle[...] = total
    normed[...] = layer_norm(total)[0].astype(LOW)


def project_out(plan, place, tokens, att, near, far):
    half = plan.heads * HEAD // 2
    weights = pl.BlockSpec(
        (plan.tensor, half, plan.width),
        lambda i, *_: (0, 0, 0),
        pipeline_mode=pl.Buffered(buffer_count=1),
    )
    rows = pl.BlockSpec((BLOCK, plan.width), lambda i, *_: (i, 0))
    return pl.pallas_call(
        functools.partial(out_kernel, plan),
        grid_spec=pltpu.PrefetchScalarGridSpec(
            num_scalar_prefetch=1,
            grid=(plan.slots,),
            in_specs=[
                rows,
                pl.BlockSpec((plan.tensor, BLOCK, 2 * half), lambda i, *_: (0, i, 0)),
                weights,
                weights,
            ],
            out_specs=[rows, rows],
        ),
        out_shape=[shape((plan.rows, plan.width), F32), shape((plan.rows, plan.width), LOW)],
        compiler_params=params(40),
        cost_estimate=about(13),
        name="project_out",
    )(place, tokens, att, near, far)


def grad_hidden_kernel(cot, wd, out):
    out[...] = dot_nt(cot[...], wd[...])


def grad_hidden_of(cot, wd, part):
    rows, width = cot.shape
    ff = wd.shape[0] // 2
    tile = min(512, ff)
    return pl.pallas_call(
        grad_hidden_kernel,
        grid=(ff // tile,),
        in_specs=[
            pl.BlockSpec((rows, width), lambda i: (0, 0)),
            pl.BlockSpec((tile, width), lambda i: (part * (ff // tile) + i, 0)),
        ],
        out_specs=pl.BlockSpec((rows, tile), lambda i: (0, i)),
        out_shape=shape((rows, ff), F32),
        compiler_params=params(60),
        cost_estimate=about(0),
        name="grad_hidden",
    )(cot, wd)


def ff_kernel(plan, place, normed, seed, late_seed, wg, wu, *refs):
    back, hidden, grad_gate, grad_up, total = refs
    step = pl.program_id(0)
    gate = dot(normed[...], wg[...])
    up = dot(normed[...], wu[...])
    grad_hidden = jnp.where(step < pl.num_programs(0) // 2, seed[...], late_seed[...])
    s = 1.0 / (1.0 + jnp.exp(-gate))
    active = gate * s
    hidden[...] = (active * up).astype(LOW)
    gu = (grad_hidden * active).astype(LOW)
    gg = (grad_hidden * up * s * (1.0 + gate * (1.0 - s))).astype(LOW)
    grad_up[...] = gu
    grad_gate[...] = gg
    part = dot_nt(gg, wg[...]) + dot_nt(gu, wu[...])

    @pl.when(step == 0)
    def _():
        total[...] = part

    @pl.when(step > 0)
    def _():
        total[...] += part

    @pl.when(step == pl.num_programs(0) - 1)
    def _():
        back[...] = total[...].astype(LOW)


def feed_forward(plan, place, normed, seeds, wg, wu):
    rows, width = normed.shape
    ff = wg.shape[1]
    tile = min(512, ff)
    whole = pl.BlockSpec(
        (rows, width), lambda i, *_: (0, 0), pipeline_mode=pl.Buffered(buffer_count=1)
    )
    count = ff // tile
    across = pl.BlockSpec((width, tile), lambda i, *_: (0, i))
    out = pl.BlockSpec((rows, tile), lambda i, *_: (0, i))
    back = pl.BlockSpec((rows, width), lambda i, *_: (0, 0))
    return pl.pallas_call(
        functools.partial(ff_kernel, plan),
        grid_spec=pltpu.PrefetchScalarGridSpec(
            num_scalar_prefetch=1,
            grid=(ff // tile,),
            in_specs=[
                whole,
                pl.BlockSpec((rows, tile), lambda i, *_: (0, jnp.minimum(i, count // 2 - 1))),
                pl.BlockSpec((rows, tile), lambda i, *_: (0, jnp.maximum(i - count // 2, 0))),
                across,
                across,
            ],
            out_specs=[back, out, out, out],
            scratch_shapes=[pltpu.VMEM((rows, width), F32)],
        ),
        out_shape=[shape((rows, width), LOW)] + [shape((rows, ff), LOW)] * 3,
        compiler_params=params(62),
        cost_estimate=about(32),
        name="feed_forward",
    )(place, normed, *seeds, wg, wu)


def down_kernel(hidden, w, out):
    out[...] = dot(hidden[...], w[...]).astype(LOW)


def project_down(hidden, w):
    rows, ff = hidden.shape
    width = w.shape[1]
    tile = min(512, width)
    return pl.pallas_call(
        down_kernel,
        grid=(width // tile,),
        in_specs=[
            pl.BlockSpec((rows, ff), lambda i: (0, 0)),
            pl.BlockSpec((ff, tile), lambda i: (0, i)),
        ],
        out_specs=pl.BlockSpec((rows, tile), lambda i: (0, i)),
        out_shape=shape((rows, width), LOW),
        compiler_params=params(60),
        cost_estimate=about(11),
        name="project_down",
    )(hidden, w)


def branch_back_kernel(plan, place, part, middle, cot, near, far, grad_middle, low, *refs):
    outs, held = refs[:-1], refs[-1]
    step = pl.program_id(0)

    @pl.when(step == 0)
    def _():
        normed, inverse = layer_norm(middle[...])
        grad = cot[...].astype(F32) + norm_back(part[...].astype(F32), normed, inverse)
        grad_middle[...] = grad
        held[...] = grad.astype(LOW)
        low[...] = held[...]

    core = place[0] % 2
    half = near.shape[1]
    for side, w in ((core, near), (1 - core, far)):
        columns = pl.ds(pl.multiple_of(side * half, half), half)
        product = dot_nt(held[...], w[0]).astype(LOW)
        for shift in range(plan.tensor):

            @pl.when(step == shift)
            def _():
                outs[shift][:, columns] = product


def branch_back(plan, place, part, middle, cot, near, far):
    half = plan.heads * HEAD // 2
    own = pl.BlockSpec((plan.own, plan.width), lambda i, place: (place[1], 0))
    mine = pl.BlockSpec((plan.own, plan.width), lambda i, *_: (0, 0))
    weights = pl.BlockSpec(
        (1, half, plan.width), lambda i, place: (lax.rem(place[1] + i, plan.tensor), 0, 0)
    )
    return pl.pallas_call(
        functools.partial(branch_back_kernel, plan),
        grid_spec=pltpu.PrefetchScalarGridSpec(
            num_scalar_prefetch=1,
            grid=(plan.tensor,),
            in_specs=[mine, own, own, weights, weights],
            out_specs=[mine, mine]
            + [pl.BlockSpec((plan.own, 2 * half), lambda i, *_: (0, 0))] * plan.tensor,
            scratch_shapes=[pltpu.VMEM((plan.own, plan.width), LOW)],
        ),
        out_shape=[shape((plan.own, plan.width), F32), shape((plan.own, plan.width), LOW)]
        + [shape((plan.own, 2 * half), LOW)] * plan.tensor,
        compiler_params=params(60),
        cost_estimate=about(9),
        name="branch_back",
    )(place, part, middle, cot, near, far)


def tokens_back_kernel(place, part, tokens, grad_middle, out):
    normed, inverse = layer_norm(tokens[...].astype(F32))
    back = norm_back(part[...].astype(F32), normed, inverse)
    out[...] = (grad_middle[...] + back).astype(LOW)


def tokens_back(plan, place, part, tokens, grad_middle):
    mine = pl.BlockSpec((plan.own, plan.width), lambda i, *_: (0, 0))
    return pl.pallas_call(
        tokens_back_kernel,
        grid_spec=pltpu.PrefetchScalarGridSpec(
            num_scalar_prefetch=1,
            grid=(1,),
            in_specs=[
                mine,
                pl.BlockSpec((plan.own, plan.width), lambda i, place: (place[1], 0)),
                mine,
            ],
            out_specs=mine,
        ),
        out_shape=shape((plan.own, plan.width), LOW),
        compiler_params=params(60),
        cost_estimate=about(4),
        name="tokens_back",
    )(place, part, tokens, grad_middle)


def joined_rows(plan, place, parts, held):
    if len(parts) == 1:
        return parts[0][...]
    for shift, part in enumerate(parts):
        origin = lax.rem(place[1] - shift + plan.tensor, plan.tensor)
        held[pl.ds(pl.multiple_of(origin * plan.own, 16), plan.own), :] = part[...]
    return held[...]


def away_kernel(plan, count, place, *refs):
    lhs, (rhs, out, held) = refs[:count], refs[count:]
    out[...] = dot_tn(joined_rows(plan, place, lhs, held), rhs[...]).astype(LOW)


def wgrad_away(plan, place, lhs, rhs):
    rows, columns = rhs.shape
    piece, count = plan.piece, plan.dp // 2
    return pl.pallas_call(
        functools.partial(away_kernel, plan, len(lhs)),
        grid_spec=pltpu.PrefetchScalarGridSpec(
            num_scalar_prefetch=1,
            grid=(count,),
            in_specs=[
                pl.BlockSpec((part.shape[0], piece), lambda i, place: (0, place[2 + i] ^ 1))
                for part in lhs
            ]
            + [pl.BlockSpec((rows, columns), lambda i, *_: (0, 0))],
            out_specs=pl.BlockSpec((piece, columns), lambda i, *_: (i, 0)),
            scratch_shapes=[pltpu.VMEM((rows, piece), LOW)],
        ),
        out_shape=shape((count * piece, columns), LOW),
        compiler_params=params(60),
        cost_estimate=about(8),
        name="wgrad_away",
    )(place, *lhs, rhs)


def keep_kernel(plan, arrays, count, place, *refs):
    lhs, (rhs, recv, a_keep, a_send, b_keep, b_send, held) = refs[:arrays], refs[arrays:]
    step = pl.program_id(0)
    product = dot_tn(joined_rows(plan, place, lhs, held), rhs[...])
    total = (product + recv[...].astype(F32)).astype(LOW)
    half = total.shape[1] // 2

    @pl.when(step < count // 2)
    def _():
        a_keep[...] = total[:, :half]

    @pl.when(step >= count // 2)
    def _():
        a_send[...] = total[:, :half]

    @pl.when(step % 2 == 0)
    def _():
        b_keep[...] = total[:, half:]

    @pl.when(step % 2 == 1)
    def _():
        b_send[...] = total[:, half:]


def wgrad_keep(plan, place, lhs, rhs, recv):
    rows, columns = rhs.shape
    piece, count = plan.piece, plan.dp // 2
    half = count // 2
    block = lambda index: pl.BlockSpec((piece, columns // 2), index)
    return pl.pallas_call(
        functools.partial(keep_kernel, plan, len(lhs), count),
        grid_spec=pltpu.PrefetchScalarGridSpec(
            num_scalar_prefetch=1,
            grid=(count,),
            in_specs=[
                pl.BlockSpec((part.shape[0], piece), lambda i, place: (0, place[2 + i]))
                for part in lhs
            ]
            + [
                pl.BlockSpec((rows, columns), lambda i, *_: (0, 0)),
                pl.BlockSpec((piece, columns), lambda i, *_: (i, 0)),
            ],
            out_specs=[
                block(lambda i, *_: (jnp.minimum(i, half - 1), 0)),
                block(lambda i, *_: (jnp.maximum(i - half, 0), 0)),
                block(lambda i, *_: (i // 2, 0)),
                block(lambda i, *_: (i // 2, 0)),
            ],
            scratch_shapes=[pltpu.VMEM((rows, piece), LOW)],
        ),
        out_shape=[shape((half * piece, columns // 2), LOW)] * 4,
        compiler_params=params(60),
        cost_estimate=about(9),
        name="wgrad_keep",
    )(place, *lhs, rhs, recv)


def stage_kernel(piece, a, a_got, b, b_got, a_keep, a_send, b_keep, b_send):
    total = a[...].astype(F32) + a_got[...].astype(F32)
    half = total.shape[0] // 2
    a_keep[...] = total[:half].astype(LOW)
    a_send[...] = total[half:].astype(LOW)
    for at in range(0, 2 * half, 2 * piece):
        for start, out in ((at, b_keep), (at + piece, b_send)):
            rows = slice(start, start + piece)
            total = b[rows, :].astype(F32) + b_got[rows, :].astype(F32)
            out[at // 2 : at // 2 + piece, :] = total.astype(LOW)


def wgrad_stage(piece, *arrays):
    rows, columns = arrays[0].shape
    tile = min(256, columns)
    block = lambda size: pl.BlockSpec((size, tile), lambda i: (0, i))
    return pl.pallas_call(
        functools.partial(stage_kernel, piece),
        grid=(columns // tile,),
        in_specs=[block(rows)] * 4,
        out_specs=[block(rows // 2)] * 4,
        out_shape=[shape((rows // 2, columns), LOW)] * 4,
        compiler_params=params(60),
        cost_estimate=about(3),
        name="wgrad_stage",
    )(*arrays)


def finish_kernel(turned, a, a_got, b, b_got, out):
    half = a.shape[1]
    for way, (keep, got) in enumerate(((a, a_got), (b, b_got))):
        total = keep[...].astype(F32) + got[...].astype(F32)
        span = slice(way * half, (way + 1) * half)
        if turned:
            out[span, :] = total.T
        else:
            out[:, span] = total


def wgrad_finish(turned, *arrays):
    piece, half = arrays[0].shape
    return pl.pallas_call(
        functools.partial(finish_kernel, turned),
        out_shape=shape((2 * half, piece) if turned else (piece, 2 * half), F32),
        compiler_params=params(60),
        cost_estimate=about(3),
        name="wgrad_finish",
    )(*arrays)


def tie(values, *others):
    many = isinstance(values, (list, tuple))
    held = lax.optimization_barrier((tuple(values) if many else (values,)) + others)
    return list(held[: len(values)]) if many else held[0]


class WeightGradient:
    def __init__(self, plan, place, chain, lhs, rhs, turned=False):
        self.plan, self.place, self.chain = plan, place, chain
        self.lhs, self.rhs, self.turned = lhs, rhs, turned
        self.stage = 0

    def swap(self, array, bit):
        return lax.ppermute(array, "dp", xor_pairs(self.plan.dp, 1 << bit))

    def away(self):
        sent = self.chain.run(lambda r: wgrad_away(self.plan, self.place, self.lhs, r), self.rhs)
        self.recv = self.swap(sent, 0)

    def keep(self):
        self.a_keep, self.a_send, self.b_keep, self.b_send = self.chain.run(
            lambda r: wgrad_keep(self.plan, self.place, self.lhs, self.rhs, r), self.recv
        )

    def send(self):
        upwards = list(range(1, self.plan.bits))
        a, b = self.chain.after(self.a_send, self.b_send)
        self.a_got = self.swap(a, upwards[self.stage])
        self.b_got = self.swap(b, upwards[-1 - self.stage])
        self.stage += 1

    def wait(self):
        self.a_got, self.b_got = self.chain.wait(self.a_got, self.b_got)

    def add(self):
        self.a_keep, self.a_send, self.b_keep, self.b_send = self.chain.run(
            lambda *p: wgrad_stage(self.plan.piece, *p),
            self.a_keep,
            self.a_got,
            self.b_keep,
            self.b_got,
        )

    def finish(self):
        while self.stage < self.plan.bits - 1:
            self.add()
            self.send()
        return self.chain.run(
            lambda *p: wgrad_finish(self.turned, *p),
            self.a_keep,
            self.a_got,
            self.b_keep,
            self.b_got,
        )


class Chain:
    def __init__(self, last):
        self.last = last

    def after(self, *values):
        held = lax.optimization_barrier(values + (self.last,))
        return held[0] if len(values) == 1 else list(held[:-1])

    def wait(self, *values):
        held = lax.optimization_barrier(values + (self.last,))
        self.last = held[0]
        return held[0] if len(values) == 1 else list(held[:-1])

    def run(self, step, *values):
        held = self.after(*values)
        out = step(*held) if len(values) > 1 else step(held)
        self.last = out[0] if isinstance(out, (list, tuple)) else out
        return out


def add_kernel(middle, part, out):
    out[...] = (middle[...] + part[...].astype(F32)).astype(LOW)


def add_residual(middle, part):
    rows, width = middle.shape
    block = pl.BlockSpec((rows // 4, width), lambda i: (i, 0))
    return pl.pallas_call(
        add_kernel,
        grid=(4,),
        in_specs=[block, block],
        out_specs=block,
        out_shape=shape((rows, width), LOW),
        compiler_params=params(60),
        cost_estimate=about(6),
        name="add_residual",
    )(middle, part)


def body(mesh, tokens, w_query, w_key, w_value, w_out, w_gate, w_up, w_down, cotangent, slot_parent):
    plan = Plan(mesh, tokens.shape[0], tokens.shape[1], w_query.shape[1] // HEAD, w_gate.shape[1])
    me = lax.axis_index("dp")
    z = lax.axis_index("tensor")
    place = jnp.stack([me, z] + [me ^ relative for relative in kept_order(plan)]).astype(jnp.int32)
    cosine, sine = (jnp.asarray(table) for table in rope_tables())
    n = plan.spread
    wide = n * HEAD

    def swap(array, mask):
        return lax.ppermute(array, "dp", xor_pairs(plan.dp, mask))

    def exchange(parts):
        return [parts[0]] + [swap(parts[d], d * plan.rest) for d in range(1, n)]

    def shifted(array, shift):
        return lax.ppermute(
            array, "tensor", [(i, (i + shift) % plan.tensor) for i in range(plan.tensor)]
        )

    half = w_out.shape[0] // 2
    mine = lax.dynamic_slice_in_dim(w_out, (me % 2) * half, half, 0)
    near = lax.all_gather(mine, "tensor", axis=0, tiled=False)

    normed_one, *sends = project_qkv(
        plan, slot_parent, place, tokens, w_query, w_key, w_value, cosine, sine
    )
    chain = Chain(normed_one)
    parts = exchange(sends)
    seeds = [chain.run(lambda cot: grad_hidden_of(cot, w_down, 0), cotangent)]
    parts = chain.wait(*parts)
    kv = jnp.stack([part[1:] for part in parts])[None]
    mask = 1
    while mask < plan.rest:
        kv = jnp.concatenate([kv, swap(kv, mask)], axis=0)
        mask *= 2
    seeds.append(chain.run(lambda cot: grad_hidden_of(cot, w_down, 1), cotangent))
    kv = chain.wait(kv.reshape(plan.dp * 2 * plan.slots, BLOCK, HEAD))
    attended_parts = exchange(chain.run(lambda *p: attend(plan, slot_parent, place, p, kv), *parts))
    attended = chain.run(lambda *p: gather_heads(plan, place, p), *attended_parts)
    everyone = lax.all_gather(tie(attended, near), "tensor", axis=0, tiled=False)
    near = chain.after(near)
    far = swap(near, 1)
    middle, normed_two = chain.run(
        lambda e, f: project_out(plan, place, tokens, e, near, f), everyone, far
    )

    partial_two, hidden, grad_gate_proj, grad_up_proj = chain.run(
        lambda v: feed_forward(plan, place, v, seeds, w_gate, w_up), normed_two
    )
    grad_normed_two = lax.psum_scatter(partial_two, "tensor", scatter_dimension=0, tiled=True)
    down = WeightGradient(plan, place, chain, [cotangent], hidden, turned=True)
    gate = WeightGradient(plan, place, chain, [normed_two], grad_gate_proj)
    up = WeightGradient(plan, place, chain, [normed_two], grad_up_proj)
    down.away()
    gate.away()
    down.keep()
    down.send()
    gate.keep()
    gate.send()
    up.away()
    mine_all = lax.dynamic_slice_in_dim(chain.after(everyone), z * plan.own, plan.own, 1)
    mine_all = mine_all.transpose(1, 0, 2).reshape(plan.own, plan.width)
    down.wait()

    grad_middle, grad_branch, *chunks = chain.run(
        lambda g: branch_back(plan, place, g, middle, cotangent, near, far), grad_normed_two
    )
    sources = [chunks[0]] + [shifted(chunks[shift], shift) for shift in range(1, plan.tensor)]
    branch_out = chain.run(lambda h: project_down(h, w_down), hidden)
    gate.wait()
    scattered = chain.run(lambda *p: scatter_heads(plan, place, p), *sources)
    grads = exchange(scattered)
    output_part = lax.psum(chain.after(branch_out), "tensor")
    out = WeightGradient(plan, place, chain, [grad_branch], mine_all, turned=True)
    out.away()
    down.add()
    out.keep()
    grads = chain.wait(*grads)
    out.send()
    *grad_queries, grad_near, grad_far = chain.run(
        lambda *g: attend_back(plan, slot_parent, place, parts, kv, g), *grads
    )
    out.wait()

    grad_far = chain.after(grad_far).reshape(plan.rest - 1, n, 2, plan.rows, HEAD)
    grad_near = grad_near.reshape(1, n, 2, plan.rows, HEAD)
    mask = plan.rest // 2
    while mask >= 1:
        got = swap(grad_far[mask - 1 : 2 * mask - 1], mask)
        if mask == 1:
            out.add()
            got = chain.wait(got)
        got = got.astype(F32)
        grad_near = grad_near + got[:1]
        if mask > 1:
            grad_far = (grad_far[: mask - 1].astype(F32) + got[1:]).astype(LOW)
        mask //= 2
    backs = chain.wait(
        *(
            jnp.concatenate([grad_queries[d][None], grad_near[0, d].astype(LOW)], axis=0)
            for d in range(n)
        )
    )
    backs = exchange(backs)
    up.keep()
    gate.add()
    partial_one, turned = chain.run(
        lambda *p: turn_back(
            plan, slot_parent, place, cosine, sine, (w_query, w_key, w_value), p
        ),
        *backs,
    )
    grad_normed_one = lax.psum_scatter(partial_one, "tensor", scatter_dimension=0, tiled=True)
    out.send()
    qkv = WeightGradient(plan, place, chain, [normed_one], turned)
    qkv.away()
    output = chain.run(lambda p: add_residual(middle, p), output_part)
    out.wait()
    out_partial = out.finish().astype(LOW)
    down.send()
    up.send()
    qkv.keep()
    grad_tokens_own = chain.run(
        lambda g: tokens_back(plan, place, g, tokens, grad_middle), grad_normed_one
    )
    grad_tokens = lax.all_gather(grad_tokens_own, "tensor", axis=0, tiled=True)
    down.wait()
    gate.send()
    up.wait()
    up.add()
    up.send()
    grad_down = down.finish()
    gate.wait()
    qkv.send()
    grad_gate = gate.finish()
    up.wait()
    grad_up = up.finish()
    qkv.wait()
    qkv.add()
    qkv.send()
    grad_qkv = qkv.finish()
    grad_out = lax.psum_scatter(
        tie(out_partial, grad_tokens), "tensor", scatter_dimension=0, tiled=True
    ).astype(F32)
    return (
        output,
        grad_tokens,
        grad_qkv[:, :wide],
        grad_qkv[:, wide : 2 * wide],
        grad_qkv[:, 2 * wide :],
        grad_out,
        grad_gate,
        grad_up,
        grad_down,
    )


def solution(mesh):
    in_specs = (
        P("dp", None),
        P(None, "tensor"),
        P(None, "tensor"),
        P(None, "tensor"),
        P("tensor", None),
        P(None, "tensor"),
        P(None, "tensor"),
        P("tensor", None),
        P("dp", None),
        P(),
    )
    out_specs = (
        P("dp", None),
        P("dp", None),
        P("dp", "tensor"),
        P("dp", "tensor"),
        P("dp", "tensor"),
        P("tensor", "dp"),
        P("dp", "tensor"),
        P("dp", "tensor"),
        P("tensor", "dp"),
    )
    return jax.shard_map(
        functools.partial(body, mesh),
        mesh=mesh,
        in_specs=in_specs,
        out_specs=out_specs,
        check_vma=False,
    )
```

```python
import functools
import math

import jax
import jax.numpy as jnp
import numpy as np
from jax import lax
from jax.experimental import pallas as pl
from jax.experimental.pallas import tpu as pltpu
from jax.sharding import PartitionSpec as P

HEAD = 128
BLOCK = 128
TRUNK_BLOCKS = 8
CHAIN = TRUNK_BLOCKS + 2
EPSILON = 1e-05
NEGATIVE = -1e30
SCALE = HEAD ** (-0.5)
LOW = jnp.bfloat16
F32 = jnp.float32
MIB = 1024 * 1024
PER_MICROSECOND = 8.0e+09

NT = (((1,), (1,)), ((), ()))
TN = (((0,), (0,)), ((), ()))


def dot(a, b):
    return jnp.dot(a, b, preferred_element_type=F32)


def dot_nt(a, b):
    return lax.dot_general(a, b, NT, preferred_element_type=F32)


def dot_tn(a, b):
    return lax.dot_general(a, b, TN, preferred_element_type=F32)


def shape(dims, dtype):
    return jax.ShapeDtypeStruct(dims, dtype)


def about(microseconds):
    return pl.CostEstimate(
        flops=int(microseconds * PER_MICROSECOND * Chain.weight), bytes_accessed=1, transcendentals=0
    )


def params(mib):
    return pltpu.CompilerParams(vmem_limit_bytes=mib * MIB)


def layer_norm(values):
    centered = values - jnp.mean(values, axis=-1, keepdims=True)
    variance = jnp.mean(centered * centered, axis=-1, keepdims=True)
    inverse = lax.rsqrt(variance + EPSILON)
    return (centered * inverse, inverse)


def norm_back(gradient, normed, inverse):
    return inverse * (
        gradient
        - jnp.mean(gradient, axis=-1, keepdims=True)
        - normed * jnp.mean(gradient * normed, axis=-1, keepdims=True)
    )


def rope_tables():
    frequency = np.exp(
        np.arange(HEAD // 2, dtype=np.float32) * np.float32(-2.0 * math.log(10000.0) / HEAD)
    ).astype(np.float32)
    angle = np.arange(CHAIN * BLOCK, dtype=np.float32)[:, None] * frequency[None, :]
    cosine, sine = np.cos(angle), np.sin(angle)
    return (
        np.concatenate([cosine, cosine], axis=1).astype(np.float32),
        np.concatenate([-sine, sine], axis=1).astype(np.float32),
    )


def depth_of(parent_ref, slot):
    def up(_, carry):
        at, depth = carry
        parent = jnp.where(at >= 0, parent_ref[jnp.maximum(at, 0)], -1)
        return parent, depth + jnp.where(parent >= 0, 1, 0).astype(jnp.int32)

    return lax.fori_loop(0, CHAIN - 1, up, (slot, jnp.int32(0)))[1]


def xor_pairs(count, mask):
    return [(index, index ^ mask) for index in range(count)]


class Plan:
    def __init__(self, mesh, rows, width, heads, ff):
        self.dp = mesh.shape["dp"]
        self.tensor = mesh.shape["tensor"]
        self.rows, self.width, self.heads, self.ff = rows, width, heads, ff
        self.slots = rows // BLOCK
        self.spread = heads
        self.rest = self.dp // heads
        self.bits = self.dp.bit_length() - 1
        self.piece = width // self.dp
        self.own = rows // self.tensor
        self.groups = 2 if self.own % 32 == 0 else 1
        self.part = rows // self.groups
        self.share = self.own // self.groups

    def own_rows(self, group):
        return pl.BlockSpec(
            (self.share, self.width), lambda i, place: (group * self.tensor + place[1], 0)
        )

    def own_part(self):
        return pl.BlockSpec((self.share, self.width), lambda i, place: (place[1], 0))


def fetch(weights, held, sems, kind):
    copies = [
        pltpu.make_async_copy(w, held.at[index], sems.at[index]) for index, w in enumerate(weights)
    ]

    @pl.when(kind == 0)
    def _():
        for copy in copies:
            copy.start()

    def wait():
        for index, copy in enumerate(copies):

            @pl.when(kind == index)
            def _():
                copy.wait()

    return wait


def qkv_kernel(plan, parent, place, x, wq, wk, wv, cosine, sine, normed, *rest):
    outs, stage = rest[: plan.spread], rest[-1]
    me = place[0]
    part = me // plan.rest
    depth = depth_of(parent, me * plan.slots + pl.program_id(0))
    rows = pl.ds(pl.multiple_of(depth * BLOCK, BLOCK), BLOCK)
    cos, sin = cosine[rows, :], sine[rows, :]
    low = layer_norm(x[...].astype(F32))[0].astype(LOW)
    normed[...] = low
    for kind, w in enumerate((wq, wk, wv)):
        y = dot(low, w[...])
        for head in range(plan.heads):
            yh = y[:, head * HEAD : (head + 1) * HEAD]
            if kind < 2:
                yh = yh * cos + pltpu.roll(yh, HEAD // 2, 1) * sin
            stage[head, kind] = yh.astype(LOW)
    for d in range(plan.spread):
        outs[d][...] = stage[part ^ d]


def kept_order(plan):
    return [
        sum(((at >> bit) & 1) << (plan.bits - 1 - bit) for bit in range(plan.bits - 1))
        for at in range(plan.dp // 2)
    ]


def project_qkv(plan, slot_parent, place, tokens, wq, wk, wv, cosine, sine):
    whole = lambda i, *_: (0, 0)
    once = pl.Buffered(buffer_count=1)
    wide = plan.heads * HEAD
    return pl.pallas_call(
        functools.partial(qkv_kernel, plan),
        grid_spec=pltpu.PrefetchScalarGridSpec(
            num_scalar_prefetch=2,
            grid=(plan.slots,),
            in_specs=[pl.BlockSpec((BLOCK, plan.width), lambda i, *_: (i, 0))]
            + [pl.BlockSpec((plan.width, wide), whole, pipeline_mode=once)] * 3
            + [pl.BlockSpec((CHAIN * BLOCK, HEAD), whole, pipeline_mode=once)] * 2,
            out_specs=[pl.BlockSpec((BLOCK, plan.width), lambda i, *_: (i, 0))]
            + [pl.BlockSpec((3, BLOCK, HEAD), lambda i, *_: (0, i, 0))] * plan.spread,
            scratch_shapes=[
                pltpu.VMEM((plan.heads, 3, BLOCK, HEAD), LOW),
            ],
        ),
        out_shape=[shape((plan.rows, plan.width), LOW)]
        + [shape((3, plan.rows, HEAD), LOW)] * plan.spread,
        compiler_params=params(60),
        cost_estimate=about(0),
        name="project_qkv",
    )(slot_parent, place, tokens, wq, wk, wv, cosine, sine)


def gather_chain(plan, parent, me, slot, kv, keys, values):
    count = jnp.int32(0)
    at = slot
    places = []
    for step in range(CHAIN):
        here = jnp.maximum(at, 0)
        relative = (here // plan.slots) ^ me
        block = (
            (relative % plan.rest) * plan.spread + relative // plan.rest
        ) * 2 * plan.slots + here % plan.slots
        keys[step * BLOCK : (step + 1) * BLOCK, :] = kv[block]
        values[step * BLOCK : (step + 1) * BLOCK, :] = kv[block + plan.slots]
        places.append(block)
        valid = at >= 0
        count = count + jnp.where(valid, 1, 0).astype(jnp.int32)
        at = jnp.where(valid, parent[here], -1)
    return count, places


def chain_weights(queries, keys, counts):
    scores = [dot_nt(k, q) * SCALE for q, k in zip(queries, keys)]
    key_at = lax.broadcasted_iota(jnp.int32, scores[0].shape, 0)
    query_at = lax.broadcasted_iota(jnp.int32, scores[0].shape, 1)
    own = (key_at >= BLOCK) | (key_at <= query_at)
    probs = []
    for score, count in zip(scores, counts):
        score = jnp.where(own & (key_at < count * BLOCK), score, NEGATIVE)
        raised = jnp.exp(score - jnp.max(score, axis=0, keepdims=True))
        probs.append(raised * (1.0 / jnp.sum(raised, axis=0, keepdims=True)))
    return probs


def attend_kernel(plan, parent, place, *refs):
    n = plan.spread
    q_refs, kv, o_refs, keys, values = refs[:n], refs[n], refs[n + 1 : 2 * n + 1], refs[-2], refs[-1]
    me = place[0]

    def one(i, carry):
        rows = pl.ds(pl.multiple_of(i * BLOCK, BLOCK), BLOCK)
        slots = [(me ^ (d * plan.rest)) * plan.slots + i for d in range(n)]
        counts = [
            gather_chain(plan, parent, me, slots[d], kv, keys.at[d], values.at[d])[0]
            for d in range(n)
        ]
        queries = [q_refs[d][0, rows, :] for d in range(n)]
        probs = chain_weights(queries, [keys[d] for d in range(n)], counts)
        for d in range(n):
            o_refs[d][rows, :] = dot_tn(probs[d].astype(LOW), values[d]).astype(LOW)
        return carry

    lax.fori_loop(0, plan.slots, one, 0)


def attend(plan, slot_parent, place, parts, kv):
    n = plan.spread
    blocks = plan.dp * 2 * plan.slots
    return pl.pallas_call(
        functools.partial(attend_kernel, plan),
        grid_spec=pltpu.PrefetchScalarGridSpec(
            num_scalar_prefetch=2,
            grid=(1,),
            in_specs=[pl.BlockSpec((1, plan.rows, HEAD), lambda i, *_: (0, 0, 0))] * n
            + [pl.BlockSpec((blocks, BLOCK, HEAD), lambda i, *_: (0, 0, 0))],
            out_specs=[pl.BlockSpec((plan.rows, HEAD), lambda i, *_: (0, 0))] * n,
            scratch_shapes=[pltpu.VMEM((n, CHAIN * BLOCK, HEAD), LOW)] * 2,
        ),
        out_shape=[shape((plan.rows, HEAD), LOW)] * n,
        compiler_params=params(60),
        cost_estimate=about(0),
        name="attend",
    )(slot_parent, place, *parts, kv)


def attend_back_kernel(plan, parent, place, *refs):
    n = plan.spread
    q_refs, kv, g_refs = refs[:n], refs[n], refs[n + 1 : 2 * n + 1]
    dq_refs = refs[2 * n + 1 : 3 * n + 1]
    near, far, keys, values, total = refs[3 * n + 1 :]
    me = place[0]
    total[...] = jnp.zeros_like(total)

    def one(i, carry):
        rows = pl.ds(pl.multiple_of(i * BLOCK, BLOCK), BLOCK)
        slots = [(me ^ (d * plan.rest)) * plan.slots + i for d in range(n)]
        chains = [
            gather_chain(plan, parent, me, slots[d], kv, keys.at[d], values.at[d])
            for d in range(n)
        ]
        queries = [q_refs[d][0, rows, :] for d in range(n)]
        grads = [g_refs[d][rows, :] for d in range(n)]
        probs = chain_weights(queries, [keys[d] for d in range(n)], [chain[0] for chain in chains])
        for d in range(n):
            grad_prob = dot_nt(values[d], grads[d])
            inner = jnp.sum(grad_prob * probs[d], axis=0, keepdims=True)
            grad_scores = (probs[d] * (grad_prob - inner)).astype(LOW)
            dv = dot(probs[d].astype(LOW), grads[d])
            dk = dot(grad_scores, queries[d]) * SCALE
            dq_refs[d][rows, :] = (dot_tn(grad_scores, keys[d]) * SCALE).astype(LOW)
            for step, block in enumerate(chains[d][1]):
                span = slice(step * BLOCK, (step + 1) * BLOCK)
                total[block] = total[block] + dk[span]
                total[block + plan.slots] = total[block + plan.slots] + dv[span]
        return carry

    lax.fori_loop(0, plan.slots, one, 0)
    half = near.shape[0]
    near[...] = total[:half]
    far[...] = total[half:].astype(LOW)


def attend_back(plan, slot_parent, place, parts, kv, grads):
    n = plan.spread
    blocks = plan.dp * 2 * plan.slots
    near = n * 2 * plan.slots
    return pl.pallas_call(
        functools.partial(attend_back_kernel, plan),
        grid_spec=pltpu.PrefetchScalarGridSpec(
            num_scalar_prefetch=2,
            grid=(1,),
            in_specs=[pl.BlockSpec((1, plan.rows, HEAD), lambda i, *_: (0, 0, 0))] * n
            + [pl.BlockSpec((blocks, BLOCK, HEAD), lambda i, *_: (0, 0, 0))]
            + [pl.BlockSpec((plan.rows, HEAD), lambda i, *_: (0, 0))] * n,
            out_specs=[pl.BlockSpec((plan.rows, HEAD), lambda i, *_: (0, 0))] * n
            + [
                pl.BlockSpec((near, BLOCK, HEAD), lambda i, *_: (0, 0, 0)),
                pl.BlockSpec((blocks - near, BLOCK, HEAD), lambda i, *_: (0, 0, 0)),
            ],
            scratch_shapes=[pltpu.VMEM((n, CHAIN * BLOCK, HEAD), LOW)] * 2
            + [pltpu.VMEM((blocks, BLOCK, HEAD), F32)],
        ),
        out_shape=[shape((plan.rows, HEAD), LOW)] * n
        + [shape((near, BLOCK, HEAD), F32), shape((blocks - near, BLOCK, HEAD), LOW)],
        compiler_params=params(60),
        cost_estimate=about(23),
        name="attend_back",
    )(slot_parent, place, *parts, kv, *grads)


def combine_kernel(plan, *refs):
    n = plan.spread
    queries, (near, got), outs = refs[:n], refs[n : n + 2], refs[n + 2 :]
    for d in range(n):
        outs[d][0] = queries[d][...]
        for kind in range(2):
            for slot in range(plan.slots):
                block = (d * 2 + kind) * plan.slots + slot
                rows = slice(slot * BLOCK, (slot + 1) * BLOCK)
                total = near[block] + got[block].astype(F32)
                outs[d][kind + 1, rows, :] = total.astype(LOW)


def combine_back(plan, queries, near, got):
    n = plan.spread
    return pl.pallas_call(
        functools.partial(combine_kernel, plan),
        out_shape=[shape((3, plan.rows, HEAD), LOW)] * n,
        compiler_params=params(60),
        cost_estimate=about(3),
        name="combine_back",
    )(*queries, near, got)


def heads_kernel(plan, place, *refs):
    part = place[0] // plan.rest
    outs = refs[plan.spread :]
    for d in range(plan.spread):
        head = pl.ds(pl.multiple_of((part ^ d) * HEAD, HEAD), HEAD)
        for group, out in enumerate(outs):
            out[:, head] = refs[d][group * plan.part : (group + 1) * plan.part, :]


def gather_heads(plan, place, parts):
    wide = plan.heads * HEAD
    return pl.pallas_call(
        functools.partial(heads_kernel, plan),
        grid_spec=pltpu.PrefetchScalarGridSpec(
            num_scalar_prefetch=1,
            grid=(1,),
            in_specs=[pl.BlockSpec((plan.rows, HEAD), lambda i, *_: (0, 0))] * plan.spread,
            out_specs=[pl.BlockSpec((plan.part, wide), lambda i, *_: (0, 0))] * plan.groups,
        ),
        out_shape=[shape((plan.part, wide), LOW)] * plan.groups,
        compiler_params=params(60),
        cost_estimate=about(0),
        name="gather_heads",
    )(place, *parts)


def scatter_kernel(plan, place, *refs):
    part, z = place[0] // plan.rest, place[1]
    sources, outs = refs[: plan.tensor], refs[plan.tensor :]
    for shift in range(plan.tensor):
        origin = lax.rem(z - shift + plan.tensor, plan.tensor)
        for group in range(plan.groups):
            start = group * plan.part + origin * plan.share
            rows = pl.ds(pl.multiple_of(start, 16), plan.share)
            share = slice(group * plan.share, (group + 1) * plan.share)
            for d in range(plan.spread):
                head = pl.ds(pl.multiple_of((part ^ d) * HEAD, HEAD), HEAD)
                outs[d][rows, :] = sources[shift][share, head]


def scatter_heads(plan, place, sources):
    return pl.pallas_call(
        functools.partial(scatter_kernel, plan),
        grid_spec=pltpu.PrefetchScalarGridSpec(
            num_scalar_prefetch=1,
            grid=(1,),
            in_specs=[pl.BlockSpec((plan.own, plan.heads * HEAD), lambda i, *_: (0, 0))]
            * plan.tensor,
            out_specs=[pl.BlockSpec((plan.rows, HEAD), lambda i, *_: (0, 0))] * plan.spread,
        ),
        out_shape=[shape((plan.rows, HEAD), LOW)] * plan.spread,
        name="scatter_heads",
    )(place, *sources)


def turn_back_kernel(plan, parent, place, cosine, sine, wq, wk, wv, *refs):
    parts, (back, out, product) = refs[: plan.spread], refs[plan.spread :]
    me = place[0]
    part = me // plan.rest
    wide = plan.heads * HEAD

    @pl.when(pl.program_id(0) == 0)
    def _():
        for slot in range(plan.slots):
            depth = depth_of(parent, me * plan.slots + slot)
            table = pl.ds(pl.multiple_of(depth * BLOCK, BLOCK), BLOCK)
            cos, sin = cosine[table, :], sine[table, :]
            rows = slice(slot * BLOCK, (slot + 1) * BLOCK)
            for d in range(plan.spread):
                for kind in range(3):
                    value = parts[d][kind, rows, :]
                    if kind < 2:
                        value = value.astype(F32)
                        value = value * cos - pltpu.roll(value, HEAD // 2, 1) * sin
                    at = pl.multiple_of((kind * plan.heads + (part ^ d)) * HEAD, HEAD)
                    out[rows, pl.ds(at, HEAD)] = value.astype(LOW)

    total = 0.0
    for kind, w in enumerate((wq, wk, wv)):
        total = total + dot_nt(out[:, kind * wide : (kind + 1) * wide], w[...])
    product[...] = total
    for device in range(plan.tensor):
        for group in range(plan.groups):
            source = (group * plan.tensor + device) * plan.share
            target = (device * plan.groups + group) * plan.share
            back[target : target + plan.share, :] = product[
                source : source + plan.share, :
            ].astype(LOW)


def turn_back(plan, slot_parent, place, cosine, sine, weights, parts):
    whole = lambda i, *_: (0, 0)
    wide = plan.heads * HEAD
    tile = min(512, plan.width)
    return pl.pallas_call(
        functools.partial(turn_back_kernel, plan),
        grid_spec=pltpu.PrefetchScalarGridSpec(
            num_scalar_prefetch=2,
            grid=(plan.width // tile,),
            in_specs=[pl.BlockSpec((CHAIN * BLOCK, HEAD), whole)] * 2
            + [pl.BlockSpec((tile, wide), lambda i, *_: (i, 0))] * 3
            + [pl.BlockSpec((3, plan.rows, HEAD), lambda i, *_: (0, 0, 0))] * plan.spread,
            out_specs=[
                pl.BlockSpec((plan.rows, tile), lambda i, *_: (0, i)),
                pl.BlockSpec((plan.rows, 3 * wide), whole),
            ],
            scratch_shapes=[pltpu.VMEM((plan.rows, tile), F32)],
        ),
        out_shape=[shape((plan.rows, plan.width), LOW), shape((plan.rows, 3 * wide), LOW)],
        compiler_params=params(60),
        cost_estimate=about(13),
        name="turn_back",
    )(slot_parent, place, cosine, sine, *weights, *parts)


def out_kernel(plan, place, x, att, near, far, middle, normed):
    half = plan.heads * HEAD // 2
    core = place[0] % 2
    total = x[...].astype(F32)
    for z in range(plan.tensor):
        for side, w in ((core, near), (1 - core, far)):
            columns = pl.ds(pl.multiple_of(side * half, half), half)
            total = total + dot(att[z, :, columns], w[z])
    middle[...] = total
    normed[...] = layer_norm(total)[0].astype(LOW)


def project_out(plan, place, group, tokens, att, near, far):
    half = plan.heads * HEAD // 2
    count = 2
    rows = plan.part // count
    weights = pl.BlockSpec(
        (plan.tensor, half, plan.width),
        lambda i, *_: (0, 0, 0),
        pipeline_mode=pl.Buffered(buffer_count=1),
    )
    out = pl.BlockSpec((rows, plan.width), lambda i, *_: (i, 0))
    return pl.pallas_call(
        functools.partial(out_kernel, plan),
        grid_spec=pltpu.PrefetchScalarGridSpec(
            num_scalar_prefetch=1,
            grid=(count,),
            in_specs=[
                pl.BlockSpec((rows, plan.width), lambda i, *_: (group * count + i, 0)),
                pl.BlockSpec((plan.tensor, rows, 2 * half), lambda i, *_: (0, i, 0)),
                weights,
                weights,
            ],
            out_specs=[out, out],
        ),
        out_shape=[shape((plan.part, plan.width), F32), shape((plan.part, plan.width), LOW)],
        compiler_params=params(60),
        cost_estimate=about(7),
        name="project_out",
    )(place, tokens, att, near, far)


def grad_hidden_kernel(cot, wd, out):
    out[...] = dot_nt(cot[...], wd[...])


def grad_hidden_of(cot, wd):
    rows, width = cot.shape
    ff = wd.shape[0]
    tile = min(512, ff)
    return pl.pallas_call(
        grad_hidden_kernel,
        grid=(ff // tile,),
        in_specs=[
            pl.BlockSpec((rows, width), lambda i: (0, 0)),
            pl.BlockSpec((tile, width), lambda i: (i, 0)),
        ],
        out_specs=pl.BlockSpec((rows, tile), lambda i: (0, i)),
        out_shape=shape((rows, ff), F32),
        compiler_params=params(60),
        cost_estimate=about(0),
        name="grad_hidden",
    )(cot, wd)


def ff_kernel(tile, normed, seed, wg, wu, back, hidden, grad_gate, grad_up, *scratch):
    gate_held, up_held, results, total, in_sems, out_sems = scratch
    count = wg.shape[1] // tile
    spans = [slice(index * tile, (index + 1) * tile) for index in range(count)]
    arrivals = [
        [
            pltpu.make_async_copy(w.at[:, span], held.at[:, span], in_sems.at[which, index])
            for which, (w, held) in enumerate(((wg, gate_held), (wu, up_held)))
        ]
        for index, span in enumerate(spans)
    ]
    departures = [
        [
            pltpu.make_async_copy(
                results.at[which, :, span], out.at[:, span], out_sems.at[which, index]
            )
            for which, out in enumerate((hidden, grad_gate, grad_up))
        ]
        for index, span in enumerate(spans)
    ]
    for pair in arrivals:
        for copy in pair:
            copy.start()
    for index, span in enumerate(spans):
        for copy in arrivals[index]:
            copy.wait()
        gate = dot(normed[...], gate_held[:, span])
        up = dot(normed[...], up_held[:, span])
        grad_hidden = seed[:, span]
        s = 1.0 / (1.0 + jnp.exp(-gate))
        active = gate * s
        gu = (grad_hidden * active).astype(LOW)
        gg = (grad_hidden * up * s * (1.0 + gate * (1.0 - s))).astype(LOW)
        results[0, :, span] = (active * up).astype(LOW)
        results[1, :, span] = gg
        results[2, :, span] = gu
        for copy in departures[index]:
            copy.start()
        part = dot_nt(gg, gate_held[:, span]) + dot_nt(gu, up_held[:, span])
        if index == 0:
            total[...] = part
        elif index < count - 1:
            total[...] += part
        else:
            back[...] = (total[...] + part).astype(LOW)
    for triple in departures:
        for copy in triple:
            copy.wait()


def feed_forward(plan, place, group, normed, seed, wg, wu):
    rows, width = normed.shape
    ff = wg.shape[1]
    tile = min(512, ff // 2)
    whole = pl.BlockSpec((rows, width), lambda i: (0, 0))
    anywhere = pl.BlockSpec(memory_space=pl.ANY)
    return pl.pallas_call(
        functools.partial(ff_kernel, tile),
        grid=(1,),
        in_specs=[whole, pl.BlockSpec((rows, ff), lambda i: (group, 0)), anywhere, anywhere],
        out_specs=[whole, anywhere, anywhere, anywhere],
        out_shape=[shape((rows, width), LOW)] + [shape((rows, ff), LOW)] * 3,
        scratch_shapes=[
            pltpu.VMEM((width, ff), LOW),
            pltpu.VMEM((width, ff), LOW),
            pltpu.VMEM((3, rows, ff), LOW),
            pltpu.VMEM((rows, width), F32),
            pltpu.SemaphoreType.DMA((2, ff // tile)),
            pltpu.SemaphoreType.DMA((3, ff // tile)),
        ],
        compiler_params=params(62),
        cost_estimate=about(17),
        name="feed_forward",
    )(normed, seed, wg, wu)


def down_kernel(plan, *refs):
    hiddens, (w, out) = refs[: plan.groups], refs[plan.groups :]
    for group, hidden in enumerate(hiddens):
        rows = slice(group * plan.part, (group + 1) * plan.part)
        out[rows, :] = dot(hidden[...], w[...]).astype(LOW)


def project_down(plan, hiddens, w):
    ff, width = w.shape
    tile = min(512, width)
    return pl.pallas_call(
        functools.partial(down_kernel, plan),
        grid=(width // tile,),
        in_specs=[pl.BlockSpec((plan.part, ff), lambda i: (0, 0))] * plan.groups
        + [pl.BlockSpec((ff, tile), lambda i: (0, i))],
        out_specs=pl.BlockSpec((plan.rows, tile), lambda i: (0, i)),
        out_shape=shape((plan.rows, width), LOW),
        compiler_params=params(60),
        cost_estimate=about(11),
        name="project_down",
    )(*hiddens, w)


def branch_back_kernel(plan, place, *refs):
    count = plan.groups
    parts, middles, cots = refs[:count], refs[count : 2 * count], refs[2 * count : 3 * count]
    near, far, grad_middle, low = refs[3 * count : 3 * count + 4]
    outs, (near_held, far_held, sems) = refs[3 * count + 4 : -3], refs[-3:]
    core, z = place[0] % 2, place[1]
    half = plan.heads * HEAD // 2
    sides = ((core, near, near_held), (1 - core, far, far_held))
    copies = [
        [
            pltpu.make_async_copy(
                w.at[lax.rem(z + shift, plan.tensor)], held.at[shift], sems.at[index, shift]
            )
            for index, (_, w, held) in enumerate(sides)
        ]
        for shift in range(plan.tensor)
    ]
    for pair in copies:
        for copy in pair:
            copy.start()
    for group in range(count):
        rows = slice(group * plan.share, (group + 1) * plan.share)
        normed, inverse = layer_norm(middles[group][...])
        back = norm_back(parts[group][...].astype(F32), normed, inverse)
        grad = cots[group][...].astype(F32) + back
        grad_middle[rows, :] = grad
        low[rows, :] = grad.astype(LOW)
    for shift in range(plan.tensor):
        for copy, (side, _, held) in zip(copies[shift], sides):
            copy.wait()
            columns = pl.ds(pl.multiple_of(side * half, half), half)
            outs[shift][:, columns] = dot_nt(low[...], held[shift]).astype(LOW)


def branch_back(plan, place, parts, middles, cot, near, far):
    half = plan.heads * HEAD // 2
    own = pl.BlockSpec((plan.own, plan.width), lambda i, *_: (0, 0))
    share = pl.BlockSpec((plan.share, plan.width), lambda i, *_: (0, 0))
    anywhere = pl.BlockSpec(memory_space=pl.ANY)
    return pl.pallas_call(
        functools.partial(branch_back_kernel, plan),
        grid_spec=pltpu.PrefetchScalarGridSpec(
            num_scalar_prefetch=1,
            grid=(1,),
            in_specs=[share] * plan.groups
            + [plan.own_part()] * plan.groups
            + [plan.own_rows(group) for group in range(plan.groups)]
            + [anywhere, anywhere],
            out_specs=[own, own]
            + [pl.BlockSpec((plan.own, 2 * half), lambda i, *_: (0, 0))] * plan.tensor,
            scratch_shapes=[pltpu.VMEM((plan.tensor, half, plan.width), LOW)] * 2
            + [pltpu.SemaphoreType.DMA((2, plan.tensor))],
        ),
        out_shape=[shape((plan.own, plan.width), F32), shape((plan.own, plan.width), LOW)]
        + [shape((plan.own, 2 * half), LOW)] * plan.tensor,
        compiler_params=params(60),
        cost_estimate=about(9),
        name="branch_back",
    )(place, *parts, *middles, *([cot] * plan.groups), near, far)


def tokens_back_kernel(plan, place, part, *refs):
    tokens, (grad_middle, out) = refs[: plan.groups], refs[plan.groups :]
    for group in range(plan.groups):
        rows = slice(group * plan.share, (group + 1) * plan.share)
        normed, inverse = layer_norm(tokens[group][...].astype(F32))
        back = norm_back(part[rows, :].astype(F32), normed, inverse)
        out[rows, :] = (grad_middle[rows, :] + back).astype(LOW)


def tokens_back(plan, place, part, tokens, grad_middle):
    own = pl.BlockSpec((plan.own, plan.width), lambda i, *_: (0, 0))
    return pl.pallas_call(
        functools.partial(tokens_back_kernel, plan),
        grid_spec=pltpu.PrefetchScalarGridSpec(
            num_scalar_prefetch=1,
            grid=(1,),
            in_specs=[own] + [plan.own_rows(group) for group in range(plan.groups)] + [own],
            out_specs=own,
        ),
        out_shape=shape((plan.own, plan.width), LOW),
        compiler_params=params(60),
        cost_estimate=about(4),
        name="tokens_back",
    )(place, part, *([tokens] * plan.groups), grad_middle)


def products(lhs, rhs):
    total, start = 0.0, 0
    for index, right in enumerate(rhs):
        rows = right.shape[0]
        left = lhs[index][...] if len(lhs) > 1 else lhs[0][start : start + rows, :]
        total = total + dot_tn(left, right[...])
        start += rows
    return total


def away_kernel(count, place, *refs):
    lhs, rhs, out = refs[:count], refs[count:-1], refs[-1]
    out[...] = products(lhs, rhs).astype(LOW)


def wgrad_away(plan, place, lhs, rhs):
    columns = rhs[0].shape[1]
    piece, count = plan.piece, plan.dp // 2
    return pl.pallas_call(
        functools.partial(away_kernel, len(lhs)),
        grid_spec=pltpu.PrefetchScalarGridSpec(
            num_scalar_prefetch=1,
            grid=(count,),
            in_specs=[
                pl.BlockSpec((part.shape[0], piece), lambda i, place: (0, place[2 + i] ^ 1))
                for part in lhs
            ]
            + [pl.BlockSpec(part.shape, lambda i, *_: (0, 0)) for part in rhs],
            out_specs=pl.BlockSpec((piece, columns), lambda i, *_: (i, 0)),
        ),
        out_shape=shape((count * piece, columns), LOW),
        compiler_params=params(60),
        cost_estimate=about(8),
        name="wgrad_away",
    )(place, *lhs, *rhs)


def keep_kernel(arrays, count, place, *refs):
    lhs, rhs = refs[:arrays], refs[arrays:-5]
    recv, a_keep, a_send, b_keep, b_send = refs[-5:]
    step = pl.program_id(0)
    total = (products(lhs, rhs) + recv[...].astype(F32)).astype(LOW)
    half = total.shape[1] // 2

    @pl.when(step < count // 2)
    def _():
        a_keep[...] = total[:, :half]

    @pl.when(step >= count // 2)
    def _():
        a_send[...] = total[:, :half]

    @pl.when(step % 2 == 0)
    def _():
        b_keep[...] = total[:, half:]

    @pl.when(step % 2 == 1)
    def _():
        b_send[...] = total[:, half:]


def wgrad_keep(plan, place, lhs, rhs, recv):
    columns = rhs[0].shape[1]
    piece, count = plan.piece, plan.dp // 2
    half = count // 2
    block = lambda index: pl.BlockSpec((piece, columns // 2), index)
    return pl.pallas_call(
        functools.partial(keep_kernel, len(lhs), count),
        grid_spec=pltpu.PrefetchScalarGridSpec(
            num_scalar_prefetch=1,
            grid=(count,),
            in_specs=[
                pl.BlockSpec((part.shape[0], piece), lambda i, place: (0, place[2 + i]))
                for part in lhs
            ]
            + [pl.BlockSpec(part.shape, lambda i, *_: (0, 0)) for part in rhs]
            + [pl.BlockSpec((piece, columns), lambda i, *_: (i, 0))],
            out_specs=[
                block(lambda i, *_: (jnp.minimum(i, half - 1), 0)),
                block(lambda i, *_: (jnp.maximum(i - half, 0), 0)),
                block(lambda i, *_: (i // 2, 0)),
                block(lambda i, *_: (i // 2, 0)),
            ],
        ),
        out_shape=[shape((half * piece, columns // 2), LOW)] * 4,
        compiler_params=params(60),
        cost_estimate=about(9),
        name="wgrad_keep",
    )(place, *lhs, *rhs, recv)


def stage_kernel(piece, a, a_got, b, b_got, a_keep, a_send, b_keep, b_send):
    total = a[...].astype(F32) + a_got[...].astype(F32)
    half = total.shape[0] // 2
    a_keep[...] = total[:half].astype(LOW)
    a_send[...] = total[half:].astype(LOW)
    for at in range(0, 2 * half, 2 * piece):
        for start, out in ((at, b_keep), (at + piece, b_send)):
            rows = slice(start, start + piece)
            total = b[rows, :].astype(F32) + b_got[rows, :].astype(F32)
            out[at // 2 : at // 2 + piece, :] = total.astype(LOW)


def wgrad_stage(piece, *arrays):
    rows, columns = arrays[0].shape
    tile = min(256, columns)
    block = lambda size: pl.BlockSpec((size, tile), lambda i: (0, i))
    return pl.pallas_call(
        functools.partial(stage_kernel, piece),
        grid=(columns // tile,),
        in_specs=[block(rows)] * 4,
        out_specs=[block(rows // 2)] * 4,
        out_shape=[shape((rows // 2, columns), LOW)] * 4,
        compiler_params=params(60),
        cost_estimate=about(3),
        name="wgrad_stage",
    )(*arrays)


def finish_kernel(turned, a, a_got, b, b_got, out):
    half = a.shape[1]
    for way, (keep, got) in enumerate(((a, a_got), (b, b_got))):
        total = keep[...].astype(F32) + got[...].astype(F32)
        span = slice(way * half, (way + 1) * half)
        if turned:
            out[span, :] = total.T
        else:
            out[:, span] = total


def wgrad_finish(turned, *arrays):
    piece, half = arrays[0].shape
    return pl.pallas_call(
        functools.partial(finish_kernel, turned),
        out_shape=shape((2 * half, piece) if turned else (piece, 2 * half), F32),
        compiler_params=params(60),
        cost_estimate=about(3),
        name="wgrad_finish",
    )(*arrays)


def split_kernel(*refs):
    arrays, outs, held = refs[:4], refs[4:-1], refs[-1]
    finish_kernel(False, *arrays, held)
    width = outs[0].shape[1]
    for index, out in enumerate(outs):
        out[...] = held[:, index * width : (index + 1) * width]


def wgrad_finish_split(*arrays):
    piece, half = arrays[0].shape
    return pl.pallas_call(
        split_kernel,
        out_shape=[shape((piece, 2 * half // 3), F32)] * 3,
        scratch_shapes=[pltpu.VMEM((piece, 2 * half), F32)],
        compiler_params=params(60),
        cost_estimate=about(3),
        name="wgrad_finish_split",
    )(*arrays)


def chunks_kernel(plan, place, *refs):
    arrays, chunks, held = refs[:4], refs[4:-1], refs[-1]
    finish_kernel(True, *arrays, held)
    rows = plan.heads * HEAD
    for index, chunk in enumerate(chunks):
        chunk[...] = held[ring_rows(plan, place, index, rows), :].astype(LOW)


def wgrad_finish_chunks(plan, place, *arrays):
    piece, half = arrays[0].shape
    rows = plan.heads * HEAD
    return pl.pallas_call(
        functools.partial(chunks_kernel, plan),
        grid_spec=pltpu.PrefetchScalarGridSpec(
            num_scalar_prefetch=1,
            grid=(1,),
            in_specs=[pl.BlockSpec((piece, half), lambda i, *_: (0, 0))] * 4,
            out_specs=[pl.BlockSpec((rows, piece), lambda i, *_: (0, 0))] * plan.tensor,
            scratch_shapes=[pltpu.VMEM((2 * half, piece), F32)],
        ),
        out_shape=[shape((rows, piece), LOW)] * plan.tensor,
        compiler_params=params(60),
        cost_estimate=about(4),
        name="wgrad_finish_chunks",
    )(place, *arrays)


def tie(values, *others):
    many = isinstance(values, (list, tuple))
    held = lax.optimization_barrier((tuple(values) if many else (values,)) + others)
    return list(held[: len(values)]) if many else held[0]


class WeightGradient:
    def __init__(self, plan, place, chain, lhs, rhs, turned=False, chunks=False, split=False):
        self.chunks, self.split = chunks, split
        self.plan, self.place, self.chain = plan, place, chain
        self.lhs, self.rhs, self.turned = lhs, rhs, turned
        self.stage = 0

    def swap(self, array, bit):
        return lax.ppermute(array, "dp", xor_pairs(self.plan.dp, 1 << bit))

    def away(self):
        sent = self.chain.run(
            lambda *r: wgrad_away(self.plan, self.place, self.lhs, r), *self.rhs
        )
        self.recv = self.swap(sent, 0)

    def keep(self):
        self.a_keep, self.a_send, self.b_keep, self.b_send = self.chain.run(
            lambda r: wgrad_keep(self.plan, self.place, self.lhs, self.rhs, r), self.recv
        )

    def send(self):
        upwards = list(range(1, self.plan.bits))
        a, b = self.chain.after(self.a_send, self.b_send)
        self.a_got = self.swap(a, upwards[self.stage])
        self.b_got = self.swap(b, upwards[-1 - self.stage])
        self.stage += 1

    def wait(self):
        self.a_got, self.b_got = self.chain.wait(self.a_got, self.b_got)

    def took(self):
        self.recv = self.chain.wait(self.recv)

    def add(self):
        self.a_keep, self.a_send, self.b_keep, self.b_send = self.chain.run(
            lambda *p: wgrad_stage(self.plan.piece, *p),
            self.a_keep,
            self.a_got,
            self.b_keep,
            self.b_got,
        )

    def finish(self):
        while self.stage < self.plan.bits - 1:
            self.add()
            self.send()
        return self.chain.run(
            lambda *p: (
                wgrad_finish_chunks(self.plan, self.place, *p)
                if self.chunks
                else wgrad_finish_split(*p)
                if self.split
                else wgrad_finish(self.turned, *p)
            ),
            self.a_keep,
            self.a_got,
            self.b_keep,
            self.b_got,
        )


class Chain:
    weight = 1.0

    def __init__(self, last):
        self.last = last

    def after(self, *values):
        held = lax.optimization_barrier(values + (self.last,))
        return held[0] if len(values) == 1 else list(held[:-1])

    def wait(self, *values):
        held = lax.optimization_barrier(values + (self.last,))
        self.last = held[0]
        return held[0] if len(values) == 1 else list(held[:-1])

    def run(self, step, *values):
        held = self.after(*values)
        out = step(*held) if len(values) > 1 else step(held)
        self.last = out[0] if isinstance(out, (list, tuple)) else out
        return out


def shifted(plan, array, shift):
    pairs = [(i, (i + shift) % plan.tensor) for i in range(plan.tensor)]
    return lax.ppermute(array, "tensor", pairs)


class RingSum:
    def __init__(self, plan, chain, chunks):
        self.plan, self.chain, self.chunks, self.at = plan, chain, chunks, 1
        self.moving = shifted(plan, chunks[0], 1)

    def step(self):
        if self.at < self.plan.tensor - 1:
            got, mine = self.chain.wait(self.moving, self.chunks[self.at])
            total = (got.astype(F32) + mine.astype(F32)).astype(LOW)
            self.chain.last = total
            self.moving = shifted(self.plan, total, 1)
            self.at += 1

    def finish(self):
        while self.at < self.plan.tensor - 1:
            self.step()
        return self.moving, self.chunks[-1]


def ring_rows(plan, place, step, rows):
    chunk = lax.rem(place[1] + (2 * plan.tensor - 1 - step), plan.tensor)
    return pl.ds(pl.multiple_of(chunk * rows, 16), rows)


def add_last_kernel(a, b, out):
    out[...] = a[...].astype(F32) + b[...].astype(F32)


def add_last(a, b):
    return pl.pallas_call(
        add_last_kernel,
        out_shape=shape(a.shape, F32),
        compiler_params=params(60),
        cost_estimate=about(2),
        name="add_last",
    )(a, b)


def add_kernel(plan, *refs):
    middles, (part, out) = refs[: plan.groups], refs[plan.groups :]
    step = pl.program_id(0)
    for group, middle in enumerate(middles):

        @pl.when(step // 2 == group)
        def _():
            out[...] = (middle[...] + part[...].astype(F32)).astype(LOW)


def add_residual(plan, middles, part):
    rows = plan.part // 2
    block = pl.BlockSpec((rows, plan.width), lambda i: (i, 0))
    return pl.pallas_call(
        functools.partial(add_kernel, plan),
        grid=(2 * plan.groups,),
        in_specs=[
            pl.BlockSpec(
                (rows, plan.width),
                lambda i, group=group: (jnp.clip(i - 2 * group, 0, 1), 0),
            )
            for group in range(plan.groups)
        ]
        + [block],
        out_specs=block,
        out_shape=shape((plan.rows, plan.width), LOW),
        compiler_params=params(60),
        cost_estimate=about(6),
        name="add_residual",
    )(*middles, part)


class State:
    pass


def body(mesh, tokens, w_query, w_key, w_value, w_out, w_gate, w_up, w_down, cotangent, slot_parent):
    plan = Plan(mesh, tokens.shape[0], tokens.shape[1], w_query.shape[1] // HEAD, w_gate.shape[1])
    me = lax.axis_index("dp")
    z = lax.axis_index("tensor")
    place = jnp.stack([me, z] + [me ^ relative for relative in kept_order(plan)]).astype(jnp.int32)
    cosine, sine = (jnp.asarray(table) for table in rope_tables())
    n = plan.spread
    wide = n * HEAD

    def swap(array, mask):
        return lax.ppermute(array, "dp", xor_pairs(plan.dp, mask))

    def exchange(parts):
        return [parts[0]] + [swap(parts[d], d * plan.rest) for d in range(1, n)]

    half = w_out.shape[0] // 2
    mine = lax.dynamic_slice_in_dim(w_out, (me % 2) * half, half, 0)
    near = lax.all_gather(mine, "tensor", axis=0, tiled=False)

    normed_one, *sends = project_qkv(
        plan, slot_parent, place, tokens, w_query, w_key, w_value, cosine, sine
    )
    chain = Chain(normed_one)
    parts = exchange(sends)
    seed = chain.run(lambda cot: grad_hidden_of(cot, w_down), cotangent)
    parts = chain.wait(*parts)
    kv = jnp.stack([part[1:] for part in parts])[None]
    mask = 1
    while mask < plan.rest:
        kv = jnp.concatenate([kv, swap(kv, mask)], axis=0)
        mask *= 2
    kv = chain.wait(kv.reshape(plan.dp * 2 * plan.slots, BLOCK, HEAD))
    attended_parts = exchange(chain.run(lambda *p: attend(plan, slot_parent, place, p, kv), *parts))
    attended = chain.run(lambda *p: gather_heads(plan, place, p), *attended_parts)
    everyone = [
        lax.all_gather(tie(part, near), "tensor", axis=0, tiled=False) for part in attended
    ]
    near = chain.after(near)
    far = swap(near, 1)

    middles, normed_two, hidden, grad_gate_proj, grad_up_proj, grad_normed_two = ([] for _ in range(6))
    for group in range(plan.groups):
        middle, normed = chain.run(
            lambda e, f: project_out(plan, place, group, tokens, e, near, f), everyone[group], far
        )
        partial_two, *rest = chain.run(
            lambda v: feed_forward(plan, place, group, v, seed, w_gate, w_up), normed
        )
        grad_normed_two.append(
            lax.psum_scatter(partial_two, "tensor", scatter_dimension=0, tiled=True)
        )
        middles.append(middle)
        normed_two.append(normed)
        for held, value in zip((hidden, grad_gate_proj, grad_up_proj), rest):
            held.append(value)
    state = State()
    down = WeightGradient(plan, place, chain, [cotangent], hidden, turned=True)
    gate = WeightGradient(plan, place, chain, normed_two, grad_gate_proj)
    up = WeightGradient(plan, place, chain, normed_two, grad_up_proj)
    out = WeightGradient(plan, place, chain, None, None, chunks=True)
    qkv = WeightGradient(plan, place, chain, None, None, split=True)

    def own():
        state.own = jnp.concatenate(
            [
                lax.dynamic_slice_in_dim(part, z * plan.share, plan.share, 1)
                .transpose(1, 0, 2)
                .reshape(plan.share, plan.width)
                for part in map(chain.after, everyone)
            ]
        )

    def branch():
        grad_middle, grad_branch, *chunks = chain.run(
            lambda *g: branch_back(plan, place, g, middles, cotangent, near, far),
            *grad_normed_two,
        )
        state.sources = [chunks[0]] + [
            shifted(plan, chunks[shift], shift) for shift in range(1, plan.tensor)
        ]
        state.grad_middle = grad_middle
        out.lhs, out.rhs = [grad_branch], [state.own]

    def output():
        branch_out = chain.run(lambda *h: project_down(plan, h, w_down), *hidden)
        state.part = lax.psum(branch_out, "tensor")

    def scatter():
        scattered = chain.run(lambda *p: scatter_heads(plan, place, p), *state.sources)
        state.grads = exchange(scattered)

    def heads():
        state.grads = chain.wait(*state.grads)

    def attend_step():
        *state.queries, state.near, state.far = chain.run(
            lambda *g: attend_back(plan, slot_parent, place, parts, kv, g), *state.grads
        )

    def sum_far():
        far_part = chain.after(state.far).reshape(plan.rest - 1, -1, BLOCK, HEAD)
        mask = plan.rest // 2
        while mask > 1:
            got = swap(far_part[mask - 1 : 2 * mask - 1], mask).astype(F32)
            state.near = state.near + got[0]
            far_part = (far_part[: mask - 1].astype(F32) + got[1:]).astype(LOW)
            mask //= 2
        state.got = swap(far_part.reshape(state.near.shape), 1)

    def sum_near():
        backs = chain.run(
            lambda g: combine_back(plan, state.queries, state.near, g), state.got
        )
        state.backs = exchange(backs)

    def arrive():
        state.backs = chain.wait(*state.backs)

    def turn():
        partial_one, turned = chain.run(
            lambda *p: turn_back(
                plan, slot_parent, place, cosine, sine, (w_query, w_key, w_value), p
            ),
            *state.backs,
        )
        state.one = lax.psum_scatter(partial_one, "tensor", scatter_dimension=0, tiled=True)
        qkv.lhs, qkv.rhs = [normed_one], [turned]

    def residual():
        state.output = chain.run(lambda p: add_residual(plan, middles, p), state.part)

    def tokens_step():
        grad_own = chain.run(
            lambda g: tokens_back(plan, place, g, tokens, state.grad_middle), state.one
        )
        state.tokens = lax.all_gather(grad_own, "tensor", axis=0, tiled=True)

    def gathered():
        state.tokens = chain.wait(state.tokens)

    def ring_start():
        state.ring = RingSum(plan, chain, chain.after(*state.out))

    def ring_end():
        got, mine = chain.wait(*state.ring.finish())
        state.out = chain.run(add_last, got, mine)

    def ring_step():
        state.ring.step()

    down.away()
    gate.away()
    down.keep()
    down.send()
    own()
    gate.keep()
    branch()
    output()
    down.wait()
    scatter()
    out.away()
    out.keep()
    heads()
    out.send()
    attend_step()
    out.wait()
    sum_far()
    out.add()
    sum_near()
    down.add()
    up.away()
    arrive()
    gate.send()
    turn()
    up.took()
    out.send()
    qkv.away()
    up.keep()
    gate.wait()
    out.wait()
    up.send()
    state.out = out.finish()
    gate.add()
    qkv.keep()
    residual()
    ring_start()
    down.send()
    gate.send()
    up.wait()
    Chain.weight = 0.03
    tokens_step()
    Chain.weight = 1.0
    state.ring.step()
    qkv.send()
    down.wait()
    up.add()
    up.send()
    state.down = down.finish()
    gate.wait()
    Chain.weight = 0.03
    state.gate = gate.finish()
    Chain.weight = 1.0
    state.ring.step()
    qkv.wait()
    qkv.add()
    qkv.send()
    ring_end()
    Chain.weight = 100.0
    state.qkv = qkv.finish()
    Chain.weight = 1.0
    state.up = up.finish()
    grad_tokens = (
        state.tokens
        .reshape(plan.tensor, plan.groups, plan.share, plan.width)
        .transpose(1, 0, 2, 3)
        .reshape(plan.rows, plan.width)
    )
    return (
        state.output,
        grad_tokens,
        *state.qkv,
        state.out,
        state.gate,
        state.up,
        state.down,
    )


def solution(mesh):
    in_specs = (
        P("dp", None),
        P(None, "tensor"),
        P(None, "tensor"),
        P(None, "tensor"),
        P("tensor", None),
        P(None, "tensor"),
        P(None, "tensor"),
        P("tensor", None),
        P("dp", None),
        P(),
    )
    out_specs = (
        P("dp", None),
        P("dp", None),
        P("dp", "tensor"),
        P("dp", "tensor"),
        P("dp", "tensor"),
        P("tensor", "dp"),
        P("dp", "tensor"),
        P("dp", "tensor"),
        P("tensor", "dp"),
    )
    return jax.shard_map(
        functools.partial(body, mesh),
        mesh=mesh,
        in_specs=in_specs,
        out_specs=out_specs,
        check_vma=False,
    )
```

```python
import functools
import math

import jax
import jax.numpy as jnp
import numpy as np
from jax import lax
from jax.experimental import pallas as pl
from jax.experimental.pallas import tpu as pltpu
from jax.sharding import PartitionSpec as P

HEAD = 128
BLOCK = 128
TRUNK_BLOCKS = 8
CHAIN = TRUNK_BLOCKS + 2
EPSILON = 1e-05
NEGATIVE = -1e30
SCALE = HEAD ** (-0.5)
LOW = jnp.bfloat16
F32 = jnp.float32
MIB = 1024 * 1024
PER_MICROSECOND = 1.6e+10

NT = (((1,), (1,)), ((), ()))
TN = (((0,), (0,)), ((), ()))


def dot(a, b):
    return jnp.dot(a, b, preferred_element_type=F32)


def dot_nt(a, b):
    return lax.dot_general(a, b, NT, preferred_element_type=F32)


def dot_tn(a, b):
    return lax.dot_general(a, b, TN, preferred_element_type=F32)


def shape(dims, dtype):
    return jax.ShapeDtypeStruct(dims, dtype)


def about(microseconds):
    return pl.CostEstimate(
        flops=int(microseconds * PER_MICROSECOND * Chain.weight), bytes_accessed=1, transcendentals=0
    )


def params(mib):
    return pltpu.CompilerParams(vmem_limit_bytes=mib * MIB)


def layer_norm(values):
    centered = values - jnp.mean(values, axis=-1, keepdims=True)
    variance = jnp.mean(centered * centered, axis=-1, keepdims=True)
    inverse = lax.rsqrt(variance + EPSILON)
    return (centered * inverse, inverse)


def norm_back(gradient, normed, inverse):
    return inverse * (
        gradient
        - jnp.mean(gradient, axis=-1, keepdims=True)
        - normed * jnp.mean(gradient * normed, axis=-1, keepdims=True)
    )


def rope_tables():
    frequency = np.exp(
        np.arange(HEAD // 2, dtype=np.float32) * np.float32(-2.0 * math.log(10000.0) / HEAD)
    ).astype(np.float32)
    angle = np.arange(CHAIN * BLOCK, dtype=np.float32)[:, None] * frequency[None, :]
    cosine, sine = np.cos(angle), np.sin(angle)
    return (
        np.concatenate([cosine, cosine], axis=1).astype(np.float32),
        np.concatenate([-sine, sine], axis=1).astype(np.float32),
    )


def depth_of(parent_ref, slot):
    def up(_, carry):
        at, depth = carry
        parent = jnp.where(at >= 0, parent_ref[jnp.maximum(at, 0)], -1)
        return parent, depth + jnp.where(parent >= 0, 1, 0).astype(jnp.int32)

    return lax.fori_loop(0, CHAIN - 1, up, (slot, jnp.int32(0)))[1]


def xor_pairs(count, mask):
    return [(index, index ^ mask) for index in range(count)]


class Plan:
    def __init__(self, mesh, rows, width, heads, ff):
        self.dp = mesh.shape["dp"]
        self.tensor = mesh.shape["tensor"]
        self.rows, self.width, self.heads, self.ff = rows, width, heads, ff
        self.slots = rows // BLOCK
        self.spread = heads
        self.rest = self.dp // heads
        self.bits = self.dp.bit_length() - 1
        self.piece = width // self.dp
        self.own = rows // self.tensor
        self.groups = 2 if self.own % 32 == 0 else 1
        self.part = rows // self.groups
        self.share = self.own // self.groups

    def own_rows(self, group):
        return pl.BlockSpec(
            (self.share, self.width), lambda i, place: (group * self.tensor + place[1], 0)
        )

    def own_part(self):
        return pl.BlockSpec((self.share, self.width), lambda i, place: (place[1], 0))


def fetch(weights, held, sems, kind):
    copies = [
        pltpu.make_async_copy(w, held.at[index], sems.at[index]) for index, w in enumerate(weights)
    ]

    @pl.when(kind == 0)
    def _():
        for copy in copies:
            copy.start()

    def wait():
        for index, copy in enumerate(copies):

            @pl.when(kind == index)
            def _():
                copy.wait()

    return wait


def qkv_kernel(plan, parent, place, x, wq, wk, wv, cosine, sine, normed, *rest):
    outs, stage = rest[: plan.spread], rest[-1]
    me = place[0]
    part = me // plan.rest
    depth = depth_of(parent, me * plan.slots + pl.program_id(0))
    rows = pl.ds(pl.multiple_of(depth * BLOCK, BLOCK), BLOCK)
    cos, sin = cosine[rows, :], sine[rows, :]
    low = layer_norm(x[...].astype(F32))[0].astype(LOW)
    normed[...] = low
    for kind, w in enumerate((wq, wk, wv)):
        y = dot(low, w[...])
        for head in range(plan.heads):
            yh = y[:, head * HEAD : (head + 1) * HEAD]
            if kind < 2:
                yh = yh * cos + pltpu.roll(yh, HEAD // 2, 1) * sin
            stage[head, kind] = yh.astype(LOW)
    for d in range(plan.spread):
        outs[d][...] = stage[part ^ d]


def kept_order(plan):
    return [
        sum(((at >> bit) & 1) << (plan.bits - 1 - bit) for bit in range(plan.bits - 1))
        for at in range(plan.dp // 2)
    ]


def project_qkv(plan, slot_parent, place, tokens, wq, wk, wv, cosine, sine):
    whole = lambda i, *_: (0, 0)
    once = pl.Buffered(buffer_count=1)
    wide = plan.heads * HEAD
    return pl.pallas_call(
        functools.partial(qkv_kernel, plan),
        grid_spec=pltpu.PrefetchScalarGridSpec(
            num_scalar_prefetch=2,
            grid=(plan.slots,),
            in_specs=[pl.BlockSpec((BLOCK, plan.width), lambda i, *_: (i, 0))]
            + [pl.BlockSpec((plan.width, wide), whole, pipeline_mode=once)] * 3
            + [pl.BlockSpec((CHAIN * BLOCK, HEAD), whole, pipeline_mode=once)] * 2,
            out_specs=[pl.BlockSpec((BLOCK, plan.width), lambda i, *_: (i, 0))]
            + [pl.BlockSpec((3, BLOCK, HEAD), lambda i, *_: (0, i, 0))] * plan.spread,
            scratch_shapes=[
                pltpu.VMEM((plan.heads, 3, BLOCK, HEAD), LOW),
            ],
        ),
        out_shape=[shape((plan.rows, plan.width), LOW)]
        + [shape((3, plan.rows, HEAD), LOW)] * plan.spread,
        compiler_params=params(60),
        cost_estimate=about(0),
        name="project_qkv",
    )(slot_parent, place, tokens, wq, wk, wv, cosine, sine)


def gather_chain(plan, parent, me, slot, kv, keys, values):
    count = jnp.int32(0)
    at = slot
    places = []
    for step in range(CHAIN):
        here = jnp.maximum(at, 0)
        relative = (here // plan.slots) ^ me
        block = (
            (relative % plan.rest) * plan.spread + relative // plan.rest
        ) * 2 * plan.slots + here % plan.slots
        keys[step * BLOCK : (step + 1) * BLOCK, :] = kv[block]
        values[step * BLOCK : (step + 1) * BLOCK, :] = kv[block + plan.slots]
        places.append(block)
        valid = at >= 0
        count = count + jnp.where(valid, 1, 0).astype(jnp.int32)
        at = jnp.where(valid, parent[here], -1)
    return count, places


def chain_weights(queries, keys, counts):
    scores = [dot_nt(k, q) * SCALE for q, k in zip(queries, keys)]
    key_at = lax.broadcasted_iota(jnp.int32, scores[0].shape, 0)
    query_at = lax.broadcasted_iota(jnp.int32, scores[0].shape, 1)
    own = (key_at >= BLOCK) | (key_at <= query_at)
    probs = []
    for score, count in zip(scores, counts):
        score = jnp.where(own & (key_at < count * BLOCK), score, NEGATIVE)
        raised = jnp.exp(score - jnp.max(score, axis=0, keepdims=True))
        probs.append(raised * (1.0 / jnp.sum(raised, axis=0, keepdims=True)))
    return probs


def attend_kernel(plan, parent, place, *refs):
    n = plan.spread
    q_refs, kv, o_refs, keys, values = refs[:n], refs[n], refs[n + 1 : 2 * n + 1], refs[-2], refs[-1]
    me = place[0]

    def one(i, carry):
        rows = pl.ds(pl.multiple_of(i * BLOCK, BLOCK), BLOCK)
        slots = [(me ^ (d * plan.rest)) * plan.slots + i for d in range(n)]
        counts = [
            gather_chain(plan, parent, me, slots[d], kv, keys.at[d], values.at[d])[0]
            for d in range(n)
        ]
        queries = [q_refs[d][0, rows, :] for d in range(n)]
        probs = chain_weights(queries, [keys[d] for d in range(n)], counts)
        for d in range(n):
            o_refs[d][rows, :] = dot_tn(probs[d].astype(LOW), values[d]).astype(LOW)
        return carry

    lax.fori_loop(0, plan.slots, one, 0)


def attend(plan, slot_parent, place, parts, kv):
    n = plan.spread
    blocks = plan.dp * 2 * plan.slots
    return pl.pallas_call(
        functools.partial(attend_kernel, plan),
        grid_spec=pltpu.PrefetchScalarGridSpec(
            num_scalar_prefetch=2,
            grid=(1,),
            in_specs=[pl.BlockSpec((1, plan.rows, HEAD), lambda i, *_: (0, 0, 0))] * n
            + [pl.BlockSpec((blocks, BLOCK, HEAD), lambda i, *_: (0, 0, 0))],
            out_specs=[pl.BlockSpec((plan.rows, HEAD), lambda i, *_: (0, 0))] * n,
            scratch_shapes=[pltpu.VMEM((n, CHAIN * BLOCK, HEAD), LOW)] * 2,
        ),
        out_shape=[shape((plan.rows, HEAD), LOW)] * n,
        compiler_params=params(60),
        cost_estimate=about(0),
        name="attend",
    )(slot_parent, place, *parts, kv)


def attend_back_kernel(plan, parent, place, *refs):
    n = plan.spread
    q_refs, kv, g_refs = refs[:n], refs[n], refs[n + 1 : 2 * n + 1]
    dq_refs = refs[2 * n + 1 : 3 * n + 1]
    near, far, keys, values, total = refs[3 * n + 1 :]
    me = place[0]
    total[...] = jnp.zeros_like(total)

    def one(i, carry):
        rows = pl.ds(pl.multiple_of(i * BLOCK, BLOCK), BLOCK)
        slots = [(me ^ (d * plan.rest)) * plan.slots + i for d in range(n)]
        chains = [
            gather_chain(plan, parent, me, slots[d], kv, keys.at[d], values.at[d])
            for d in range(n)
        ]
        queries = [q_refs[d][0, rows, :] for d in range(n)]
        grads = [g_refs[d][rows, :] for d in range(n)]
        probs = chain_weights(queries, [keys[d] for d in range(n)], [chain[0] for chain in chains])
        for d in range(n):
            grad_prob = dot_nt(values[d], grads[d])
            inner = jnp.sum(grad_prob * probs[d], axis=0, keepdims=True)
            grad_scores = (probs[d] * (grad_prob - inner)).astype(LOW)
            dv = dot(probs[d].astype(LOW), grads[d])
            dk = dot(grad_scores, queries[d]) * SCALE
            dq_refs[d][rows, :] = (dot_tn(grad_scores, keys[d]) * SCALE).astype(LOW)
            for step, block in enumerate(chains[d][1]):
                span = slice(step * BLOCK, (step + 1) * BLOCK)
                total[block] = total[block] + dk[span]
                total[block + plan.slots] = total[block + plan.slots] + dv[span]
        return carry

    lax.fori_loop(0, plan.slots, one, 0)
    half = near.shape[0]
    near[...] = total[:half]
    far[...] = total[half:].astype(LOW)


def attend_back(plan, slot_parent, place, parts, kv, grads):
    n = plan.spread
    blocks = plan.dp * 2 * plan.slots
    near = n * 2 * plan.slots
    return pl.pallas_call(
        functools.partial(attend_back_kernel, plan),
        grid_spec=pltpu.PrefetchScalarGridSpec(
            num_scalar_prefetch=2,
            grid=(1,),
            in_specs=[pl.BlockSpec((1, plan.rows, HEAD), lambda i, *_: (0, 0, 0))] * n
            + [pl.BlockSpec((blocks, BLOCK, HEAD), lambda i, *_: (0, 0, 0))]
            + [pl.BlockSpec((plan.rows, HEAD), lambda i, *_: (0, 0))] * n,
            out_specs=[pl.BlockSpec((plan.rows, HEAD), lambda i, *_: (0, 0))] * n
            + [
                pl.BlockSpec((near, BLOCK, HEAD), lambda i, *_: (0, 0, 0)),
                pl.BlockSpec((blocks - near, BLOCK, HEAD), lambda i, *_: (0, 0, 0)),
            ],
            scratch_shapes=[pltpu.VMEM((n, CHAIN * BLOCK, HEAD), LOW)] * 2
            + [pltpu.VMEM((blocks, BLOCK, HEAD), F32)],
        ),
        out_shape=[shape((plan.rows, HEAD), LOW)] * n
        + [shape((near, BLOCK, HEAD), F32), shape((blocks - near, BLOCK, HEAD), LOW)],
        compiler_params=params(60),
        cost_estimate=about(23),
        name="attend_back",
    )(slot_parent, place, *parts, kv, *grads)


def combine_kernel(plan, *refs):
    n = plan.spread
    queries, (near, got), outs = refs[:n], refs[n : n + 2], refs[n + 2 :]
    for d in range(n):
        outs[d][0] = queries[d][...]
        for kind in range(2):
            for slot in range(plan.slots):
                block = (d * 2 + kind) * plan.slots + slot
                rows = slice(slot * BLOCK, (slot + 1) * BLOCK)
                total = near[block] + got[block].astype(F32)
                outs[d][kind + 1, rows, :] = total.astype(LOW)


def combine_back(plan, queries, near, got):
    n = plan.spread
    return pl.pallas_call(
        functools.partial(combine_kernel, plan),
        out_shape=[shape((3, plan.rows, HEAD), LOW)] * n,
        compiler_params=params(60),
        cost_estimate=about(3),
        name="combine_back",
    )(*queries, near, got)


def heads_kernel(plan, place, *refs):
    part = place[0] // plan.rest
    outs = refs[plan.spread :]
    for d in range(plan.spread):
        head = pl.ds(pl.multiple_of((part ^ d) * HEAD, HEAD), HEAD)
        for group, out in enumerate(outs):
            out[:, head] = refs[d][group * plan.part : (group + 1) * plan.part, :]


def gather_heads(plan, place, parts):
    wide = plan.heads * HEAD
    return pl.pallas_call(
        functools.partial(heads_kernel, plan),
        grid_spec=pltpu.PrefetchScalarGridSpec(
            num_scalar_prefetch=1,
            grid=(1,),
            in_specs=[pl.BlockSpec((plan.rows, HEAD), lambda i, *_: (0, 0))] * plan.spread,
            out_specs=[pl.BlockSpec((plan.part, wide), lambda i, *_: (0, 0))] * plan.groups,
        ),
        out_shape=[shape((plan.part, wide), LOW)] * plan.groups,
        compiler_params=params(60),
        cost_estimate=about(0),
        name="gather_heads",
    )(place, *parts)


def scatter_kernel(plan, place, *refs):
    part, z = place[0] // plan.rest, place[1]
    sources, outs = refs[: plan.tensor], refs[plan.tensor :]
    for shift in range(plan.tensor):
        origin = lax.rem(z - shift + plan.tensor, plan.tensor)
        for group in range(plan.groups):
            start = group * plan.part + origin * plan.share
            rows = pl.ds(pl.multiple_of(start, 16), plan.share)
            share = slice(group * plan.share, (group + 1) * plan.share)
            for d in range(plan.spread):
                head = pl.ds(pl.multiple_of((part ^ d) * HEAD, HEAD), HEAD)
                outs[d][rows, :] = sources[shift][share, head]


def scatter_heads(plan, place, sources):
    return pl.pallas_call(
        functools.partial(scatter_kernel, plan),
        grid_spec=pltpu.PrefetchScalarGridSpec(
            num_scalar_prefetch=1,
            grid=(1,),
            in_specs=[pl.BlockSpec((plan.own, plan.heads * HEAD), lambda i, *_: (0, 0))]
            * plan.tensor,
            out_specs=[pl.BlockSpec((plan.rows, HEAD), lambda i, *_: (0, 0))] * plan.spread,
        ),
        out_shape=[shape((plan.rows, HEAD), LOW)] * plan.spread,
        name="scatter_heads",
    )(place, *sources)


def turn_back_kernel(plan, parent, place, cosine, sine, wq, wk, wv, *refs):
    parts, (back, out, product) = refs[: plan.spread], refs[plan.spread :]
    me = place[0]
    part = me // plan.rest
    wide = plan.heads * HEAD

    @pl.when(pl.program_id(0) == 0)
    def _():
        for slot in range(plan.slots):
            depth = depth_of(parent, me * plan.slots + slot)
            table = pl.ds(pl.multiple_of(depth * BLOCK, BLOCK), BLOCK)
            cos, sin = cosine[table, :], sine[table, :]
            rows = slice(slot * BLOCK, (slot + 1) * BLOCK)
            for d in range(plan.spread):
                for kind in range(3):
                    value = parts[d][kind, rows, :]
                    if kind < 2:
                        value = value.astype(F32)
                        value = value * cos - pltpu.roll(value, HEAD // 2, 1) * sin
                    at = pl.multiple_of((kind * plan.heads + (part ^ d)) * HEAD, HEAD)
                    out[rows, pl.ds(at, HEAD)] = value.astype(LOW)

    total = 0.0
    for kind, w in enumerate((wq, wk, wv)):
        total = total + dot_nt(out[:, kind * wide : (kind + 1) * wide], w[...])
    product[...] = total
    for device in range(plan.tensor):
        for group in range(plan.groups):
            source = (group * plan.tensor + device) * plan.share
            target = (device * plan.groups + group) * plan.share
            back[target : target + plan.share, :] = product[
                source : source + plan.share, :
            ].astype(LOW)


def turn_back(plan, slot_parent, place, cosine, sine, weights, parts):
    whole = lambda i, *_: (0, 0)
    wide = plan.heads * HEAD
    tile = min(512, plan.width)
    return pl.pallas_call(
        functools.partial(turn_back_kernel, plan),
        grid_spec=pltpu.PrefetchScalarGridSpec(
            num_scalar_prefetch=2,
            grid=(plan.width // tile,),
            in_specs=[pl.BlockSpec((CHAIN * BLOCK, HEAD), whole)] * 2
            + [pl.BlockSpec((tile, wide), lambda i, *_: (i, 0))] * 3
            + [pl.BlockSpec((3, plan.rows, HEAD), lambda i, *_: (0, 0, 0))] * plan.spread,
            out_specs=[
                pl.BlockSpec((plan.rows, tile), lambda i, *_: (0, i)),
                pl.BlockSpec((plan.rows, 3 * wide), whole),
            ],
            scratch_shapes=[pltpu.VMEM((plan.rows, tile), F32)],
        ),
        out_shape=[shape((plan.rows, plan.width), LOW), shape((plan.rows, 3 * wide), LOW)],
        compiler_params=params(60),
        cost_estimate=about(13),
        name="turn_back",
    )(slot_parent, place, cosine, sine, *weights, *parts)


def out_kernel(plan, place, x, att, near, far, middle, normed):
    half = plan.heads * HEAD // 2
    core = place[0] % 2
    total = x[...].astype(F32)
    for z in range(plan.tensor):
        for side, w in ((core, near), (1 - core, far)):
            columns = pl.ds(pl.multiple_of(side * half, half), half)
            total = total + dot(att[z, :, columns], w[z])
    middle[...] = total
    normed[...] = layer_norm(total)[0].astype(LOW)


def project_out(plan, place, group, tokens, att, near, far):
    half = plan.heads * HEAD // 2
    count = 2
    rows = plan.part // count
    weights = pl.BlockSpec(
        (plan.tensor, half, plan.width),
        lambda i, *_: (0, 0, 0),
        pipeline_mode=pl.Buffered(buffer_count=1),
    )
    out = pl.BlockSpec((rows, plan.width), lambda i, *_: (i, 0))
    return pl.pallas_call(
        functools.partial(out_kernel, plan),
        grid_spec=pltpu.PrefetchScalarGridSpec(
            num_scalar_prefetch=1,
            grid=(count,),
            in_specs=[
                pl.BlockSpec((rows, plan.width), lambda i, *_: (group * count + i, 0)),
                pl.BlockSpec((plan.tensor, rows, 2 * half), lambda i, *_: (0, i, 0)),
                weights,
                weights,
            ],
            out_specs=[out, out],
        ),
        out_shape=[shape((plan.part, plan.width), F32), shape((plan.part, plan.width), LOW)],
        compiler_params=params(60),
        cost_estimate=about(7),
        name="project_out",
    )(place, tokens, att, near, far)


def grad_hidden_kernel(cot, wd, out):
    out[...] = dot_nt(cot[...], wd[...])


def grad_hidden_of(cot, wd):
    rows, width = cot.shape
    ff = wd.shape[0]
    tile = min(512, ff)
    return pl.pallas_call(
        grad_hidden_kernel,
        grid=(ff // tile,),
        in_specs=[
            pl.BlockSpec((rows, width), lambda i: (0, 0)),
            pl.BlockSpec((tile, width), lambda i: (i, 0)),
        ],
        out_specs=pl.BlockSpec((rows, tile), lambda i: (0, i)),
        out_shape=shape((rows, ff), F32),
        compiler_params=params(60),
        cost_estimate=about(0),
        name="grad_hidden",
    )(cot, wd)


def ff_kernel(tile, normed, seed, wg, wu, back, hidden, grad_gate, grad_up, *scratch):
    gate_held, up_held, results, total, in_sems, out_sems = scratch
    count = wg.shape[1] // tile
    spans = [slice(index * tile, (index + 1) * tile) for index in range(count)]
    arrivals = [
        [
            pltpu.make_async_copy(w.at[:, span], held.at[:, span], in_sems.at[which, index])
            for which, (w, held) in enumerate(((wg, gate_held), (wu, up_held)))
        ]
        for index, span in enumerate(spans)
    ]
    departures = [
        [
            pltpu.make_async_copy(
                results.at[which, :, span], out.at[:, span], out_sems.at[which, index]
            )
            for which, out in enumerate((hidden, grad_gate, grad_up))
        ]
        for index, span in enumerate(spans)
    ]
    for pair in arrivals:
        for copy in pair:
            copy.start()
    for index, span in enumerate(spans):
        for copy in arrivals[index]:
            copy.wait()
        gate = dot(normed[...], gate_held[:, span])
        up = dot(normed[...], up_held[:, span])
        grad_hidden = seed[:, span]
        s = 1.0 / (1.0 + jnp.exp(-gate))
        active = gate * s
        gu = (grad_hidden * active).astype(LOW)
        gg = (grad_hidden * up * s * (1.0 + gate * (1.0 - s))).astype(LOW)
        results[0, :, span] = (active * up).astype(LOW)
        results[1, :, span] = gg
        results[2, :, span] = gu
        for copy in departures[index]:
            copy.start()
        part = dot_nt(gg, gate_held[:, span]) + dot_nt(gu, up_held[:, span])
        if index == 0:
            total[...] = part
        elif index < count - 1:
            total[...] += part
        else:
            back[...] = (total[...] + part).astype(LOW)
    for triple in departures:
        for copy in triple:
            copy.wait()


def feed_forward(plan, place, group, normed, seed, wg, wu):
    rows, width = normed.shape
    ff = wg.shape[1]
    tile = min(512, ff // 2)
    whole = pl.BlockSpec((rows, width), lambda i: (0, 0))
    anywhere = pl.BlockSpec(memory_space=pl.ANY)
    return pl.pallas_call(
        functools.partial(ff_kernel, tile),
        grid=(1,),
        in_specs=[whole, pl.BlockSpec((rows, ff), lambda i: (group, 0)), anywhere, anywhere],
        out_specs=[whole, anywhere, anywhere, anywhere],
        out_shape=[shape((rows, width), LOW)] + [shape((rows, ff), LOW)] * 3,
        scratch_shapes=[
            pltpu.VMEM((width, ff), LOW),
            pltpu.VMEM((width, ff), LOW),
            pltpu.VMEM((3, rows, ff), LOW),
            pltpu.VMEM((rows, width), F32),
            pltpu.SemaphoreType.DMA((2, ff // tile)),
            pltpu.SemaphoreType.DMA((3, ff // tile)),
        ],
        compiler_params=params(62),
        cost_estimate=about(17),
        name="feed_forward",
    )(normed, seed, wg, wu)


def down_kernel(plan, *refs):
    hiddens, (w, out) = refs[: plan.groups], refs[plan.groups :]
    for group, hidden in enumerate(hiddens):
        rows = slice(group * plan.part, (group + 1) * plan.part)
        out[rows, :] = dot(hidden[...], w[...]).astype(LOW)


def project_down(plan, hiddens, w):
    ff, width = w.shape
    tile = min(512, width)
    return pl.pallas_call(
        functools.partial(down_kernel, plan),
        grid=(width // tile,),
        in_specs=[pl.BlockSpec((plan.part, ff), lambda i: (0, 0))] * plan.groups
        + [pl.BlockSpec((ff, tile), lambda i: (0, i))],
        out_specs=pl.BlockSpec((plan.rows, tile), lambda i: (0, i)),
        out_shape=shape((plan.rows, width), LOW),
        compiler_params=params(60),
        cost_estimate=about(11),
        name="project_down",
    )(*hiddens, w)


def branch_back_kernel(plan, place, *refs):
    count = plan.groups
    parts, middles, cots = refs[:count], refs[count : 2 * count], refs[2 * count : 3 * count]
    near, far, grad_middle, low = refs[3 * count : 3 * count + 4]
    outs, (near_held, far_held, sems) = refs[3 * count + 4 : -3], refs[-3:]
    core, z = place[0] % 2, place[1]
    half = plan.heads * HEAD // 2
    sides = ((core, near, near_held), (1 - core, far, far_held))
    copies = [
        [
            pltpu.make_async_copy(
                w.at[lax.rem(z + shift, plan.tensor)], held.at[shift], sems.at[index, shift]
            )
            for index, (_, w, held) in enumerate(sides)
        ]
        for shift in range(plan.tensor)
    ]
    for pair in copies:
        for copy in pair:
            copy.start()
    for group in range(count):
        rows = slice(group * plan.share, (group + 1) * plan.share)
        normed, inverse = layer_norm(middles[group][...])
        back = norm_back(parts[group][...].astype(F32), normed, inverse)
        grad = cots[group][...].astype(F32) + back
        grad_middle[rows, :] = grad
        low[rows, :] = grad.astype(LOW)
    for shift in range(plan.tensor):
        for copy, (side, _, held) in zip(copies[shift], sides):
            copy.wait()
            columns = pl.ds(pl.multiple_of(side * half, half), half)
            outs[shift][:, columns] = dot_nt(low[...], held[shift]).astype(LOW)


def branch_back(plan, place, parts, middles, cot, near, far):
    half = plan.heads * HEAD // 2
    own = pl.BlockSpec((plan.own, plan.width), lambda i, *_: (0, 0))
    share = pl.BlockSpec((plan.share, plan.width), lambda i, *_: (0, 0))
    anywhere = pl.BlockSpec(memory_space=pl.ANY)
    return pl.pallas_call(
        functools.partial(branch_back_kernel, plan),
        grid_spec=pltpu.PrefetchScalarGridSpec(
            num_scalar_prefetch=1,
            grid=(1,),
            in_specs=[share] * plan.groups
            + [plan.own_part()] * plan.groups
            + [plan.own_rows(group) for group in range(plan.groups)]
            + [anywhere, anywhere],
            out_specs=[own, own]
            + [pl.BlockSpec((plan.own, 2 * half), lambda i, *_: (0, 0))] * plan.tensor,
            scratch_shapes=[pltpu.VMEM((plan.tensor, half, plan.width), LOW)] * 2
            + [pltpu.SemaphoreType.DMA((2, plan.tensor))],
        ),
        out_shape=[shape((plan.own, plan.width), F32), shape((plan.own, plan.width), LOW)]
        + [shape((plan.own, 2 * half), LOW)] * plan.tensor,
        compiler_params=params(60),
        cost_estimate=about(9),
        name="branch_back",
    )(place, *parts, *middles, *([cot] * plan.groups), near, far)


def tokens_back_kernel(plan, place, part, *refs):
    tokens, (grad_middle, out) = refs[: plan.groups], refs[plan.groups :]
    for group in range(plan.groups):
        rows = slice(group * plan.share, (group + 1) * plan.share)
        normed, inverse = layer_norm(tokens[group][...].astype(F32))
        back = norm_back(part[rows, :].astype(F32), normed, inverse)
        out[rows, :] = (grad_middle[rows, :] + back).astype(LOW)


def tokens_back(plan, place, part, tokens, grad_middle):
    own = pl.BlockSpec((plan.own, plan.width), lambda i, *_: (0, 0))
    return pl.pallas_call(
        functools.partial(tokens_back_kernel, plan),
        grid_spec=pltpu.PrefetchScalarGridSpec(
            num_scalar_prefetch=1,
            grid=(1,),
            in_specs=[own] + [plan.own_rows(group) for group in range(plan.groups)] + [own],
            out_specs=own,
        ),
        out_shape=shape((plan.own, plan.width), LOW),
        compiler_params=params(60),
        cost_estimate=about(4),
        name="tokens_back",
    )(place, part, *([tokens] * plan.groups), grad_middle)


def products(lhs, rhs):
    total, start = 0.0, 0
    for index, right in enumerate(rhs):
        rows = right.shape[0]
        left = lhs[index][...] if len(lhs) > 1 else lhs[0][start : start + rows, :]
        total = total + dot_tn(left, right[...])
        start += rows
    return total


def away_kernel(count, place, *refs):
    lhs, rhs, out = refs[:count], refs[count:-1], refs[-1]
    out[...] = products(lhs, rhs).astype(LOW)


def wgrad_away(plan, place, lhs, rhs):
    columns = rhs[0].shape[1]
    piece, count = plan.piece, plan.dp // 2
    return pl.pallas_call(
        functools.partial(away_kernel, len(lhs)),
        grid_spec=pltpu.PrefetchScalarGridSpec(
            num_scalar_prefetch=1,
            grid=(count,),
            in_specs=[
                pl.BlockSpec((part.shape[0], piece), lambda i, place: (0, place[2 + i] ^ 1))
                for part in lhs
            ]
            + [pl.BlockSpec(part.shape, lambda i, *_: (0, 0)) for part in rhs],
            out_specs=pl.BlockSpec((piece, columns), lambda i, *_: (i, 0)),
        ),
        out_shape=shape((count * piece, columns), LOW),
        compiler_params=params(60),
        cost_estimate=about(8),
        name="wgrad_away",
    )(place, *lhs, *rhs)


def keep_kernel(arrays, count, place, *refs):
    lhs, rhs = refs[:arrays], refs[arrays:-5]
    recv, a_keep, a_send, b_keep, b_send = refs[-5:]
    step = pl.program_id(0)
    total = (products(lhs, rhs) + recv[...].astype(F32)).astype(LOW)
    half = total.shape[1] // 2

    @pl.when(step < count // 2)
    def _():
        a_keep[...] = total[:, :half]

    @pl.when(step >= count // 2)
    def _():
        a_send[...] = total[:, :half]

    @pl.when(step % 2 == 0)
    def _():
        b_keep[...] = total[:, half:]

    @pl.when(step % 2 == 1)
    def _():
        b_send[...] = total[:, half:]


def wgrad_keep(plan, place, lhs, rhs, recv):
    columns = rhs[0].shape[1]
    piece, count = plan.piece, plan.dp // 2
    half = count // 2
    block = lambda index: pl.BlockSpec((piece, columns // 2), index)
    return pl.pallas_call(
        functools.partial(keep_kernel, len(lhs), count),
        grid_spec=pltpu.PrefetchScalarGridSpec(
            num_scalar_prefetch=1,
            grid=(count,),
            in_specs=[
                pl.BlockSpec((part.shape[0], piece), lambda i, place: (0, place[2 + i]))
                for part in lhs
            ]
            + [pl.BlockSpec(part.shape, lambda i, *_: (0, 0)) for part in rhs]
            + [pl.BlockSpec((piece, columns), lambda i, *_: (i, 0))],
            out_specs=[
                block(lambda i, *_: (jnp.minimum(i, half - 1), 0)),
                block(lambda i, *_: (jnp.maximum(i - half, 0), 0)),
                block(lambda i, *_: (i // 2, 0)),
                block(lambda i, *_: (i // 2, 0)),
            ],
        ),
        out_shape=[shape((half * piece, columns // 2), LOW)] * 4,
        compiler_params=params(60),
        cost_estimate=about(9),
        name="wgrad_keep",
    )(place, *lhs, *rhs, recv)


def stage_kernel(piece, a, a_got, b, b_got, a_keep, a_send, b_keep, b_send):
    total = a[...].astype(F32) + a_got[...].astype(F32)
    half = total.shape[0] // 2
    a_keep[...] = total[:half].astype(LOW)
    a_send[...] = total[half:].astype(LOW)
    for at in range(0, 2 * half, 2 * piece):
        for start, out in ((at, b_keep), (at + piece, b_send)):
            rows = slice(start, start + piece)
            total = b[rows, :].astype(F32) + b_got[rows, :].astype(F32)
            out[at // 2 : at // 2 + piece, :] = total.astype(LOW)


def wgrad_stage(piece, *arrays):
    rows, columns = arrays[0].shape
    tile = columns // 2 if columns % 256 == 0 else columns
    block = lambda size: pl.BlockSpec((size, tile), lambda i: (0, i))
    return pl.pallas_call(
        functools.partial(stage_kernel, piece),
        grid=(columns // tile,),
        in_specs=[block(rows)] * 4,
        out_specs=[block(rows // 2)] * 4,
        out_shape=[shape((rows // 2, columns), LOW)] * 4,
        compiler_params=params(60),
        cost_estimate=about(3),
        name="wgrad_stage",
    )(*arrays)


def finish_kernel(turned, a, a_got, b, b_got, out):
    half = a.shape[1]
    for way, (keep, got) in enumerate(((a, a_got), (b, b_got))):
        total = keep[...].astype(F32) + got[...].astype(F32)
        span = slice(way * half, (way + 1) * half)
        if turned:
            out[span, :] = total.T
        else:
            out[:, span] = total


def wgrad_finish(turned, *arrays):
    piece, half = arrays[0].shape
    return pl.pallas_call(
        functools.partial(finish_kernel, turned),
        out_shape=shape((2 * half, piece) if turned else (piece, 2 * half), F32),
        compiler_params=params(60),
        cost_estimate=about(3),
        name="wgrad_finish",
    )(*arrays)


def split_kernel(*refs):
    arrays, outs, held = refs[:4], refs[4:-1], refs[-1]
    finish_kernel(False, *arrays, held)
    width = outs[0].shape[1]
    for index, out in enumerate(outs):
        out[...] = held[:, index * width : (index + 1) * width]


def wgrad_finish_split(*arrays):
    piece, half = arrays[0].shape
    return pl.pallas_call(
        split_kernel,
        out_shape=[shape((piece, 2 * half // 3), F32)] * 3,
        scratch_shapes=[pltpu.VMEM((piece, 2 * half), F32)],
        compiler_params=params(60),
        cost_estimate=about(3),
        name="wgrad_finish_split",
    )(*arrays)


def chunks_kernel(plan, place, *refs):
    arrays, chunks, held = refs[:4], refs[4:-1], refs[-1]
    finish_kernel(True, *arrays, held)
    rows = plan.heads * HEAD
    for index, chunk in enumerate(chunks):
        chunk[...] = held[ring_rows(plan, place, index, rows), :].astype(LOW)


def wgrad_finish_chunks(plan, place, *arrays):
    piece, half = arrays[0].shape
    rows = plan.heads * HEAD
    return pl.pallas_call(
        functools.partial(chunks_kernel, plan),
        grid_spec=pltpu.PrefetchScalarGridSpec(
            num_scalar_prefetch=1,
            grid=(1,),
            in_specs=[pl.BlockSpec((piece, half), lambda i, *_: (0, 0))] * 4,
            out_specs=[pl.BlockSpec((rows, piece), lambda i, *_: (0, 0))] * plan.tensor,
            scratch_shapes=[pltpu.VMEM((2 * half, piece), F32)],
        ),
        out_shape=[shape((rows, piece), LOW)] * plan.tensor,
        compiler_params=params(60),
        cost_estimate=about(4),
        name="wgrad_finish_chunks",
    )(place, *arrays)


def tie(values, *others):
    many = isinstance(values, (list, tuple))
    held = lax.optimization_barrier((tuple(values) if many else (values,)) + others)
    return list(held[: len(values)]) if many else held[0]


class WeightGradient:
    def __init__(self, plan, place, chain, lhs, rhs, turned=False, chunks=False, split=False):
        self.chunks, self.split = chunks, split
        self.plan, self.place, self.chain = plan, place, chain
        self.lhs, self.rhs, self.turned = lhs, rhs, turned
        self.stage = 0

    def swap(self, array, bit):
        return lax.ppermute(array, "dp", xor_pairs(self.plan.dp, 1 << bit))

    def away(self):
        sent = self.chain.run(
            lambda *r: wgrad_away(self.plan, self.place, self.lhs, r), *self.rhs
        )
        self.recv = self.swap(sent, 0)

    def keep(self):
        self.a_keep, self.a_send, self.b_keep, self.b_send = self.chain.run(
            lambda r: wgrad_keep(self.plan, self.place, self.lhs, self.rhs, r), self.recv
        )

    def send(self):
        upwards = list(range(1, self.plan.bits))
        a, b = self.chain.after(self.a_send, self.b_send)
        self.a_got = self.swap(a, upwards[self.stage])
        self.b_got = self.swap(b, upwards[-1 - self.stage])
        self.stage += 1

    def wait(self):
        self.a_got, self.b_got = self.chain.wait(self.a_got, self.b_got)

    def took(self):
        self.recv = self.chain.wait(self.recv)

    def add(self):
        self.a_keep, self.a_send, self.b_keep, self.b_send = self.chain.run(
            lambda *p: wgrad_stage(self.plan.piece, *p),
            self.a_keep,
            self.a_got,
            self.b_keep,
            self.b_got,
        )

    def finish(self):
        while self.stage < self.plan.bits - 1:
            self.add()
            self.send()
        return self.chain.run(
            lambda *p: (
                wgrad_finish_chunks(self.plan, self.place, *p)
                if self.chunks
                else wgrad_finish_split(*p)
                if self.split
                else wgrad_finish(self.turned, *p)
            ),
            self.a_keep,
            self.a_got,
            self.b_keep,
            self.b_got,
        )


class Chain:
    weight = 1.0

    def __init__(self, last):
        self.last = last

    def after(self, *values):
        held = lax.optimization_barrier(values + (self.last,))
        return held[0] if len(values) == 1 else list(held[:-1])

    def wait(self, *values):
        held = lax.optimization_barrier(values + (self.last,))
        self.last = held[0]
        return held[0] if len(values) == 1 else list(held[:-1])

    def run(self, step, *values):
        held = self.after(*values)
        out = step(*held) if len(values) > 1 else step(held)
        self.last = out[0] if isinstance(out, (list, tuple)) else out
        return out


def shifted(plan, array, shift):
    pairs = [(i, (i + shift) % plan.tensor) for i in range(plan.tensor)]
    return lax.ppermute(array, "tensor", pairs)


class RingSum:
    def __init__(self, plan, chain, chunks):
        self.plan, self.chain, self.chunks, self.at = plan, chain, chunks, 1
        self.moving = shifted(plan, chunks[0], 1)

    def step(self):
        if self.at < self.plan.tensor - 1:
            got, mine = self.chain.wait(self.moving, self.chunks[self.at])
            total = (got.astype(F32) + mine.astype(F32)).astype(LOW)
            self.chain.last = total
            self.moving = shifted(self.plan, total, 1)
            self.at += 1

    def finish(self):
        while self.at < self.plan.tensor - 1:
            self.step()
        return self.moving, self.chunks[-1]


def ring_rows(plan, place, step, rows):
    chunk = lax.rem(place[1] + (2 * plan.tensor - 1 - step), plan.tensor)
    return pl.ds(pl.multiple_of(chunk * rows, 16), rows)


def add_last_kernel(a, b, out):
    out[...] = a[...].astype(F32) + b[...].astype(F32)


def add_last(a, b):
    return pl.pallas_call(
        add_last_kernel,
        out_shape=shape(a.shape, F32),
        compiler_params=params(60),
        cost_estimate=about(2),
        name="add_last",
    )(a, b)


def add_kernel(plan, *refs):
    middles, (part, out) = refs[: plan.groups], refs[plan.groups :]
    step = pl.program_id(0)
    for group, middle in enumerate(middles):

        @pl.when(step // 2 == group)
        def _():
            out[...] = (middle[...] + part[...].astype(F32)).astype(LOW)


def add_residual(plan, middles, part):
    rows = plan.part // 2
    block = pl.BlockSpec((rows, plan.width), lambda i: (i, 0))
    return pl.pallas_call(
        functools.partial(add_kernel, plan),
        grid=(2 * plan.groups,),
        in_specs=[
            pl.BlockSpec(
                (rows, plan.width),
                lambda i, group=group: (jnp.clip(i - 2 * group, 0, 1), 0),
            )
            for group in range(plan.groups)
        ]
        + [block],
        out_specs=block,
        out_shape=shape((plan.rows, plan.width), LOW),
        compiler_params=params(60),
        cost_estimate=about(6),
        name="add_residual",
    )(*middles, part)


class State:
    pass


def body(mesh, tokens, w_query, w_key, w_value, w_out, w_gate, w_up, w_down, cotangent, slot_parent):
    plan = Plan(mesh, tokens.shape[0], tokens.shape[1], w_query.shape[1] // HEAD, w_gate.shape[1])
    me = lax.axis_index("dp")
    z = lax.axis_index("tensor")
    place = jnp.stack([me, z] + [me ^ relative for relative in kept_order(plan)]).astype(jnp.int32)
    cosine, sine = (jnp.asarray(table) for table in rope_tables())
    n = plan.spread
    wide = n * HEAD

    def swap(array, mask):
        return lax.ppermute(array, "dp", xor_pairs(plan.dp, mask))

    def exchange(parts):
        return [parts[0]] + [swap(parts[d], d * plan.rest) for d in range(1, n)]

    half = w_out.shape[0] // 2
    mine = lax.dynamic_slice_in_dim(w_out, (me % 2) * half, half, 0)
    near = lax.all_gather(mine, "tensor", axis=0, tiled=False)

    normed_one, *sends = project_qkv(
        plan, slot_parent, place, tokens, w_query, w_key, w_value, cosine, sine
    )
    chain = Chain(normed_one)
    parts = exchange(sends)
    seed = chain.run(lambda cot: grad_hidden_of(cot, w_down), cotangent)
    parts = chain.wait(*parts)
    kv = jnp.stack([part[1:] for part in parts])[None]
    mask = 1
    while mask < plan.rest:
        kv = jnp.concatenate([kv, swap(kv, mask)], axis=0)
        mask *= 2
    kv = chain.wait(kv.reshape(plan.dp * 2 * plan.slots, BLOCK, HEAD))
    attended_parts = exchange(chain.run(lambda *p: attend(plan, slot_parent, place, p, kv), *parts))
    attended = chain.run(lambda *p: gather_heads(plan, place, p), *attended_parts)
    everyone = [
        lax.all_gather(tie(part, near), "tensor", axis=0, tiled=False) for part in attended
    ]
    near = chain.after(near)
    far = swap(near, 1)

    middles, normed_two, hidden, grad_gate_proj, grad_up_proj, grad_normed_two = ([] for _ in range(6))
    for group in range(plan.groups):
        middle, normed = chain.run(
            lambda e, f: project_out(plan, place, group, tokens, e, near, f), everyone[group], far
        )
        partial_two, *rest = chain.run(
            lambda v: feed_forward(plan, place, group, v, seed, w_gate, w_up), normed
        )
        grad_normed_two.append(
            lax.psum_scatter(partial_two, "tensor", scatter_dimension=0, tiled=True)
        )
        middles.append(middle)
        normed_two.append(normed)
        for held, value in zip((hidden, grad_gate_proj, grad_up_proj), rest):
            held.append(value)
    state = State()
    down = WeightGradient(plan, place, chain, [cotangent], hidden, turned=True)
    gate = WeightGradient(plan, place, chain, normed_two, grad_gate_proj)
    up = WeightGradient(plan, place, chain, normed_two, grad_up_proj)
    out = WeightGradient(plan, place, chain, None, None, chunks=True)
    qkv = WeightGradient(plan, place, chain, None, None, split=True)

    def own():
        state.own = jnp.concatenate(
            [
                lax.dynamic_slice_in_dim(part, z * plan.share, plan.share, 1)
                .transpose(1, 0, 2)
                .reshape(plan.share, plan.width)
                for part in map(chain.after, everyone)
            ]
        )

    def branch():
        grad_middle, grad_branch, *chunks = chain.run(
            lambda *g: branch_back(plan, place, g, middles, cotangent, near, far),
            *grad_normed_two,
        )
        state.sources = [chunks[0]] + [
            shifted(plan, chunks[shift], shift) for shift in range(1, plan.tensor)
        ]
        state.grad_middle = grad_middle
        out.lhs, out.rhs = [grad_branch], [state.own]

    def output():
        branch_out = chain.run(lambda *h: project_down(plan, h, w_down), *hidden)
        state.part = lax.psum(branch_out, "tensor")

    def scatter():
        scattered = chain.run(lambda *p: scatter_heads(plan, place, p), *state.sources)
        state.grads = exchange(scattered)

    def heads():
        state.grads = chain.wait(*state.grads)

    def attend_step():
        *state.queries, state.near, state.far = chain.run(
            lambda *g: attend_back(plan, slot_parent, place, parts, kv, g), *state.grads
        )

    def sum_far():
        far_part = chain.after(state.far).reshape(plan.rest - 1, -1, BLOCK, HEAD)
        mask = plan.rest // 2
        while mask > 1:
            got = swap(far_part[mask - 1 : 2 * mask - 1], mask).astype(F32)
            state.near = state.near + got[0]
            far_part = (far_part[: mask - 1].astype(F32) + got[1:]).astype(LOW)
            mask //= 2
        state.got = swap(far_part.reshape(state.near.shape), 1)

    def sum_near():
        backs = chain.run(
            lambda g: combine_back(plan, state.queries, state.near, g), state.got
        )
        state.backs = exchange(backs)

    def arrive():
        state.backs = chain.wait(*state.backs)

    def turn():
        partial_one, turned = chain.run(
            lambda *p: turn_back(
                plan, slot_parent, place, cosine, sine, (w_query, w_key, w_value), p
            ),
            *state.backs,
        )
        state.one = lax.psum_scatter(partial_one, "tensor", scatter_dimension=0, tiled=True)
        qkv.lhs, qkv.rhs = [normed_one], [turned]

    def residual():
        state.output = chain.run(lambda p: add_residual(plan, middles, p), state.part)

    def tokens_step():
        grad_own = chain.run(
            lambda g: tokens_back(plan, place, g, tokens, state.grad_middle), state.one
        )
        state.tokens = lax.all_gather(grad_own, "tensor", axis=0, tiled=True)

    def gathered():
        state.tokens = chain.wait(state.tokens)

    def ring_start():
        state.ring = RingSum(plan, chain, chain.after(*state.out))

    def ring_end():
        got, mine = chain.wait(*state.ring.finish())
        state.out = chain.run(add_last, got, mine)

    def ring_step():
        state.ring.step()

    down.away()
    gate.away()
    down.took()
    down.keep()
    Chain.weight = 100.0
    down.send()
    Chain.weight = 1.0
    own()
    branch()
    down.wait()
    output()
    scatter()
    Chain.weight = 10.0
    out.away()
    Chain.weight = 1.0
    out.took()
    out.keep()
    heads()
    out.send()
    attend_step()
    Chain.weight = 0.001
    out.wait()
    Chain.weight = 1.0
    sum_far()
    Chain.weight = 0.3
    out.add()
    Chain.weight = 1.0
    sum_near()
    down.add()
    up.away()
    gate.keep()
    gate.send()
    arrive()
    turn()
    up.took()
    Chain.weight = 0.3
    out.send()
    Chain.weight = 1.0
    qkv.away()
    Chain.weight = 0.03
    up.keep()
    Chain.weight = 1.0
    up.send()
    Chain.weight = 100.0
    gate.wait()
    Chain.weight = 1.0
    state.out = out.finish()
    gate.add()
    qkv.took()
    qkv.keep()
    residual()
    ring_start()
    Chain.weight = 100.0
    down.send()
    Chain.weight = 1.0
    gate.send()
    up.wait()
    Chain.weight = 0.03
    tokens_step()
    Chain.weight = 1.0
    state.ring.step()
    qkv.send()
    down.wait()
    up.add()
    state.ring.step()
    gate.wait()
    state.down = down.finish()
    up.send()
    state.gate = gate.finish()
    qkv.wait()
    Chain.weight = 0.3
    qkv.add()
    Chain.weight = 1.0
    qkv.send()
    state.up = up.finish()
    ring_end()
    Chain.weight = 100.0
    state.qkv = qkv.finish()
    Chain.weight = 1.0
    grad_tokens = (
        state.tokens
        .reshape(plan.tensor, plan.groups, plan.share, plan.width)
        .transpose(1, 0, 2, 3)
        .reshape(plan.rows, plan.width)
    )
    return (
        state.output,
        grad_tokens,
        *state.qkv,
        state.out,
        state.gate,
        state.up,
        state.down,
    )


def solution(mesh):
    in_specs = (
        P("dp", None),
        P(None, "tensor"),
        P(None, "tensor"),
        P(None, "tensor"),
        P("tensor", None),
        P(None, "tensor"),
        P(None, "tensor"),
        P("tensor", None),
        P("dp", None),
        P(),
    )
    out_specs = (
        P("dp", None),
        P("dp", None),
        P("dp", "tensor"),
        P("dp", "tensor"),
        P("dp", "tensor"),
        P("tensor", "dp"),
        P("dp", "tensor"),
        P("dp", "tensor"),
        P("tensor", "dp"),
    )
    return jax.shard_map(
        functools.partial(body, mesh),
        mesh=mesh,
        in_specs=in_specs,
        out_specs=out_specs,
        check_vma=False,
    )
```

```python
import functools
import math

import jax
import jax.numpy as jnp
import numpy as np
from jax import lax
from jax.experimental import pallas as pl
from jax.experimental.pallas import tpu as pltpu
from jax.sharding import PartitionSpec as P

HEAD = 128
BLOCK = 128
TRUNK_BLOCKS = 8
CHAIN = TRUNK_BLOCKS + 2
EPSILON = 1e-05
NEGATIVE = -1e30
SCALE = HEAD ** (-0.5)
LOW = jnp.bfloat16
F32 = jnp.float32
MIB = 1024 * 1024
PER_MICROSECOND = 1.0e+11

NT = (((1,), (1,)), ((), ()))
TN = (((0,), (0,)), ((), ()))


def dot(a, b):
    return jnp.dot(a, b, preferred_element_type=F32)


def dot_nt(a, b):
    return lax.dot_general(a, b, NT, preferred_element_type=F32)


def dot_tn(a, b):
    return lax.dot_general(a, b, TN, preferred_element_type=F32)


def shape(dims, dtype):
    return jax.ShapeDtypeStruct(dims, dtype)


def about(microseconds):
    return pl.CostEstimate(
        flops=int(microseconds * PER_MICROSECOND * Chain.weight), bytes_accessed=1, transcendentals=0
    )


def params(mib):
    return pltpu.CompilerParams(vmem_limit_bytes=mib * MIB)


def layer_norm(values):
    centered = values - jnp.mean(values, axis=-1, keepdims=True)
    variance = jnp.mean(centered * centered, axis=-1, keepdims=True)
    inverse = lax.rsqrt(variance + EPSILON)
    return (centered * inverse, inverse)


def norm_back(gradient, normed, inverse):
    return inverse * (
        gradient
        - jnp.mean(gradient, axis=-1, keepdims=True)
        - normed * jnp.mean(gradient * normed, axis=-1, keepdims=True)
    )


def rope_tables():
    frequency = np.exp(
        np.arange(HEAD // 2, dtype=np.float32) * np.float32(-2.0 * math.log(10000.0) / HEAD)
    ).astype(np.float32)
    angle = np.arange(CHAIN * BLOCK, dtype=np.float32)[:, None] * frequency[None, :]
    cosine, sine = np.cos(angle), np.sin(angle)
    return (
        np.concatenate([cosine, cosine], axis=1).astype(np.float32),
        np.concatenate([-sine, sine], axis=1).astype(np.float32),
    )


def depth_of(parent_ref, slot):
    def up(_, carry):
        at, depth = carry
        parent = jnp.where(at >= 0, parent_ref[jnp.maximum(at, 0)], -1)
        return parent, depth + jnp.where(parent >= 0, 1, 0).astype(jnp.int32)

    return lax.fori_loop(0, CHAIN - 1, up, (slot, jnp.int32(0)))[1]


def xor_pairs(count, mask):
    return [(index, index ^ mask) for index in range(count)]


class Plan:
    def __init__(self, mesh, rows, width, heads, ff):
        self.dp = mesh.shape["dp"]
        self.tensor = mesh.shape["tensor"]
        self.rows, self.width, self.heads, self.ff = rows, width, heads, ff
        self.slots = rows // BLOCK
        self.spread = heads
        self.rest = self.dp // heads
        self.bits = self.dp.bit_length() - 1
        self.piece = width // self.dp
        self.own = rows // self.tensor
        self.groups = 2 if self.own % 32 == 0 else 1
        self.part = rows // self.groups
        self.share = self.own // self.groups

    def own_rows(self, group):
        return pl.BlockSpec(
            (self.share, self.width), lambda i, place: (group * self.tensor + place[1], 0)
        )

    def own_part(self):
        return pl.BlockSpec((self.share, self.width), lambda i, place: (place[1], 0))


def fetch(weights, held, sems, kind):
    copies = [
        pltpu.make_async_copy(w, held.at[index], sems.at[index]) for index, w in enumerate(weights)
    ]

    @pl.when(kind == 0)
    def _():
        for copy in copies:
            copy.start()

    def wait():
        for index, copy in enumerate(copies):

            @pl.when(kind == index)
            def _():
                copy.wait()

    return wait


def qkv_kernel(plan, parent, place, x, wq, wk, wv, cosine, sine, normed, *rest):
    outs, stage = rest[: plan.spread], rest[-1]
    me = place[0]
    part = me // plan.rest
    depth = depth_of(parent, me * plan.slots + pl.program_id(0))
    rows = pl.ds(pl.multiple_of(depth * BLOCK, BLOCK), BLOCK)
    cos, sin = cosine[rows, :], sine[rows, :]
    low = layer_norm(x[...].astype(F32))[0].astype(LOW)
    normed[...] = low
    for kind, w in enumerate((wq, wk, wv)):
        y = dot(low, w[...])
        for head in range(plan.heads):
            yh = y[:, head * HEAD : (head + 1) * HEAD]
            if kind < 2:
                yh = yh * cos + pltpu.roll(yh, HEAD // 2, 1) * sin
            stage[head, kind] = yh.astype(LOW)
    for d in range(plan.spread):
        outs[d][...] = stage[part ^ d]


def kept_order(plan):
    return [
        sum(((at >> bit) & 1) << (plan.bits - 1 - bit) for bit in range(plan.bits - 1))
        for at in range(plan.dp // 2)
    ]


def project_qkv(plan, slot_parent, place, tokens, wq, wk, wv, cosine, sine):
    whole = lambda i, *_: (0, 0)
    once = pl.Buffered(buffer_count=1)
    wide = plan.heads * HEAD
    return pl.pallas_call(
        functools.partial(qkv_kernel, plan),
        grid_spec=pltpu.PrefetchScalarGridSpec(
            num_scalar_prefetch=2,
            grid=(plan.slots,),
            in_specs=[pl.BlockSpec((BLOCK, plan.width), lambda i, *_: (i, 0))]
            + [pl.BlockSpec((plan.width, wide), whole, pipeline_mode=once)] * 3
            + [pl.BlockSpec((CHAIN * BLOCK, HEAD), whole, pipeline_mode=once)] * 2,
            out_specs=[pl.BlockSpec((BLOCK, plan.width), lambda i, *_: (i, 0))]
            + [pl.BlockSpec((3, BLOCK, HEAD), lambda i, *_: (0, i, 0))] * plan.spread,
            scratch_shapes=[
                pltpu.VMEM((plan.heads, 3, BLOCK, HEAD), LOW),
            ],
        ),
        out_shape=[shape((plan.rows, plan.width), LOW)]
        + [shape((3, plan.rows, HEAD), LOW)] * plan.spread,
        compiler_params=params(60),
        cost_estimate=about(0),
        name="project_qkv",
    )(slot_parent, place, tokens, wq, wk, wv, cosine, sine)


def gather_chain(plan, parent, me, slot, kv, keys, values):
    count = jnp.int32(0)
    at = slot
    places = []
    for step in range(CHAIN):
        here = jnp.maximum(at, 0)
        relative = (here // plan.slots) ^ me
        block = (
            (relative % plan.rest) * plan.spread + relative // plan.rest
        ) * 2 * plan.slots + here % plan.slots
        keys[step * BLOCK : (step + 1) * BLOCK, :] = kv[block]
        values[step * BLOCK : (step + 1) * BLOCK, :] = kv[block + plan.slots]
        places.append(block)
        valid = at >= 0
        count = count + jnp.where(valid, 1, 0).astype(jnp.int32)
        at = jnp.where(valid, parent[here], -1)
    return count, places


def chain_weights(queries, keys, counts):
    scores = [dot_nt(k, q) * SCALE for q, k in zip(queries, keys)]
    key_at = lax.broadcasted_iota(jnp.int32, scores[0].shape, 0)
    query_at = lax.broadcasted_iota(jnp.int32, scores[0].shape, 1)
    own = (key_at >= BLOCK) | (key_at <= query_at)
    probs = []
    for score, count in zip(scores, counts):
        score = jnp.where(own & (key_at < count * BLOCK), score, NEGATIVE)
        raised = jnp.exp(score - jnp.max(score, axis=0, keepdims=True))
        probs.append(raised * (1.0 / jnp.sum(raised, axis=0, keepdims=True)))
    return probs


def attend_kernel(plan, parent, place, *refs):
    n = plan.spread
    q_refs, kv, o_refs, keys, values = refs[:n], refs[n], refs[n + 1 : 2 * n + 1], refs[-2], refs[-1]
    me = place[0]

    def one(i, carry):
        rows = pl.ds(pl.multiple_of(i * BLOCK, BLOCK), BLOCK)
        slots = [(me ^ (d * plan.rest)) * plan.slots + i for d in range(n)]
        counts = [
            gather_chain(plan, parent, me, slots[d], kv, keys.at[d], values.at[d])[0]
            for d in range(n)
        ]
        queries = [q_refs[d][0, rows, :] for d in range(n)]
        probs = chain_weights(queries, [keys[d] for d in range(n)], counts)
        for d in range(n):
            o_refs[d][rows, :] = dot_tn(probs[d].astype(LOW), values[d]).astype(LOW)
        return carry

    lax.fori_loop(0, plan.slots, one, 0)


def attend(plan, slot_parent, place, parts, kv):
    n = plan.spread
    blocks = plan.dp * 2 * plan.slots
    return pl.pallas_call(
        functools.partial(attend_kernel, plan),
        grid_spec=pltpu.PrefetchScalarGridSpec(
            num_scalar_prefetch=2,
            grid=(1,),
            in_specs=[pl.BlockSpec((1, plan.rows, HEAD), lambda i, *_: (0, 0, 0))] * n
            + [pl.BlockSpec((blocks, BLOCK, HEAD), lambda i, *_: (0, 0, 0))],
            out_specs=[pl.BlockSpec((plan.rows, HEAD), lambda i, *_: (0, 0))] * n,
            scratch_shapes=[pltpu.VMEM((n, CHAIN * BLOCK, HEAD), LOW)] * 2,
        ),
        out_shape=[shape((plan.rows, HEAD), LOW)] * n,
        compiler_params=params(60),
        cost_estimate=about(0),
        name="attend",
    )(slot_parent, place, *parts, kv)


def attend_back_kernel(plan, parent, place, *refs):
    n = plan.spread
    q_refs, kv, g_refs = refs[:n], refs[n], refs[n + 1 : 2 * n + 1]
    dq_refs = refs[2 * n + 1 : 3 * n + 1]
    near, far, keys, values, total = refs[3 * n + 1 :]
    me = place[0]
    total[...] = jnp.zeros_like(total)

    def one(i, carry):
        rows = pl.ds(pl.multiple_of(i * BLOCK, BLOCK), BLOCK)
        slots = [(me ^ (d * plan.rest)) * plan.slots + i for d in range(n)]
        chains = [
            gather_chain(plan, parent, me, slots[d], kv, keys.at[d], values.at[d])
            for d in range(n)
        ]
        queries = [q_refs[d][0, rows, :] for d in range(n)]
        grads = [g_refs[d][rows, :] for d in range(n)]
        probs = chain_weights(queries, [keys[d] for d in range(n)], [chain[0] for chain in chains])
        for d in range(n):
            grad_prob = dot_nt(values[d], grads[d])
            inner = jnp.sum(grad_prob * probs[d], axis=0, keepdims=True)
            grad_scores = (probs[d] * (grad_prob - inner)).astype(LOW)
            dv = dot(probs[d].astype(LOW), grads[d])
            dk = dot(grad_scores, queries[d]) * SCALE
            dq_refs[d][rows, :] = (dot_tn(grad_scores, keys[d]) * SCALE).astype(LOW)
            for step, block in enumerate(chains[d][1]):
                span = slice(step * BLOCK, (step + 1) * BLOCK)
                total[block] = total[block] + dk[span]
                total[block + plan.slots] = total[block + plan.slots] + dv[span]
        return carry

    lax.fori_loop(0, plan.slots, one, 0)
    half = near.shape[0]
    near[...] = total[:half]
    far[...] = total[half:].astype(LOW)


def attend_back(plan, slot_parent, place, parts, kv, grads):
    n = plan.spread
    blocks = plan.dp * 2 * plan.slots
    near = n * 2 * plan.slots
    return pl.pallas_call(
        functools.partial(attend_back_kernel, plan),
        grid_spec=pltpu.PrefetchScalarGridSpec(
            num_scalar_prefetch=2,
            grid=(1,),
            in_specs=[pl.BlockSpec((1, plan.rows, HEAD), lambda i, *_: (0, 0, 0))] * n
            + [pl.BlockSpec((blocks, BLOCK, HEAD), lambda i, *_: (0, 0, 0))]
            + [pl.BlockSpec((plan.rows, HEAD), lambda i, *_: (0, 0))] * n,
            out_specs=[pl.BlockSpec((plan.rows, HEAD), lambda i, *_: (0, 0))] * n
            + [
                pl.BlockSpec((near, BLOCK, HEAD), lambda i, *_: (0, 0, 0)),
                pl.BlockSpec((blocks - near, BLOCK, HEAD), lambda i, *_: (0, 0, 0)),
            ],
            scratch_shapes=[pltpu.VMEM((n, CHAIN * BLOCK, HEAD), LOW)] * 2
            + [pltpu.VMEM((blocks, BLOCK, HEAD), F32)],
        ),
        out_shape=[shape((plan.rows, HEAD), LOW)] * n
        + [shape((near, BLOCK, HEAD), F32), shape((blocks - near, BLOCK, HEAD), LOW)],
        compiler_params=params(60),
        cost_estimate=about(23),
        name="attend_back",
    )(slot_parent, place, *parts, kv, *grads)


def combine_kernel(plan, *refs):
    n = plan.spread
    queries, (near, got), outs = refs[:n], refs[n : n + 2], refs[n + 2 :]
    for d in range(n):
        outs[d][0] = queries[d][...]
        for kind in range(2):
            for slot in range(plan.slots):
                block = (d * 2 + kind) * plan.slots + slot
                rows = slice(slot * BLOCK, (slot + 1) * BLOCK)
                total = near[block] + got[block].astype(F32)
                outs[d][kind + 1, rows, :] = total.astype(LOW)


def combine_back(plan, queries, near, got):
    n = plan.spread
    return pl.pallas_call(
        functools.partial(combine_kernel, plan),
        out_shape=[shape((3, plan.rows, HEAD), LOW)] * n,
        compiler_params=params(60),
        cost_estimate=about(3),
        name="combine_back",
    )(*queries, near, got)


def heads_kernel(plan, place, *refs):
    part = place[0] // plan.rest
    outs = refs[plan.spread :]
    for d in range(plan.spread):
        head = pl.ds(pl.multiple_of((part ^ d) * HEAD, HEAD), HEAD)
        for group, out in enumerate(outs):
            out[:, head] = refs[d][group * plan.part : (group + 1) * plan.part, :]


def gather_heads(plan, place, parts):
    wide = plan.heads * HEAD
    return pl.pallas_call(
        functools.partial(heads_kernel, plan),
        grid_spec=pltpu.PrefetchScalarGridSpec(
            num_scalar_prefetch=1,
            grid=(1,),
            in_specs=[pl.BlockSpec((plan.rows, HEAD), lambda i, *_: (0, 0))] * plan.spread,
            out_specs=[pl.BlockSpec((plan.part, wide), lambda i, *_: (0, 0))] * plan.groups,
        ),
        out_shape=[shape((plan.part, wide), LOW)] * plan.groups,
        compiler_params=params(60),
        cost_estimate=about(0),
        name="gather_heads",
    )(place, *parts)


def scatter_kernel(plan, place, *refs):
    part, z = place[0] // plan.rest, place[1]
    sources, outs = refs[: plan.tensor], refs[plan.tensor :]
    for shift in range(plan.tensor):
        origin = lax.rem(z - shift + plan.tensor, plan.tensor)
        for group in range(plan.groups):
            start = group * plan.part + origin * plan.share
            rows = pl.ds(pl.multiple_of(start, 16), plan.share)
            share = slice(group * plan.share, (group + 1) * plan.share)
            for d in range(plan.spread):
                head = pl.ds(pl.multiple_of((part ^ d) * HEAD, HEAD), HEAD)
                outs[d][rows, :] = sources[shift][share, head]


def scatter_heads(plan, place, sources):
    return pl.pallas_call(
        functools.partial(scatter_kernel, plan),
        grid_spec=pltpu.PrefetchScalarGridSpec(
            num_scalar_prefetch=1,
            grid=(1,),
            in_specs=[pl.BlockSpec((plan.own, plan.heads * HEAD), lambda i, *_: (0, 0))]
            * plan.tensor,
            out_specs=[pl.BlockSpec((plan.rows, HEAD), lambda i, *_: (0, 0))] * plan.spread,
        ),
        out_shape=[shape((plan.rows, HEAD), LOW)] * plan.spread,
        name="scatter_heads",
    )(place, *sources)


def turn_back_kernel(plan, parent, place, cosine, sine, wq, wk, wv, *refs):
    parts, (back, out, product) = refs[: plan.spread], refs[plan.spread :]
    me = place[0]
    part = me // plan.rest
    wide = plan.heads * HEAD

    @pl.when(pl.program_id(0) == 0)
    def _():
        for slot in range(plan.slots):
            depth = depth_of(parent, me * plan.slots + slot)
            table = pl.ds(pl.multiple_of(depth * BLOCK, BLOCK), BLOCK)
            cos, sin = cosine[table, :], sine[table, :]
            rows = slice(slot * BLOCK, (slot + 1) * BLOCK)
            for d in range(plan.spread):
                for kind in range(3):
                    value = parts[d][kind, rows, :]
                    if kind < 2:
                        value = value.astype(F32)
                        value = value * cos - pltpu.roll(value, HEAD // 2, 1) * sin
                    at = pl.multiple_of((kind * plan.heads + (part ^ d)) * HEAD, HEAD)
                    out[rows, pl.ds(at, HEAD)] = value.astype(LOW)

    total = 0.0
    for kind, w in enumerate((wq, wk, wv)):
        total = total + dot_nt(out[:, kind * wide : (kind + 1) * wide], w[...])
    product[...] = total
    for device in range(plan.tensor):
        for group in range(plan.groups):
            source = (group * plan.tensor + device) * plan.share
            target = (device * plan.groups + group) * plan.share
            back[target : target + plan.share, :] = product[
                source : source + plan.share, :
            ].astype(LOW)


def turn_back(plan, slot_parent, place, cosine, sine, weights, parts):
    whole = lambda i, *_: (0, 0)
    wide = plan.heads * HEAD
    tile = min(512, plan.width)
    return pl.pallas_call(
        functools.partial(turn_back_kernel, plan),
        grid_spec=pltpu.PrefetchScalarGridSpec(
            num_scalar_prefetch=2,
            grid=(plan.width // tile,),
            in_specs=[pl.BlockSpec((CHAIN * BLOCK, HEAD), whole)] * 2
            + [pl.BlockSpec((tile, wide), lambda i, *_: (i, 0))] * 3
            + [pl.BlockSpec((3, plan.rows, HEAD), lambda i, *_: (0, 0, 0))] * plan.spread,
            out_specs=[
                pl.BlockSpec((plan.rows, tile), lambda i, *_: (0, i)),
                pl.BlockSpec((plan.rows, 3 * wide), whole),
            ],
            scratch_shapes=[pltpu.VMEM((plan.rows, tile), F32)],
        ),
        out_shape=[shape((plan.rows, plan.width), LOW), shape((plan.rows, 3 * wide), LOW)],
        compiler_params=params(60),
        cost_estimate=about(13),
        name="turn_back",
    )(slot_parent, place, cosine, sine, *weights, *parts)


def out_kernel(plan, place, x, att, near, far, middle, normed):
    half = plan.heads * HEAD // 2
    core = place[0] % 2
    total = x[...].astype(F32)
    for z in range(plan.tensor):
        for side, w in ((core, near), (1 - core, far)):
            columns = pl.ds(pl.multiple_of(side * half, half), half)
            total = total + dot(att[z, :, columns], w[z])
    middle[...] = total
    normed[...] = layer_norm(total)[0].astype(LOW)


def project_out(plan, place, group, tokens, att, near, far):
    half = plan.heads * HEAD // 2
    count = 2
    rows = plan.part // count
    weights = pl.BlockSpec(
        (plan.tensor, half, plan.width),
        lambda i, *_: (0, 0, 0),
        pipeline_mode=pl.Buffered(buffer_count=1),
    )
    out = pl.BlockSpec((rows, plan.width), lambda i, *_: (i, 0))
    return pl.pallas_call(
        functools.partial(out_kernel, plan),
        grid_spec=pltpu.PrefetchScalarGridSpec(
            num_scalar_prefetch=1,
            grid=(count,),
            in_specs=[
                pl.BlockSpec((rows, plan.width), lambda i, *_: (group * count + i, 0)),
                pl.BlockSpec((plan.tensor, rows, 2 * half), lambda i, *_: (0, i, 0)),
                weights,
                weights,
            ],
            out_specs=[out, out],
        ),
        out_shape=[shape((plan.part, plan.width), F32), shape((plan.part, plan.width), LOW)],
        compiler_params=params(60),
        cost_estimate=about(7),
        name="project_out",
    )(place, tokens, att, near, far)


def grad_hidden_kernel(cot, wd, out):
    out[...] = dot_nt(cot[...], wd[...])


def grad_hidden_of(cot, wd):
    rows, width = cot.shape
    ff = wd.shape[0]
    tile = min(512, ff)
    return pl.pallas_call(
        grad_hidden_kernel,
        grid=(ff // tile,),
        in_specs=[
            pl.BlockSpec((rows, width), lambda i: (0, 0)),
            pl.BlockSpec((tile, width), lambda i: (i, 0)),
        ],
        out_specs=pl.BlockSpec((rows, tile), lambda i: (0, i)),
        out_shape=shape((rows, ff), F32),
        compiler_params=params(60),
        cost_estimate=about(0),
        name="grad_hidden",
    )(cot, wd)


def ff_kernel(tile, normed, seed, wg, wu, back, hidden, grad_gate, grad_up, *scratch):
    gate_held, up_held, results, total, in_sems, out_sems = scratch
    count = wg.shape[1] // tile
    spans = [slice(index * tile, (index + 1) * tile) for index in range(count)]
    arrivals = [
        [
            pltpu.make_async_copy(w.at[:, span], held.at[:, span], in_sems.at[which, index])
            for which, (w, held) in enumerate(((wg, gate_held), (wu, up_held)))
        ]
        for index, span in enumerate(spans)
    ]
    departures = [
        [
            pltpu.make_async_copy(
                results.at[which, :, span], out.at[:, span], out_sems.at[which, index]
            )
            for which, out in enumerate((hidden, grad_gate, grad_up))
        ]
        for index, span in enumerate(spans)
    ]
    for pair in arrivals:
        for copy in pair:
            copy.start()
    for index, span in enumerate(spans):
        for copy in arrivals[index]:
            copy.wait()
        gate = dot(normed[...], gate_held[:, span])
        up = dot(normed[...], up_held[:, span])
        grad_hidden = seed[:, span]
        s = 1.0 / (1.0 + jnp.exp(-gate))
        active = gate * s
        gu = (grad_hidden * active).astype(LOW)
        gg = (grad_hidden * up * s * (1.0 + gate * (1.0 - s))).astype(LOW)
        results[0, :, span] = (active * up).astype(LOW)
        results[1, :, span] = gg
        results[2, :, span] = gu
        for copy in departures[index]:
            copy.start()
        part = dot_nt(gg, gate_held[:, span]) + dot_nt(gu, up_held[:, span])
        if index == 0:
            total[...] = part
        elif index < count - 1:
            total[...] += part
        else:
            back[...] = (total[...] + part).astype(LOW)
    for triple in departures:
        for copy in triple:
            copy.wait()


def feed_forward(plan, place, group, normed, seed, wg, wu):
    rows, width = normed.shape
    ff = wg.shape[1]
    tile = min(512, ff // 2)
    whole = pl.BlockSpec((rows, width), lambda i: (0, 0))
    anywhere = pl.BlockSpec(memory_space=pl.ANY)
    return pl.pallas_call(
        functools.partial(ff_kernel, tile),
        grid=(1,),
        in_specs=[whole, pl.BlockSpec((rows, ff), lambda i: (group, 0)), anywhere, anywhere],
        out_specs=[whole, anywhere, anywhere, anywhere],
        out_shape=[shape((rows, width), LOW)] + [shape((rows, ff), LOW)] * 3,
        scratch_shapes=[
            pltpu.VMEM((width, ff), LOW),
            pltpu.VMEM((width, ff), LOW),
            pltpu.VMEM((3, rows, ff), LOW),
            pltpu.VMEM((rows, width), F32),
            pltpu.SemaphoreType.DMA((2, ff // tile)),
            pltpu.SemaphoreType.DMA((3, ff // tile)),
        ],
        compiler_params=params(62),
        cost_estimate=about(17),
        name="feed_forward",
    )(normed, seed, wg, wu)


def down_kernel(plan, *refs):
    hiddens, (w, out) = refs[: plan.groups], refs[plan.groups :]
    for group, hidden in enumerate(hiddens):
        rows = slice(group * plan.part, (group + 1) * plan.part)
        out[rows, :] = dot(hidden[...], w[...]).astype(LOW)


def project_down(plan, hiddens, w):
    ff, width = w.shape
    tile = min(512, width)
    return pl.pallas_call(
        functools.partial(down_kernel, plan),
        grid=(width // tile,),
        in_specs=[pl.BlockSpec((plan.part, ff), lambda i: (0, 0))] * plan.groups
        + [pl.BlockSpec((ff, tile), lambda i: (0, i))],
        out_specs=pl.BlockSpec((plan.rows, tile), lambda i: (0, i)),
        out_shape=shape((plan.rows, width), LOW),
        compiler_params=params(60),
        cost_estimate=about(11),
        name="project_down",
    )(*hiddens, w)


def branch_back_kernel(plan, place, *refs):
    count = plan.groups
    parts, middles, cots = refs[:count], refs[count : 2 * count], refs[2 * count : 3 * count]
    near, far, grad_middle, low = refs[3 * count : 3 * count + 4]
    outs, (near_held, far_held, sems) = refs[3 * count + 4 : -3], refs[-3:]
    core, z = place[0] % 2, place[1]
    half = plan.heads * HEAD // 2
    sides = ((core, near, near_held), (1 - core, far, far_held))
    copies = [
        [
            pltpu.make_async_copy(
                w.at[lax.rem(z + shift, plan.tensor)], held.at[shift], sems.at[index, shift]
            )
            for index, (_, w, held) in enumerate(sides)
        ]
        for shift in range(plan.tensor)
    ]
    for pair in copies:
        for copy in pair:
            copy.start()
    for group in range(count):
        rows = slice(group * plan.share, (group + 1) * plan.share)
        normed, inverse = layer_norm(middles[group][...])
        back = norm_back(parts[group][...].astype(F32), normed, inverse)
        grad = cots[group][...].astype(F32) + back
        grad_middle[rows, :] = grad
        low[rows, :] = grad.astype(LOW)
    for shift in range(plan.tensor):
        for copy, (side, _, held) in zip(copies[shift], sides):
            copy.wait()
            columns = pl.ds(pl.multiple_of(side * half, half), half)
            outs[shift][:, columns] = dot_nt(low[...], held[shift]).astype(LOW)


def branch_back(plan, place, parts, middles, cot, near, far):
    half = plan.heads * HEAD // 2
    own = pl.BlockSpec((plan.own, plan.width), lambda i, *_: (0, 0))
    share = pl.BlockSpec((plan.share, plan.width), lambda i, *_: (0, 0))
    anywhere = pl.BlockSpec(memory_space=pl.ANY)
    return pl.pallas_call(
        functools.partial(branch_back_kernel, plan),
        grid_spec=pltpu.PrefetchScalarGridSpec(
            num_scalar_prefetch=1,
            grid=(1,),
            in_specs=[share] * plan.groups
            + [plan.own_part()] * plan.groups
            + [plan.own_rows(group) for group in range(plan.groups)]
            + [anywhere, anywhere],
            out_specs=[own, own]
            + [pl.BlockSpec((plan.own, 2 * half), lambda i, *_: (0, 0))] * plan.tensor,
            scratch_shapes=[pltpu.VMEM((plan.tensor, half, plan.width), LOW)] * 2
            + [pltpu.SemaphoreType.DMA((2, plan.tensor))],
        ),
        out_shape=[shape((plan.own, plan.width), F32), shape((plan.own, plan.width), LOW)]
        + [shape((plan.own, 2 * half), LOW)] * plan.tensor,
        compiler_params=params(60),
        cost_estimate=about(9),
        name="branch_back",
    )(place, *parts, *middles, *([cot] * plan.groups), near, far)


def tokens_back_kernel(plan, place, part, *refs):
    tokens, (grad_middle, out) = refs[: plan.groups], refs[plan.groups :]
    for group in range(plan.groups):
        rows = slice(group * plan.share, (group + 1) * plan.share)
        normed, inverse = layer_norm(tokens[group][...].astype(F32))
        back = norm_back(part[rows, :].astype(F32), normed, inverse)
        out[rows, :] = (grad_middle[rows, :] + back).astype(LOW)


def tokens_back(plan, place, part, tokens, grad_middle):
    own = pl.BlockSpec((plan.own, plan.width), lambda i, *_: (0, 0))
    return pl.pallas_call(
        functools.partial(tokens_back_kernel, plan),
        grid_spec=pltpu.PrefetchScalarGridSpec(
            num_scalar_prefetch=1,
            grid=(1,),
            in_specs=[own] + [plan.own_rows(group) for group in range(plan.groups)] + [own],
            out_specs=own,
        ),
        out_shape=shape((plan.own, plan.width), LOW),
        compiler_params=params(60),
        cost_estimate=about(4),
        name="tokens_back",
    )(place, part, *([tokens] * plan.groups), grad_middle)


def products(lhs, rhs):
    total, start = 0.0, 0
    for index, right in enumerate(rhs):
        rows = right.shape[0]
        left = lhs[index][...] if len(lhs) > 1 else lhs[0][start : start + rows, :]
        total = total + dot_tn(left, right[...])
        start += rows
    return total


def away_kernel(count, place, *refs):
    lhs, rhs, out = refs[:count], refs[count:-1], refs[-1]
    out[...] = products(lhs, rhs).astype(LOW)


def wgrad_away(plan, place, lhs, rhs):
    columns = rhs[0].shape[1]
    piece, count = plan.piece, plan.dp // 2
    return pl.pallas_call(
        functools.partial(away_kernel, len(lhs)),
        grid_spec=pltpu.PrefetchScalarGridSpec(
            num_scalar_prefetch=1,
            grid=(count,),
            in_specs=[
                pl.BlockSpec((part.shape[0], piece), lambda i, place: (0, place[2 + i] ^ 1))
                for part in lhs
            ]
            + [pl.BlockSpec(part.shape, lambda i, *_: (0, 0)) for part in rhs],
            out_specs=pl.BlockSpec((piece, columns), lambda i, *_: (i, 0)),
        ),
        out_shape=shape((count * piece, columns), LOW),
        compiler_params=params(60),
        cost_estimate=about(8),
        name="wgrad_away",
    )(place, *lhs, *rhs)


def keep_kernel(arrays, count, place, *refs):
    lhs, rhs = refs[:arrays], refs[arrays:-5]
    recv, a_keep, a_send, b_keep, b_send = refs[-5:]
    step = pl.program_id(0)
    total = (products(lhs, rhs) + recv[...].astype(F32)).astype(LOW)
    half = total.shape[1] // 2

    @pl.when(step < count // 2)
    def _():
        a_keep[...] = total[:, :half]

    @pl.when(step >= count // 2)
    def _():
        a_send[...] = total[:, :half]

    @pl.when(step % 2 == 0)
    def _():
        b_keep[...] = total[:, half:]

    @pl.when(step % 2 == 1)
    def _():
        b_send[...] = total[:, half:]


def wgrad_keep(plan, place, lhs, rhs, recv):
    columns = rhs[0].shape[1]
    piece, count = plan.piece, plan.dp // 2
    half = count // 2
    block = lambda index: pl.BlockSpec((piece, columns // 2), index)
    return pl.pallas_call(
        functools.partial(keep_kernel, len(lhs), count),
        grid_spec=pltpu.PrefetchScalarGridSpec(
            num_scalar_prefetch=1,
            grid=(count,),
            in_specs=[
                pl.BlockSpec((part.shape[0], piece), lambda i, place: (0, place[2 + i]))
                for part in lhs
            ]
            + [pl.BlockSpec(part.shape, lambda i, *_: (0, 0)) for part in rhs]
            + [pl.BlockSpec((piece, columns), lambda i, *_: (i, 0))],
            out_specs=[
                block(lambda i, *_: (jnp.minimum(i, half - 1), 0)),
                block(lambda i, *_: (jnp.maximum(i - half, 0), 0)),
                block(lambda i, *_: (i // 2, 0)),
                block(lambda i, *_: (i // 2, 0)),
            ],
        ),
        out_shape=[shape((half * piece, columns // 2), LOW)] * 4,
        compiler_params=params(60),
        cost_estimate=about(9),
        name="wgrad_keep",
    )(place, *lhs, *rhs, recv)


def stage_kernel(piece, a, a_got, b, b_got, a_keep, a_send, b_keep, b_send):
    total = a[...].astype(F32) + a_got[...].astype(F32)
    half = total.shape[0] // 2
    a_keep[...] = total[:half].astype(LOW)
    a_send[...] = total[half:].astype(LOW)
    for at in range(0, 2 * half, 2 * piece):
        for start, out in ((at, b_keep), (at + piece, b_send)):
            rows = slice(start, start + piece)
            total = b[rows, :].astype(F32) + b_got[rows, :].astype(F32)
            out[at // 2 : at // 2 + piece, :] = total.astype(LOW)


def wgrad_stage(piece, *arrays):
    rows, columns = arrays[0].shape
    tile = columns // 2 if columns % 256 == 0 else columns
    block = lambda size: pl.BlockSpec((size, tile), lambda i: (0, i))
    return pl.pallas_call(
        functools.partial(stage_kernel, piece),
        grid=(columns // tile,),
        in_specs=[block(rows)] * 4,
        out_specs=[block(rows // 2)] * 4,
        out_shape=[shape((rows // 2, columns), LOW)] * 4,
        compiler_params=params(60),
        cost_estimate=about(3),
        name="wgrad_stage",
    )(*arrays)


def finish_kernel(turned, a, a_got, b, b_got, out):
    half = a.shape[1]
    for way, (keep, got) in enumerate(((a, a_got), (b, b_got))):
        total = keep[...].astype(F32) + got[...].astype(F32)
        span = slice(way * half, (way + 1) * half)
        if turned:
            out[span, :] = total.T
        else:
            out[:, span] = total


def wgrad_finish(turned, *arrays):
    piece, half = arrays[0].shape
    return pl.pallas_call(
        functools.partial(finish_kernel, turned),
        out_shape=shape((2 * half, piece) if turned else (piece, 2 * half), F32),
        compiler_params=params(60),
        cost_estimate=about(3),
        name="wgrad_finish",
    )(*arrays)


def split_kernel(*refs):
    arrays, outs, held = refs[:4], refs[4:-1], refs[-1]
    finish_kernel(False, *arrays, held)
    width = outs[0].shape[1]
    for index, out in enumerate(outs):
        out[...] = held[:, index * width : (index + 1) * width]


def wgrad_finish_split(*arrays):
    piece, half = arrays[0].shape
    return pl.pallas_call(
        split_kernel,
        out_shape=[shape((piece, 2 * half // 3), F32)] * 3,
        scratch_shapes=[pltpu.VMEM((piece, 2 * half), F32)],
        compiler_params=params(60),
        cost_estimate=about(3),
        name="wgrad_finish_split",
    )(*arrays)


def chunks_kernel(plan, place, *refs):
    arrays, chunks, held = refs[:4], refs[4:-1], refs[-1]
    finish_kernel(True, *arrays, held)
    rows = plan.heads * HEAD
    for index, chunk in enumerate(chunks):
        chunk[...] = held[ring_rows(plan, place, index, rows), :].astype(LOW)


def wgrad_finish_chunks(plan, place, *arrays):
    piece, half = arrays[0].shape
    rows = plan.heads * HEAD
    return pl.pallas_call(
        functools.partial(chunks_kernel, plan),
        grid_spec=pltpu.PrefetchScalarGridSpec(
            num_scalar_prefetch=1,
            grid=(1,),
            in_specs=[pl.BlockSpec((piece, half), lambda i, *_: (0, 0))] * 4,
            out_specs=[pl.BlockSpec((rows, piece), lambda i, *_: (0, 0))] * plan.tensor,
            scratch_shapes=[pltpu.VMEM((2 * half, piece), F32)],
        ),
        out_shape=[shape((rows, piece), LOW)] * plan.tensor,
        compiler_params=params(60),
        cost_estimate=about(4),
        name="wgrad_finish_chunks",
    )(place, *arrays)


def tie(values, *others):
    many = isinstance(values, (list, tuple))
    held = lax.optimization_barrier((tuple(values) if many else (values,)) + others)
    return list(held[: len(values)]) if many else held[0]


class WeightGradient:
    def __init__(self, plan, place, chain, lhs, rhs, turned=False, chunks=False, split=False):
        self.chunks, self.split = chunks, split
        self.plan, self.place, self.chain = plan, place, chain
        self.lhs, self.rhs, self.turned = lhs, rhs, turned
        self.stage = 0

    def swap(self, array, bit):
        return lax.ppermute(array, "dp", xor_pairs(self.plan.dp, 1 << bit))

    def away(self):
        sent = self.chain.run(
            lambda *r: wgrad_away(self.plan, self.place, self.lhs, r), *self.rhs
        )
        self.recv = self.swap(sent, 0)

    def keep(self):
        self.a_keep, self.a_send, self.b_keep, self.b_send = self.chain.run(
            lambda r: wgrad_keep(self.plan, self.place, self.lhs, self.rhs, r), self.recv
        )

    def send(self):
        upwards = list(range(1, self.plan.bits))
        a, b = self.chain.after(self.a_send, self.b_send)
        self.a_got = self.swap(a, upwards[self.stage])
        self.b_got = self.swap(b, upwards[-1 - self.stage])
        self.stage += 1

    def wait(self):
        self.a_got, self.b_got = self.chain.wait(self.a_got, self.b_got)

    def took(self):
        self.recv = self.chain.wait(self.recv)

    def add(self):
        self.a_keep, self.a_send, self.b_keep, self.b_send = self.chain.run(
            lambda *p: wgrad_stage(self.plan.piece, *p),
            self.a_keep,
            self.a_got,
            self.b_keep,
            self.b_got,
        )

    def finish(self):
        while self.stage < self.plan.bits - 1:
            self.add()
            self.send()
        return self.chain.run(
            lambda *p: (
                wgrad_finish_chunks(self.plan, self.place, *p)
                if self.chunks
                else wgrad_finish_split(*p)
                if self.split
                else wgrad_finish(self.turned, *p)
            ),
            self.a_keep,
            self.a_got,
            self.b_keep,
            self.b_got,
        )


class Chain:
    weight = 1.0

    def __init__(self, last):
        self.last = last

    def after(self, *values):
        held = lax.optimization_barrier(values + (self.last,))
        return held[0] if len(values) == 1 else list(held[:-1])

    def wait(self, *values):
        held = lax.optimization_barrier(values + (self.last,))
        self.last = held[0]
        return held[0] if len(values) == 1 else list(held[:-1])

    def run(self, step, *values):
        held = self.after(*values)
        out = step(*held) if len(values) > 1 else step(held)
        self.last = out[0] if isinstance(out, (list, tuple)) else out
        return out


def shifted(plan, array, shift):
    pairs = [(i, (i + shift) % plan.tensor) for i in range(plan.tensor)]
    return lax.ppermute(array, "tensor", pairs)


class RingSum:
    def __init__(self, plan, chain, chunks):
        self.plan, self.chain, self.chunks, self.at = plan, chain, chunks, 1
        self.moving = shifted(plan, chunks[0], 1)

    def step(self):
        if self.at < self.plan.tensor - 1:
            got, mine = self.chain.wait(self.moving, self.chunks[self.at])
            total = (got.astype(F32) + mine.astype(F32)).astype(LOW)
            self.chain.last = total
            self.moving = shifted(self.plan, total, 1)
            self.at += 1

    def finish(self):
        while self.at < self.plan.tensor - 1:
            self.step()
        return self.moving, self.chunks[-1]


def ring_rows(plan, place, step, rows):
    chunk = lax.rem(place[1] + (2 * plan.tensor - 1 - step), plan.tensor)
    return pl.ds(pl.multiple_of(chunk * rows, 16), rows)


def add_last_kernel(a, b, out):
    out[...] = a[...].astype(F32) + b[...].astype(F32)


def add_last(a, b):
    return pl.pallas_call(
        add_last_kernel,
        out_shape=shape(a.shape, F32),
        compiler_params=params(60),
        cost_estimate=about(2),
        name="add_last",
    )(a, b)


def add_kernel(plan, *refs):
    middles, (part, out) = refs[: plan.groups], refs[plan.groups :]
    step = pl.program_id(0)
    for group, middle in enumerate(middles):

        @pl.when(step // 2 == group)
        def _():
            out[...] = (middle[...] + part[...].astype(F32)).astype(LOW)


def add_residual(plan, middles, part):
    rows = plan.part // 2
    block = pl.BlockSpec((rows, plan.width), lambda i: (i, 0))
    return pl.pallas_call(
        functools.partial(add_kernel, plan),
        grid=(2 * plan.groups,),
        in_specs=[
            pl.BlockSpec(
                (rows, plan.width),
                lambda i, group=group: (jnp.clip(i - 2 * group, 0, 1), 0),
            )
            for group in range(plan.groups)
        ]
        + [block],
        out_specs=block,
        out_shape=shape((plan.rows, plan.width), LOW),
        compiler_params=params(60),
        cost_estimate=about(6),
        name="add_residual",
    )(*middles, part)


class State:
    pass


def body(mesh, tokens, w_query, w_key, w_value, w_out, w_gate, w_up, w_down, cotangent, slot_parent):
    plan = Plan(mesh, tokens.shape[0], tokens.shape[1], w_query.shape[1] // HEAD, w_gate.shape[1])
    me = lax.axis_index("dp")
    z = lax.axis_index("tensor")
    place = jnp.stack([me, z] + [me ^ relative for relative in kept_order(plan)]).astype(jnp.int32)
    cosine, sine = (jnp.asarray(table) for table in rope_tables())
    n = plan.spread
    wide = n * HEAD

    def swap(array, mask):
        return lax.ppermute(array, "dp", xor_pairs(plan.dp, mask))

    def exchange(parts):
        return [parts[0]] + [swap(parts[d], d * plan.rest) for d in range(1, n)]

    half = w_out.shape[0] // 2
    mine = lax.dynamic_slice_in_dim(w_out, (me % 2) * half, half, 0)
    near = lax.all_gather(mine, "tensor", axis=0, tiled=False)

    normed_one, *sends = project_qkv(
        plan, slot_parent, place, tokens, w_query, w_key, w_value, cosine, sine
    )
    chain = Chain(normed_one)
    parts = exchange(sends)
    seed = chain.run(lambda cot: grad_hidden_of(cot, w_down), cotangent)
    parts = chain.wait(*parts)
    kv = jnp.stack([part[1:] for part in parts])[None]
    mask = 1
    while mask < plan.rest:
        kv = jnp.concatenate([kv, swap(kv, mask)], axis=0)
        mask *= 2
    kv = chain.wait(kv.reshape(plan.dp * 2 * plan.slots, BLOCK, HEAD))
    attended_parts = exchange(chain.run(lambda *p: attend(plan, slot_parent, place, p, kv), *parts))
    attended = chain.run(lambda *p: gather_heads(plan, place, p), *attended_parts)
    everyone = [
        lax.all_gather(tie(part, near), "tensor", axis=0, tiled=False) for part in attended
    ]
    near = chain.after(near)
    far = swap(near, 1)

    middles, normed_two, hidden, grad_gate_proj, grad_up_proj, grad_normed_two = ([] for _ in range(6))
    for group in range(plan.groups):
        middle, normed = chain.run(
            lambda e, f: project_out(plan, place, group, tokens, e, near, f), everyone[group], far
        )
        partial_two, *rest = chain.run(
            lambda v: feed_forward(plan, place, group, v, seed, w_gate, w_up), normed
        )
        grad_normed_two.append(
            lax.psum_scatter(partial_two, "tensor", scatter_dimension=0, tiled=True)
        )
        middles.append(middle)
        normed_two.append(normed)
        for held, value in zip((hidden, grad_gate_proj, grad_up_proj), rest):
            held.append(value)
    state = State()
    down = WeightGradient(plan, place, chain, [cotangent], hidden, turned=True)
    gate = WeightGradient(plan, place, chain, normed_two, grad_gate_proj)
    up = WeightGradient(plan, place, chain, normed_two, grad_up_proj)
    out = WeightGradient(plan, place, chain, None, None, chunks=True)
    qkv = WeightGradient(plan, place, chain, None, None, split=True)

    def own():
        state.own = jnp.concatenate(
            [
                lax.dynamic_slice_in_dim(part, z * plan.share, plan.share, 1)
                .transpose(1, 0, 2)
                .reshape(plan.share, plan.width)
                for part in map(chain.after, everyone)
            ]
        )

    def branch():
        grad_middle, grad_branch, *chunks = chain.run(
            lambda *g: branch_back(plan, place, g, middles, cotangent, near, far),
            *grad_normed_two,
        )
        state.sources = [chunks[0]] + [
            shifted(plan, chunks[shift], shift) for shift in range(1, plan.tensor)
        ]
        state.grad_middle = grad_middle
        out.lhs, out.rhs = [grad_branch], [state.own]

    def output():
        branch_out = chain.run(lambda *h: project_down(plan, h, w_down), *hidden)
        state.part = lax.psum(branch_out, "tensor")

    def scatter():
        scattered = chain.run(lambda *p: scatter_heads(plan, place, p), *state.sources)
        state.grads = exchange(scattered)

    def heads():
        state.grads = chain.wait(*state.grads)

    def attend_step():
        *state.queries, state.near, state.far = chain.run(
            lambda *g: attend_back(plan, slot_parent, place, parts, kv, g), *state.grads
        )

    def sum_far():
        far_part = chain.after(state.far).reshape(plan.rest - 1, -1, BLOCK, HEAD)
        mask = plan.rest // 2
        while mask > 1:
            got = swap(far_part[mask - 1 : 2 * mask - 1], mask).astype(F32)
            state.near = state.near + got[0]
            far_part = (far_part[: mask - 1].astype(F32) + got[1:]).astype(LOW)
            mask //= 2
        state.got = swap(far_part.reshape(state.near.shape), 1)

    def sum_near():
        backs = chain.run(
            lambda g: combine_back(plan, state.queries, state.near, g), state.got
        )
        state.backs = exchange(backs)

    def arrive():
        state.backs = chain.wait(*state.backs)

    def turn():
        partial_one, turned = chain.run(
            lambda *p: turn_back(
                plan, slot_parent, place, cosine, sine, (w_query, w_key, w_value), p
            ),
            *state.backs,
        )
        state.one = lax.psum_scatter(partial_one, "tensor", scatter_dimension=0, tiled=True)
        qkv.lhs, qkv.rhs = [normed_one], [turned]

    def residual():
        state.output = chain.run(lambda p: add_residual(plan, middles, p), state.part)

    def tokens_step():
        grad_own = chain.run(
            lambda g: tokens_back(plan, place, g, tokens, state.grad_middle), state.one
        )
        state.tokens = lax.all_gather(grad_own, "tensor", axis=0, tiled=True)

    def gathered():
        state.tokens = chain.wait(state.tokens)

    def ring_start():
        state.ring = RingSum(plan, chain, chain.after(*state.out))

    def ring_end():
        got, mine = chain.wait(*state.ring.finish())
        state.out = chain.run(add_last, got, mine)

    def ring_step():
        state.ring.step()

    down.away()
    gate.away()
    Chain.weight = 0.3
    down.keep()
    Chain.weight = 1.0
    down.send()
    output()
    own()
    branch()
    scatter()
    out.away()
    gate.keep()
    out.keep()
    down.wait()
    heads()
    out.send()
    attend_step()
    out.wait()
    sum_far()
    out.add()
    sum_near()
    gate.send()
    down.add()
    up.away()
    arrive()
    turn()
    up.took()
    out.send()
    qkv.away()
    up.keep()
    Chain.weight = 0.3
    up.send()
    Chain.weight = 1.0
    gate.wait()
    state.out = out.finish()
    gate.add()
    qkv.keep()
    residual()
    ring_start()
    down.send()
    gate.send()
    up.wait()
    tokens_step()
    state.ring.step()
    qkv.send()
    down.wait()
    up.add()
    gate.wait()
    state.ring.step()
    state.down = down.finish()
    up.send()
    state.gate = gate.finish()
    qkv.wait()
    qkv.add()
    qkv.send()
    state.up = up.finish()
    ring_end()
    state.qkv = qkv.finish()
    grad_tokens = (
        state.tokens
        .reshape(plan.tensor, plan.groups, plan.share, plan.width)
        .transpose(1, 0, 2, 3)
        .reshape(plan.rows, plan.width)
    )
    return (
        state.output,
        grad_tokens,
        *state.qkv,
        state.out,
        state.gate,
        state.up,
        state.down,
    )


def solution(mesh):
    in_specs = (
        P("dp", None),
        P(None, "tensor"),
        P(None, "tensor"),
        P(None, "tensor"),
        P("tensor", None),
        P(None, "tensor"),
        P(None, "tensor"),
        P("tensor", None),
        P("dp", None),
        P(),
    )
    out_specs = (
        P("dp", None),
        P("dp", None),
        P("dp", "tensor"),
        P("dp", "tensor"),
        P("dp", "tensor"),
        P("tensor", "dp"),
        P("dp", "tensor"),
        P("dp", "tensor"),
        P("tensor", "dp"),
    )
    return jax.shard_map(
        functools.partial(body, mesh),
        mesh=mesh,
        in_specs=in_specs,
        out_specs=out_specs,
        check_vma=False,
    )
```

```python
import functools
import math

import jax
import jax.numpy as jnp
import numpy as np
from jax import lax
from jax.experimental import pallas as pl
from jax.experimental.pallas import tpu as pltpu
from jax.sharding import PartitionSpec as P

HEAD = 128
BLOCK = 128
TRUNK_BLOCKS = 8
CHAIN = TRUNK_BLOCKS + 2
EPSILON = 1e-05
NEGATIVE = -1e30
SCALE = HEAD ** (-0.5)
LOW = jnp.bfloat16
F32 = jnp.float32
MIB = 1024 * 1024
PER_MICROSECOND = 1.0e+11

NT = (((1,), (1,)), ((), ()))
TN = (((0,), (0,)), ((), ()))


def dot(a, b):
    return jnp.dot(a, b, preferred_element_type=F32)


def dot_nt(a, b):
    return lax.dot_general(a, b, NT, preferred_element_type=F32)


def dot_tn(a, b):
    return lax.dot_general(a, b, TN, preferred_element_type=F32)


def shape(dims, dtype):
    return jax.ShapeDtypeStruct(dims, dtype)


def about(microseconds):
    return pl.CostEstimate(
        flops=int(microseconds * PER_MICROSECOND * Chain.weight), bytes_accessed=1, transcendentals=0
    )


def params(mib):
    return pltpu.CompilerParams(vmem_limit_bytes=mib * MIB)


def layer_norm(values):
    centered = values - jnp.mean(values, axis=-1, keepdims=True)
    variance = jnp.mean(centered * centered, axis=-1, keepdims=True)
    inverse = lax.rsqrt(variance + EPSILON)
    return (centered * inverse, inverse)


def norm_back(gradient, normed, inverse):
    return inverse * (
        gradient
        - jnp.mean(gradient, axis=-1, keepdims=True)
        - normed * jnp.mean(gradient * normed, axis=-1, keepdims=True)
    )


def rope_tables():
    frequency = np.exp(
        np.arange(HEAD // 2, dtype=np.float32) * np.float32(-2.0 * math.log(10000.0) / HEAD)
    ).astype(np.float32)
    angle = np.arange(CHAIN * BLOCK, dtype=np.float32)[:, None] * frequency[None, :]
    cosine, sine = np.cos(angle), np.sin(angle)
    return (
        np.concatenate([cosine, cosine], axis=1).astype(np.float32),
        np.concatenate([-sine, sine], axis=1).astype(np.float32),
    )


def depth_of(parent_ref, slot):
    def up(_, carry):
        at, depth = carry
        parent = jnp.where(at >= 0, parent_ref[jnp.maximum(at, 0)], -1)
        return parent, depth + jnp.where(parent >= 0, 1, 0).astype(jnp.int32)

    return lax.fori_loop(0, CHAIN - 1, up, (slot, jnp.int32(0)))[1]


def xor_pairs(count, mask):
    return [(index, index ^ mask) for index in range(count)]


class Plan:
    def __init__(self, mesh, rows, width, heads, ff):
        self.dp = mesh.shape["dp"]
        self.tensor = mesh.shape["tensor"]
        self.rows, self.width, self.heads, self.ff = rows, width, heads, ff
        self.slots = rows // BLOCK
        self.spread = heads
        self.rest = self.dp // heads
        self.bits = self.dp.bit_length() - 1
        self.piece = width // self.dp
        self.own = rows // self.tensor
        self.groups = 2 if self.own % 32 == 0 else 1
        self.part = rows // self.groups
        self.share = self.own // self.groups

    def own_rows(self, group):
        return pl.BlockSpec(
            (self.share, self.width), lambda i, place: (group * self.tensor + place[1], 0)
        )

    def own_part(self):
        return pl.BlockSpec((self.share, self.width), lambda i, place: (place[1], 0))


def fetch(weights, held, sems, kind):
    copies = [
        pltpu.make_async_copy(w, held.at[index], sems.at[index]) for index, w in enumerate(weights)
    ]

    @pl.when(kind == 0)
    def _():
        for copy in copies:
            copy.start()

    def wait():
        for index, copy in enumerate(copies):

            @pl.when(kind == index)
            def _():
                copy.wait()

    return wait


def qkv_kernel(plan, parent, place, x, wq, wk, wv, cosine, sine, normed, *rest):
    outs, stage = rest[: plan.spread], rest[-1]
    me = place[0]
    part = me // plan.rest
    depth = depth_of(parent, me * plan.slots + pl.program_id(0))
    rows = pl.ds(pl.multiple_of(depth * BLOCK, BLOCK), BLOCK)
    cos, sin = cosine[rows, :], sine[rows, :]
    low = layer_norm(x[...].astype(F32))[0].astype(LOW)
    normed[...] = low
    for kind, w in enumerate((wq, wk, wv)):
        y = dot(low, w[...])
        for head in range(plan.heads):
            yh = y[:, head * HEAD : (head + 1) * HEAD]
            if kind < 2:
                yh = yh * cos + pltpu.roll(yh, HEAD // 2, 1) * sin
            stage[head, kind] = yh.astype(LOW)
    for d in range(plan.spread):
        outs[d][...] = stage[part ^ d]


def kept_order(plan):
    return [
        sum(((at >> bit) & 1) << (plan.bits - 1 - bit) for bit in range(plan.bits - 1))
        for at in range(plan.dp // 2)
    ]


def project_qkv(plan, slot_parent, place, tokens, wq, wk, wv, cosine, sine):
    whole = lambda i, *_: (0, 0)
    once = pl.Buffered(buffer_count=1)
    wide = plan.heads * HEAD
    return pl.pallas_call(
        functools.partial(qkv_kernel, plan),
        grid_spec=pltpu.PrefetchScalarGridSpec(
            num_scalar_prefetch=2,
            grid=(plan.slots,),
            in_specs=[pl.BlockSpec((BLOCK, plan.width), lambda i, *_: (i, 0))]
            + [pl.BlockSpec((plan.width, wide), whole, pipeline_mode=once)] * 3
            + [pl.BlockSpec((CHAIN * BLOCK, HEAD), whole, pipeline_mode=once)] * 2,
            out_specs=[pl.BlockSpec((BLOCK, plan.width), lambda i, *_: (i, 0))]
            + [pl.BlockSpec((3, BLOCK, HEAD), lambda i, *_: (0, i, 0))] * plan.spread,
            scratch_shapes=[
                pltpu.VMEM((plan.heads, 3, BLOCK, HEAD), LOW),
            ],
        ),
        out_shape=[shape((plan.rows, plan.width), LOW)]
        + [shape((3, plan.rows, HEAD), LOW)] * plan.spread,
        compiler_params=params(60),
        cost_estimate=about(0),
        name="project_qkv",
    )(slot_parent, place, tokens, wq, wk, wv, cosine, sine)


def gather_chain(plan, parent, me, slot, kv, keys, values):
    count = jnp.int32(0)
    at = slot
    places = []
    for step in range(CHAIN):
        here = jnp.maximum(at, 0)
        relative = (here // plan.slots) ^ me
        block = (
            (relative % plan.rest) * plan.spread + relative // plan.rest
        ) * 2 * plan.slots + here % plan.slots
        keys[step * BLOCK : (step + 1) * BLOCK, :] = kv[block]
        values[step * BLOCK : (step + 1) * BLOCK, :] = kv[block + plan.slots]
        places.append(block)
        valid = at >= 0
        count = count + jnp.where(valid, 1, 0).astype(jnp.int32)
        at = jnp.where(valid, parent[here], -1)
    return count, places


def chain_weights(queries, keys, counts):
    scores = [dot_nt(k, q) * SCALE for q, k in zip(queries, keys)]
    key_at = lax.broadcasted_iota(jnp.int32, scores[0].shape, 0)
    query_at = lax.broadcasted_iota(jnp.int32, scores[0].shape, 1)
    own = (key_at >= BLOCK) | (key_at <= query_at)
    probs = []
    for score, count in zip(scores, counts):
        score = jnp.where(own & (key_at < count * BLOCK), score, NEGATIVE)
        raised = jnp.exp(score - jnp.max(score, axis=0, keepdims=True))
        probs.append(raised * (1.0 / jnp.sum(raised, axis=0, keepdims=True)))
    return probs


def attend_kernel(plan, parent, place, *refs):
    n = plan.spread
    q_refs, kv, o_refs, keys, values = refs[:n], refs[n], refs[n + 1 : 2 * n + 1], refs[-2], refs[-1]
    me = place[0]

    def one(i, carry):
        rows = pl.ds(pl.multiple_of(i * BLOCK, BLOCK), BLOCK)
        slots = [(me ^ (d * plan.rest)) * plan.slots + i for d in range(n)]
        counts = [
            gather_chain(plan, parent, me, slots[d], kv, keys.at[d], values.at[d])[0]
            for d in range(n)
        ]
        queries = [q_refs[d][0, rows, :] for d in range(n)]
        probs = chain_weights(queries, [keys[d] for d in range(n)], counts)
        for d in range(n):
            o_refs[d][rows, :] = dot_tn(probs[d].astype(LOW), values[d]).astype(LOW)
        return carry

    lax.fori_loop(0, plan.slots, one, 0)


def attend(plan, slot_parent, place, parts, kv):
    n = plan.spread
    blocks = plan.dp * 2 * plan.slots
    return pl.pallas_call(
        functools.partial(attend_kernel, plan),
        grid_spec=pltpu.PrefetchScalarGridSpec(
            num_scalar_prefetch=2,
            grid=(1,),
            in_specs=[pl.BlockSpec((1, plan.rows, HEAD), lambda i, *_: (0, 0, 0))] * n
            + [pl.BlockSpec((blocks, BLOCK, HEAD), lambda i, *_: (0, 0, 0))],
            out_specs=[pl.BlockSpec((plan.rows, HEAD), lambda i, *_: (0, 0))] * n,
            scratch_shapes=[pltpu.VMEM((n, CHAIN * BLOCK, HEAD), LOW)] * 2,
        ),
        out_shape=[shape((plan.rows, HEAD), LOW)] * n,
        compiler_params=params(60),
        cost_estimate=about(0),
        name="attend",
    )(slot_parent, place, *parts, kv)


def attend_back_kernel(plan, parent, place, *refs):
    n = plan.spread
    q_refs, kv, g_refs = refs[:n], refs[n], refs[n + 1 : 2 * n + 1]
    dq_refs = refs[2 * n + 1 : 3 * n + 1]
    near, far, keys, values, total = refs[3 * n + 1 :]
    me = place[0]
    total[...] = jnp.zeros_like(total)

    def one(i, carry):
        rows = pl.ds(pl.multiple_of(i * BLOCK, BLOCK), BLOCK)
        slots = [(me ^ (d * plan.rest)) * plan.slots + i for d in range(n)]
        chains = [
            gather_chain(plan, parent, me, slots[d], kv, keys.at[d], values.at[d])
            for d in range(n)
        ]
        queries = [q_refs[d][0, rows, :] for d in range(n)]
        grads = [g_refs[d][rows, :] for d in range(n)]
        probs = chain_weights(queries, [keys[d] for d in range(n)], [chain[0] for chain in chains])
        for d in range(n):
            grad_prob = dot_nt(values[d], grads[d])
            inner = jnp.sum(grad_prob * probs[d], axis=0, keepdims=True)
            grad_scores = (probs[d] * (grad_prob - inner)).astype(LOW)
            dv = dot(probs[d].astype(LOW), grads[d])
            dk = dot(grad_scores, queries[d]) * SCALE
            dq_refs[d][rows, :] = (dot_tn(grad_scores, keys[d]) * SCALE).astype(LOW)
            for step, block in enumerate(chains[d][1]):
                span = slice(step * BLOCK, (step + 1) * BLOCK)
                total[block] = total[block] + dk[span]
                total[block + plan.slots] = total[block + plan.slots] + dv[span]
        return carry

    lax.fori_loop(0, plan.slots, one, 0)
    half = near.shape[0]
    near[...] = total[:half]
    far[...] = total[half:].astype(LOW)


def attend_back(plan, slot_parent, place, parts, kv, grads):
    n = plan.spread
    blocks = plan.dp * 2 * plan.slots
    near = n * 2 * plan.slots
    return pl.pallas_call(
        functools.partial(attend_back_kernel, plan),
        grid_spec=pltpu.PrefetchScalarGridSpec(
            num_scalar_prefetch=2,
            grid=(1,),
            in_specs=[pl.BlockSpec((1, plan.rows, HEAD), lambda i, *_: (0, 0, 0))] * n
            + [pl.BlockSpec((blocks, BLOCK, HEAD), lambda i, *_: (0, 0, 0))]
            + [pl.BlockSpec((plan.rows, HEAD), lambda i, *_: (0, 0))] * n,
            out_specs=[pl.BlockSpec((plan.rows, HEAD), lambda i, *_: (0, 0))] * n
            + [
                pl.BlockSpec((near, BLOCK, HEAD), lambda i, *_: (0, 0, 0)),
                pl.BlockSpec((blocks - near, BLOCK, HEAD), lambda i, *_: (0, 0, 0)),
            ],
            scratch_shapes=[pltpu.VMEM((n, CHAIN * BLOCK, HEAD), LOW)] * 2
            + [pltpu.VMEM((blocks, BLOCK, HEAD), F32)],
        ),
        out_shape=[shape((plan.rows, HEAD), LOW)] * n
        + [shape((near, BLOCK, HEAD), F32), shape((blocks - near, BLOCK, HEAD), LOW)],
        compiler_params=params(60),
        cost_estimate=about(23),
        name="attend_back",
    )(slot_parent, place, *parts, kv, *grads)


def combine_kernel(plan, *refs):
    n = plan.spread
    queries, (near, got), outs = refs[:n], refs[n : n + 2], refs[n + 2 :]
    for d in range(n):
        outs[d][0] = queries[d][...]
        for kind in range(2):
            for slot in range(plan.slots):
                block = (d * 2 + kind) * plan.slots + slot
                rows = slice(slot * BLOCK, (slot + 1) * BLOCK)
                total = near[block] + got[block].astype(F32)
                outs[d][kind + 1, rows, :] = total.astype(LOW)


def combine_back(plan, queries, near, got):
    n = plan.spread
    return pl.pallas_call(
        functools.partial(combine_kernel, plan),
        out_shape=[shape((3, plan.rows, HEAD), LOW)] * n,
        compiler_params=params(60),
        cost_estimate=about(3),
        name="combine_back",
    )(*queries, near, got)


def heads_kernel(plan, place, *refs):
    part = place[0] // plan.rest
    outs = refs[plan.spread :]
    for d in range(plan.spread):
        head = pl.ds(pl.multiple_of((part ^ d) * HEAD, HEAD), HEAD)
        for group, out in enumerate(outs):
            out[:, head] = refs[d][group * plan.part : (group + 1) * plan.part, :]


def gather_heads(plan, place, parts):
    wide = plan.heads * HEAD
    return pl.pallas_call(
        functools.partial(heads_kernel, plan),
        grid_spec=pltpu.PrefetchScalarGridSpec(
            num_scalar_prefetch=1,
            grid=(1,),
            in_specs=[pl.BlockSpec((plan.rows, HEAD), lambda i, *_: (0, 0))] * plan.spread,
            out_specs=[pl.BlockSpec((plan.part, wide), lambda i, *_: (0, 0))] * plan.groups,
        ),
        out_shape=[shape((plan.part, wide), LOW)] * plan.groups,
        compiler_params=params(60),
        cost_estimate=about(0),
        name="gather_heads",
    )(place, *parts)


def scatter_kernel(plan, place, *refs):
    part, z = place[0] // plan.rest, place[1]
    sources, outs = refs[: plan.tensor], refs[plan.tensor :]
    for shift in range(plan.tensor):
        origin = lax.rem(z - shift + plan.tensor, plan.tensor)
        for group in range(plan.groups):
            start = group * plan.part + origin * plan.share
            rows = pl.ds(pl.multiple_of(start, 16), plan.share)
            share = slice(group * plan.share, (group + 1) * plan.share)
            for d in range(plan.spread):
                head = pl.ds(pl.multiple_of((part ^ d) * HEAD, HEAD), HEAD)
                outs[d][rows, :] = sources[shift][share, head]


def scatter_heads(plan, place, sources):
    return pl.pallas_call(
        functools.partial(scatter_kernel, plan),
        grid_spec=pltpu.PrefetchScalarGridSpec(
            num_scalar_prefetch=1,
            grid=(1,),
            in_specs=[pl.BlockSpec((plan.own, plan.heads * HEAD), lambda i, *_: (0, 0))]
            * plan.tensor,
            out_specs=[pl.BlockSpec((plan.rows, HEAD), lambda i, *_: (0, 0))] * plan.spread,
        ),
        out_shape=[shape((plan.rows, HEAD), LOW)] * plan.spread,
        name="scatter_heads",
    )(place, *sources)


def turn_back_kernel(plan, parent, place, cosine, sine, wq, wk, wv, *refs):
    parts, (back, out, product) = refs[: plan.spread], refs[plan.spread :]
    me = place[0]
    part = me // plan.rest
    wide = plan.heads * HEAD

    @pl.when(pl.program_id(0) == 0)
    def _():
        for slot in range(plan.slots):
            depth = depth_of(parent, me * plan.slots + slot)
            table = pl.ds(pl.multiple_of(depth * BLOCK, BLOCK), BLOCK)
            cos, sin = cosine[table, :], sine[table, :]
            rows = slice(slot * BLOCK, (slot + 1) * BLOCK)
            for d in range(plan.spread):
                for kind in range(3):
                    value = parts[d][kind, rows, :]
                    if kind < 2:
                        value = value.astype(F32)
                        value = value * cos - pltpu.roll(value, HEAD // 2, 1) * sin
                    at = pl.multiple_of((kind * plan.heads + (part ^ d)) * HEAD, HEAD)
                    out[rows, pl.ds(at, HEAD)] = value.astype(LOW)

    total = 0.0
    for kind, w in enumerate((wq, wk, wv)):
        total = total + dot_nt(out[:, kind * wide : (kind + 1) * wide], w[...])
    product[...] = total
    for device in range(plan.tensor):
        for group in range(plan.groups):
            source = (group * plan.tensor + device) * plan.share
            target = (device * plan.groups + group) * plan.share
            back[target : target + plan.share, :] = product[
                source : source + plan.share, :
            ].astype(LOW)


def turn_back(plan, slot_parent, place, cosine, sine, weights, parts):
    whole = lambda i, *_: (0, 0)
    wide = plan.heads * HEAD
    tile = min(512, plan.width)
    return pl.pallas_call(
        functools.partial(turn_back_kernel, plan),
        grid_spec=pltpu.PrefetchScalarGridSpec(
            num_scalar_prefetch=2,
            grid=(plan.width // tile,),
            in_specs=[pl.BlockSpec((CHAIN * BLOCK, HEAD), whole)] * 2
            + [pl.BlockSpec((tile, wide), lambda i, *_: (i, 0))] * 3
            + [pl.BlockSpec((3, plan.rows, HEAD), lambda i, *_: (0, 0, 0))] * plan.spread,
            out_specs=[
                pl.BlockSpec((plan.rows, tile), lambda i, *_: (0, i)),
                pl.BlockSpec((plan.rows, 3 * wide), whole),
            ],
            scratch_shapes=[pltpu.VMEM((plan.rows, tile), F32)],
        ),
        out_shape=[shape((plan.rows, plan.width), LOW), shape((plan.rows, 3 * wide), LOW)],
        compiler_params=params(60),
        cost_estimate=about(13),
        name="turn_back",
    )(slot_parent, place, cosine, sine, *weights, *parts)


def out_kernel(plan, place, x, att, near, far, middle, normed):
    half = plan.heads * HEAD // 2
    core = place[0] % 2
    total = x[...].astype(F32)
    for z in range(plan.tensor):
        for side, w in ((core, near), (1 - core, far)):
            columns = pl.ds(pl.multiple_of(side * half, half), half)
            total = total + dot(att[z, :, columns], w[z])
    middle[...] = total
    normed[...] = layer_norm(total)[0].astype(LOW)


def project_out(plan, place, group, tokens, att, near, far):
    half = plan.heads * HEAD // 2
    count = 2
    rows = plan.part // count
    weights = pl.BlockSpec(
        (plan.tensor, half, plan.width),
        lambda i, *_: (0, 0, 0),
        pipeline_mode=pl.Buffered(buffer_count=1),
    )
    out = pl.BlockSpec((rows, plan.width), lambda i, *_: (i, 0))
    return pl.pallas_call(
        functools.partial(out_kernel, plan),
        grid_spec=pltpu.PrefetchScalarGridSpec(
            num_scalar_prefetch=1,
            grid=(count,),
            in_specs=[
                pl.BlockSpec((rows, plan.width), lambda i, *_: (group * count + i, 0)),
                pl.BlockSpec((plan.tensor, rows, 2 * half), lambda i, *_: (0, i, 0)),
                weights,
                weights,
            ],
            out_specs=[out, out],
        ),
        out_shape=[shape((plan.part, plan.width), F32), shape((plan.part, plan.width), LOW)],
        compiler_params=params(60),
        cost_estimate=about(7),
        name="project_out",
    )(place, tokens, att, near, far)


def grad_hidden_kernel(cot, wd, out):
    out[...] = dot_nt(cot[...], wd[...])


def grad_hidden_of(cot, wd):
    rows, width = cot.shape
    ff = wd.shape[0]
    tile = min(512, ff)
    return pl.pallas_call(
        grad_hidden_kernel,
        grid=(ff // tile,),
        in_specs=[
            pl.BlockSpec((rows, width), lambda i: (0, 0)),
            pl.BlockSpec((tile, width), lambda i: (i, 0)),
        ],
        out_specs=pl.BlockSpec((rows, tile), lambda i: (0, i)),
        out_shape=shape((rows, ff), F32),
        compiler_params=params(60),
        cost_estimate=about(0),
        name="grad_hidden",
    )(cot, wd)


def ff_kernel(tile, normed, seed, wg, wu, back, hidden, grad_gate, grad_up, *scratch):
    gate_held, up_held, results, total, in_sems, out_sems = scratch
    count = wg.shape[1] // tile
    spans = [slice(index * tile, (index + 1) * tile) for index in range(count)]
    arrivals = [
        [
            pltpu.make_async_copy(w.at[:, span], held.at[:, span], in_sems.at[which, index])
            for which, (w, held) in enumerate(((wg, gate_held), (wu, up_held)))
        ]
        for index, span in enumerate(spans)
    ]
    departures = [
        [
            pltpu.make_async_copy(
                results.at[which, :, span], out.at[:, span], out_sems.at[which, index]
            )
            for which, out in enumerate((hidden, grad_gate, grad_up))
        ]
        for index, span in enumerate(spans)
    ]
    for pair in arrivals:
        for copy in pair:
            copy.start()
    for index, span in enumerate(spans):
        for copy in arrivals[index]:
            copy.wait()
        gate = dot(normed[...], gate_held[:, span])
        up = dot(normed[...], up_held[:, span])
        grad_hidden = seed[:, span]
        s = 1.0 / (1.0 + jnp.exp(-gate))
        active = gate * s
        gu = (grad_hidden * active).astype(LOW)
        gg = (grad_hidden * up * s * (1.0 + gate * (1.0 - s))).astype(LOW)
        results[0, :, span] = (active * up).astype(LOW)
        results[1, :, span] = gg
        results[2, :, span] = gu
        for copy in departures[index]:
            copy.start()
        part = dot_nt(gg, gate_held[:, span]) + dot_nt(gu, up_held[:, span])
        if index == 0:
            total[...] = part
        elif index < count - 1:
            total[...] += part
        else:
            back[...] = (total[...] + part).astype(LOW)
    for triple in departures:
        for copy in triple:
            copy.wait()


def feed_forward(plan, place, group, normed, seed, wg, wu):
    rows, width = normed.shape
    ff = wg.shape[1]
    tile = min(512, ff // 2)
    whole = pl.BlockSpec((rows, width), lambda i: (0, 0))
    anywhere = pl.BlockSpec(memory_space=pl.ANY)
    return pl.pallas_call(
        functools.partial(ff_kernel, tile),
        grid=(1,),
        in_specs=[whole, pl.BlockSpec((rows, ff), lambda i: (group, 0)), anywhere, anywhere],
        out_specs=[whole, anywhere, anywhere, anywhere],
        out_shape=[shape((rows, width), LOW)] + [shape((rows, ff), LOW)] * 3,
        scratch_shapes=[
            pltpu.VMEM((width, ff), LOW),
            pltpu.VMEM((width, ff), LOW),
            pltpu.VMEM((3, rows, ff), LOW),
            pltpu.VMEM((rows, width), F32),
            pltpu.SemaphoreType.DMA((2, ff // tile)),
            pltpu.SemaphoreType.DMA((3, ff // tile)),
        ],
        compiler_params=params(62),
        cost_estimate=about(17),
        name="feed_forward",
    )(normed, seed, wg, wu)


def down_kernel(plan, *refs):
    hiddens, (w, out) = refs[: plan.groups], refs[plan.groups :]
    for group, hidden in enumerate(hiddens):
        rows = slice(group * plan.part, (group + 1) * plan.part)
        out[rows, :] = dot(hidden[...], w[...]).astype(LOW)


def project_down(plan, hiddens, w):
    ff, width = w.shape
    tile = min(512, width)
    return pl.pallas_call(
        functools.partial(down_kernel, plan),
        grid=(width // tile,),
        in_specs=[pl.BlockSpec((plan.part, ff), lambda i: (0, 0))] * plan.groups
        + [pl.BlockSpec((ff, tile), lambda i: (0, i))],
        out_specs=pl.BlockSpec((plan.rows, tile), lambda i: (0, i)),
        out_shape=shape((plan.rows, width), LOW),
        compiler_params=params(60),
        cost_estimate=about(11),
        name="project_down",
    )(*hiddens, w)


def branch_back_kernel(plan, place, *refs):
    count = plan.groups
    parts, middles, cots = refs[:count], refs[count : 2 * count], refs[2 * count : 3 * count]
    near, far, grad_middle, low = refs[3 * count : 3 * count + 4]
    outs, (near_held, far_held, sems) = refs[3 * count + 4 : -3], refs[-3:]
    core, z = place[0] % 2, place[1]
    half = plan.heads * HEAD // 2
    sides = ((core, near, near_held), (1 - core, far, far_held))
    copies = [
        [
            pltpu.make_async_copy(
                w.at[lax.rem(z + shift, plan.tensor)], held.at[shift], sems.at[index, shift]
            )
            for index, (_, w, held) in enumerate(sides)
        ]
        for shift in range(plan.tensor)
    ]
    for pair in copies:
        for copy in pair:
            copy.start()
    for group in range(count):
        rows = slice(group * plan.share, (group + 1) * plan.share)
        normed, inverse = layer_norm(middles[group][...])
        back = norm_back(parts[group][...].astype(F32), normed, inverse)
        grad = cots[group][...].astype(F32) + back
        grad_middle[rows, :] = grad
        low[rows, :] = grad.astype(LOW)
    for shift in range(plan.tensor):
        for copy, (side, _, held) in zip(copies[shift], sides):
            copy.wait()
            columns = pl.ds(pl.multiple_of(side * half, half), half)
            outs[shift][:, columns] = dot_nt(low[...], held[shift]).astype(LOW)


def branch_back(plan, place, parts, middles, cot, near, far):
    half = plan.heads * HEAD // 2
    own = pl.BlockSpec((plan.own, plan.width), lambda i, *_: (0, 0))
    share = pl.BlockSpec((plan.share, plan.width), lambda i, *_: (0, 0))
    anywhere = pl.BlockSpec(memory_space=pl.ANY)
    return pl.pallas_call(
        functools.partial(branch_back_kernel, plan),
        grid_spec=pltpu.PrefetchScalarGridSpec(
            num_scalar_prefetch=1,
            grid=(1,),
            in_specs=[share] * plan.groups
            + [plan.own_part()] * plan.groups
            + [plan.own_rows(group) for group in range(plan.groups)]
            + [anywhere, anywhere],
            out_specs=[own, own]
            + [pl.BlockSpec((plan.own, 2 * half), lambda i, *_: (0, 0))] * plan.tensor,
            scratch_shapes=[pltpu.VMEM((plan.tensor, half, plan.width), LOW)] * 2
            + [pltpu.SemaphoreType.DMA((2, plan.tensor))],
        ),
        out_shape=[shape((plan.own, plan.width), F32), shape((plan.own, plan.width), LOW)]
        + [shape((plan.own, 2 * half), LOW)] * plan.tensor,
        compiler_params=params(60),
        cost_estimate=about(9),
        name="branch_back",
    )(place, *parts, *middles, *([cot] * plan.groups), near, far)


def tokens_back_kernel(plan, place, part, *refs):
    tokens, (grad_middle, out) = refs[: plan.groups], refs[plan.groups :]
    for group in range(plan.groups):
        rows = slice(group * plan.share, (group + 1) * plan.share)
        normed, inverse = layer_norm(tokens[group][...].astype(F32))
        back = norm_back(part[rows, :].astype(F32), normed, inverse)
        out[rows, :] = (grad_middle[rows, :] + back).astype(LOW)


def tokens_back(plan, place, part, tokens, grad_middle):
    own = pl.BlockSpec((plan.own, plan.width), lambda i, *_: (0, 0))
    return pl.pallas_call(
        functools.partial(tokens_back_kernel, plan),
        grid_spec=pltpu.PrefetchScalarGridSpec(
            num_scalar_prefetch=1,
            grid=(1,),
            in_specs=[own] + [plan.own_rows(group) for group in range(plan.groups)] + [own],
            out_specs=own,
        ),
        out_shape=shape((plan.own, plan.width), LOW),
        compiler_params=params(60),
        cost_estimate=about(4),
        name="tokens_back",
    )(place, part, *([tokens] * plan.groups), grad_middle)


def products(lhs, rhs):
    total, start = 0.0, 0
    for index, right in enumerate(rhs):
        rows = right.shape[0]
        left = lhs[index][...] if len(lhs) > 1 else lhs[0][start : start + rows, :]
        total = total + dot_tn(left, right[...])
        start += rows
    return total


def away_kernel(count, place, *refs):
    lhs, rhs, out = refs[:count], refs[count:-1], refs[-1]
    out[...] = products(lhs, rhs).astype(LOW)


def wgrad_away(plan, place, lhs, rhs):
    columns = rhs[0].shape[1]
    piece, count = plan.piece, plan.dp // 2
    return pl.pallas_call(
        functools.partial(away_kernel, len(lhs)),
        grid_spec=pltpu.PrefetchScalarGridSpec(
            num_scalar_prefetch=1,
            grid=(count,),
            in_specs=[
                pl.BlockSpec((part.shape[0], piece), lambda i, place: (0, place[2 + i] ^ 1))
                for part in lhs
            ]
            + [pl.BlockSpec(part.shape, lambda i, *_: (0, 0)) for part in rhs],
            out_specs=pl.BlockSpec((piece, columns), lambda i, *_: (i, 0)),
        ),
        out_shape=shape((count * piece, columns), LOW),
        compiler_params=params(60),
        cost_estimate=about(8),
        name="wgrad_away",
    )(place, *lhs, *rhs)


def keep_kernel(arrays, count, place, *refs):
    lhs, rhs = refs[:arrays], refs[arrays:-5]
    recv, a_keep, a_send, b_keep, b_send = refs[-5:]
    step = pl.program_id(0)
    total = (products(lhs, rhs) + recv[...].astype(F32)).astype(LOW)
    half = total.shape[1] // 2

    @pl.when(step < count // 2)
    def _():
        a_keep[...] = total[:, :half]

    @pl.when(step >= count // 2)
    def _():
        a_send[...] = total[:, :half]

    @pl.when(step % 2 == 0)
    def _():
        b_keep[...] = total[:, half:]

    @pl.when(step % 2 == 1)
    def _():
        b_send[...] = total[:, half:]


def wgrad_keep(plan, place, lhs, rhs, recv):
    columns = rhs[0].shape[1]
    piece, count = plan.piece, plan.dp // 2
    half = count // 2
    block = lambda index: pl.BlockSpec((piece, columns // 2), index)
    return pl.pallas_call(
        functools.partial(keep_kernel, len(lhs), count),
        grid_spec=pltpu.PrefetchScalarGridSpec(
            num_scalar_prefetch=1,
            grid=(count,),
            in_specs=[
                pl.BlockSpec((part.shape[0], piece), lambda i, place: (0, place[2 + i]))
                for part in lhs
            ]
            + [pl.BlockSpec(part.shape, lambda i, *_: (0, 0)) for part in rhs]
            + [pl.BlockSpec((piece, columns), lambda i, *_: (i, 0))],
            out_specs=[
                block(lambda i, *_: (jnp.minimum(i, half - 1), 0)),
                block(lambda i, *_: (jnp.maximum(i - half, 0), 0)),
                block(lambda i, *_: (i // 2, 0)),
                block(lambda i, *_: (i // 2, 0)),
            ],
        ),
        out_shape=[shape((half * piece, columns // 2), LOW)] * 4,
        compiler_params=params(60),
        cost_estimate=about(9),
        name="wgrad_keep",
    )(place, *lhs, *rhs, recv)


def stage_kernel(piece, a, a_got, b, b_got, a_keep, a_send, b_keep, b_send):
    total = a[...].astype(F32) + a_got[...].astype(F32)
    half = total.shape[0] // 2
    a_keep[...] = total[:half].astype(LOW)
    a_send[...] = total[half:].astype(LOW)
    for at in range(0, 2 * half, 2 * piece):
        for start, out in ((at, b_keep), (at + piece, b_send)):
            rows = slice(start, start + piece)
            total = b[rows, :].astype(F32) + b_got[rows, :].astype(F32)
            out[at // 2 : at // 2 + piece, :] = total.astype(LOW)


def wgrad_stage(piece, *arrays):
    rows, columns = arrays[0].shape
    tile = columns // 2 if columns % 256 == 0 else columns
    block = lambda size: pl.BlockSpec((size, tile), lambda i: (0, i))
    return pl.pallas_call(
        functools.partial(stage_kernel, piece),
        grid=(columns // tile,),
        in_specs=[block(rows)] * 4,
        out_specs=[block(rows // 2)] * 4,
        out_shape=[shape((rows // 2, columns), LOW)] * 4,
        compiler_params=params(60),
        cost_estimate=about(3),
        name="wgrad_stage",
    )(*arrays)


def finish_kernel(turned, a, a_got, b, b_got, out):
    half = a.shape[1]
    for way, (keep, got) in enumerate(((a, a_got), (b, b_got))):
        total = keep[...].astype(F32) + got[...].astype(F32)
        span = slice(way * half, (way + 1) * half)
        if turned:
            out[span, :] = total.T
        else:
            out[:, span] = total


def wgrad_finish(turned, *arrays):
    piece, half = arrays[0].shape
    return pl.pallas_call(
        functools.partial(finish_kernel, turned),
        out_shape=shape((2 * half, piece) if turned else (piece, 2 * half), F32),
        compiler_params=params(60),
        cost_estimate=about(3),
        name="wgrad_finish",
    )(*arrays)


def split_kernel(*refs):
    arrays, outs, held = refs[:4], refs[4:-1], refs[-1]
    finish_kernel(False, *arrays, held)
    width = outs[0].shape[1]
    for index, out in enumerate(outs):
        out[...] = held[:, index * width : (index + 1) * width]


def wgrad_finish_split(*arrays):
    piece, half = arrays[0].shape
    return pl.pallas_call(
        split_kernel,
        out_shape=[shape((piece, 2 * half // 3), F32)] * 3,
        scratch_shapes=[pltpu.VMEM((piece, 2 * half), F32)],
        compiler_params=params(60),
        cost_estimate=about(3),
        name="wgrad_finish_split",
    )(*arrays)


def chunks_kernel(plan, place, *refs):
    arrays, chunks, held = refs[:4], refs[4:-1], refs[-1]
    finish_kernel(True, *arrays, held)
    rows = plan.heads * HEAD
    for index, chunk in enumerate(chunks):
        chunk[...] = held[ring_rows(plan, place, index, rows), :].astype(LOW)


def wgrad_finish_chunks(plan, place, *arrays):
    piece, half = arrays[0].shape
    rows = plan.heads * HEAD
    return pl.pallas_call(
        functools.partial(chunks_kernel, plan),
        grid_spec=pltpu.PrefetchScalarGridSpec(
            num_scalar_prefetch=1,
            grid=(1,),
            in_specs=[pl.BlockSpec((piece, half), lambda i, *_: (0, 0))] * 4,
            out_specs=[pl.BlockSpec((rows, piece), lambda i, *_: (0, 0))] * plan.tensor,
            scratch_shapes=[pltpu.VMEM((2 * half, piece), F32)],
        ),
        out_shape=[shape((rows, piece), LOW)] * plan.tensor,
        compiler_params=params(60),
        cost_estimate=about(4),
        name="wgrad_finish_chunks",
    )(place, *arrays)


def tie(values, *others):
    many = isinstance(values, (list, tuple))
    held = lax.optimization_barrier((tuple(values) if many else (values,)) + others)
    return list(held[: len(values)]) if many else held[0]


class WeightGradient:
    def __init__(self, plan, place, chain, lhs, rhs, turned=False, chunks=False, split=False):
        self.chunks, self.split = chunks, split
        self.plan, self.place, self.chain = plan, place, chain
        self.lhs, self.rhs, self.turned = lhs, rhs, turned
        self.stage = 0

    def swap(self, array, bit):
        return lax.ppermute(array, "dp", xor_pairs(self.plan.dp, 1 << bit))

    def away(self):
        sent = self.chain.run(
            lambda *r: wgrad_away(self.plan, self.place, self.lhs, r), *self.rhs
        )
        self.recv = self.swap(sent, 0)

    def keep(self):
        self.a_keep, self.a_send, self.b_keep, self.b_send = self.chain.run(
            lambda r: wgrad_keep(self.plan, self.place, self.lhs, self.rhs, r), self.recv
        )

    def send(self):
        upwards = list(range(1, self.plan.bits))
        a, b = self.chain.after(self.a_send, self.b_send)
        self.a_got = self.swap(a, upwards[self.stage])
        self.b_got = self.swap(b, upwards[-1 - self.stage])
        self.stage += 1

    def wait(self):
        self.a_got, self.b_got = self.chain.wait(self.a_got, self.b_got)

    def took(self):
        self.recv = self.chain.wait(self.recv)

    def add(self):
        self.a_keep, self.a_send, self.b_keep, self.b_send = self.chain.run(
            lambda *p: wgrad_stage(self.plan.piece, *p),
            self.a_keep,
            self.a_got,
            self.b_keep,
            self.b_got,
        )

    def finish(self):
        while self.stage < self.plan.bits - 1:
            self.add()
            self.send()
        return self.chain.run(
            lambda *p: (
                wgrad_finish_chunks(self.plan, self.place, *p)
                if self.chunks
                else wgrad_finish_split(*p)
                if self.split
                else wgrad_finish(self.turned, *p)
            ),
            self.a_keep,
            self.a_got,
            self.b_keep,
            self.b_got,
        )


class Chain:
    weight = 1.0

    def __init__(self, last):
        self.last = last

    def after(self, *values):
        held = lax.optimization_barrier(values + (self.last,))
        return held[0] if len(values) == 1 else list(held[:-1])

    def wait(self, *values):
        held = lax.optimization_barrier(values + (self.last,))
        self.last = held[0]
        return held[0] if len(values) == 1 else list(held[:-1])

    def run(self, step, *values):
        held = self.after(*values)
        out = step(*held) if len(values) > 1 else step(held)
        self.last = out[0] if isinstance(out, (list, tuple)) else out
        return out


def shifted(plan, array, shift):
    pairs = [(i, (i + shift) % plan.tensor) for i in range(plan.tensor)]
    return lax.ppermute(array, "tensor", pairs)


class RingSum:
    def __init__(self, plan, chain, chunks):
        self.plan, self.chain, self.chunks, self.at = plan, chain, chunks, 1
        self.moving = shifted(plan, chunks[0], 1)

    def step(self):
        if self.at < self.plan.tensor - 1:
            got, mine = self.chain.wait(self.moving, self.chunks[self.at])
            total = (got.astype(F32) + mine.astype(F32)).astype(LOW)
            self.chain.last = total
            self.moving = shifted(self.plan, total, 1)
            self.at += 1

    def finish(self):
        while self.at < self.plan.tensor - 1:
            self.step()
        return self.moving, self.chunks[-1]


def ring_rows(plan, place, step, rows):
    chunk = lax.rem(place[1] + (2 * plan.tensor - 1 - step), plan.tensor)
    return pl.ds(pl.multiple_of(chunk * rows, 16), rows)


def add_last_kernel(a, b, out):
    out[...] = a[...].astype(F32) + b[...].astype(F32)


def add_last(a, b):
    return pl.pallas_call(
        add_last_kernel,
        out_shape=shape(a.shape, F32),
        compiler_params=params(60),
        cost_estimate=about(2),
        name="add_last",
    )(a, b)


def add_kernel(plan, *refs):
    middles, (part, out) = refs[: plan.groups], refs[plan.groups :]
    step = pl.program_id(0)
    for group, middle in enumerate(middles):

        @pl.when(step // 2 == group)
        def _():
            out[...] = (middle[...] + part[...].astype(F32)).astype(LOW)


def add_residual(plan, middles, part):
    rows = plan.part // 2
    block = pl.BlockSpec((rows, plan.width), lambda i: (i, 0))
    return pl.pallas_call(
        functools.partial(add_kernel, plan),
        grid=(2 * plan.groups,),
        in_specs=[
            pl.BlockSpec(
                (rows, plan.width),
                lambda i, group=group: (jnp.clip(i - 2 * group, 0, 1), 0),
            )
            for group in range(plan.groups)
        ]
        + [block],
        out_specs=block,
        out_shape=shape((plan.rows, plan.width), LOW),
        compiler_params=params(60),
        cost_estimate=about(6),
        name="add_residual",
    )(*middles, part)


class State:
    pass


def body(mesh, tokens, w_query, w_key, w_value, w_out, w_gate, w_up, w_down, cotangent, slot_parent):
    plan = Plan(mesh, tokens.shape[0], tokens.shape[1], w_query.shape[1] // HEAD, w_gate.shape[1])
    me = lax.axis_index("dp")
    z = lax.axis_index("tensor")
    place = jnp.stack([me, z] + [me ^ relative for relative in kept_order(plan)]).astype(jnp.int32)
    cosine, sine = (jnp.asarray(table) for table in rope_tables())
    n = plan.spread
    wide = n * HEAD

    def swap(array, mask):
        return lax.ppermute(array, "dp", xor_pairs(plan.dp, mask))

    def exchange(parts):
        return [parts[0]] + [swap(parts[d], d * plan.rest) for d in range(1, n)]

    half = w_out.shape[0] // 2
    mine = lax.dynamic_slice_in_dim(w_out, (me % 2) * half, half, 0)
    near = lax.all_gather(mine, "tensor", axis=0, tiled=False)

    normed_one, *sends = project_qkv(
        plan, slot_parent, place, tokens, w_query, w_key, w_value, cosine, sine
    )
    chain = Chain(normed_one)
    parts = exchange(sends)
    seed = chain.run(lambda cot: grad_hidden_of(cot, w_down), cotangent)
    parts = chain.wait(*parts)
    kv = jnp.stack([part[1:] for part in parts])[None]
    mask = 1
    while mask < plan.rest:
        kv = jnp.concatenate([kv, swap(kv, mask)], axis=0)
        mask *= 2
    kv = chain.wait(kv.reshape(plan.dp * 2 * plan.slots, BLOCK, HEAD))
    attended_parts = exchange(chain.run(lambda *p: attend(plan, slot_parent, place, p, kv), *parts))
    attended = chain.run(lambda *p: gather_heads(plan, place, p), *attended_parts)
    everyone = [
        lax.all_gather(tie(part, near), "tensor", axis=0, tiled=False) for part in attended
    ]
    near = chain.after(near)
    far = swap(near, 1)

    middles, normed_two, hidden, grad_gate_proj, grad_up_proj, grad_normed_two = ([] for _ in range(6))
    for group in range(plan.groups):
        middle, normed = chain.run(
            lambda e, f: project_out(plan, place, group, tokens, e, near, f), everyone[group], far
        )
        partial_two, *rest = chain.run(
            lambda v: feed_forward(plan, place, group, v, seed, w_gate, w_up), normed
        )
        grad_normed_two.append(
            lax.psum_scatter(partial_two, "tensor", scatter_dimension=0, tiled=True)
        )
        middles.append(middle)
        normed_two.append(normed)
        for held, value in zip((hidden, grad_gate_proj, grad_up_proj), rest):
            held.append(value)
    state = State()
    down = WeightGradient(plan, place, chain, [cotangent], hidden, turned=True)
    gate = WeightGradient(plan, place, chain, normed_two, grad_gate_proj)
    up = WeightGradient(plan, place, chain, normed_two, grad_up_proj)
    out = WeightGradient(plan, place, chain, None, None, chunks=True)
    qkv = WeightGradient(plan, place, chain, None, None, split=True)

    def own():
        state.own = jnp.concatenate(
            [
                lax.dynamic_slice_in_dim(part, z * plan.share, plan.share, 1)
                .transpose(1, 0, 2)
                .reshape(plan.share, plan.width)
                for part in map(chain.after, everyone)
            ]
        )

    def branch():
        grad_middle, grad_branch, *chunks = chain.run(
            lambda *g: branch_back(plan, place, g, middles, cotangent, near, far),
            *grad_normed_two,
        )
        state.sources = [chunks[0]] + [
            shifted(plan, chunks[shift], shift) for shift in range(1, plan.tensor)
        ]
        state.grad_middle = grad_middle
        out.lhs, out.rhs = [grad_branch], [state.own]

    def output():
        branch_out = chain.run(lambda *h: project_down(plan, h, w_down), *hidden)
        state.part = lax.psum(branch_out, "tensor")

    def scatter():
        scattered = chain.run(lambda *p: scatter_heads(plan, place, p), *state.sources)
        state.grads = exchange(scattered)

    def heads():
        state.grads = chain.wait(*state.grads)

    def attend_step():
        *state.queries, state.near, state.far = chain.run(
            lambda *g: attend_back(plan, slot_parent, place, parts, kv, g), *state.grads
        )

    def sum_far():
        far_part = chain.after(state.far).reshape(plan.rest - 1, -1, BLOCK, HEAD)
        mask = plan.rest // 2
        while mask > 1:
            got = swap(far_part[mask - 1 : 2 * mask - 1], mask).astype(F32)
            state.near = state.near + got[0]
            far_part = (far_part[: mask - 1].astype(F32) + got[1:]).astype(LOW)
            mask //= 2
        state.got = swap(far_part.reshape(state.near.shape), 1)

    def sum_near():
        backs = chain.run(
            lambda g: combine_back(plan, state.queries, state.near, g), state.got
        )
        state.backs = exchange(backs)

    def arrive():
        state.backs = chain.wait(*state.backs)

    def turn():
        partial_one, turned = chain.run(
            lambda *p: turn_back(
                plan, slot_parent, place, cosine, sine, (w_query, w_key, w_value), p
            ),
            *state.backs,
        )
        state.one = lax.psum_scatter(partial_one, "tensor", scatter_dimension=0, tiled=True)
        qkv.lhs, qkv.rhs = [normed_one], [turned]

    def residual():
        state.output = chain.run(lambda p: add_residual(plan, middles, p), state.part)

    def tokens_step():
        grad_own = chain.run(
            lambda g: tokens_back(plan, place, g, tokens, state.grad_middle), state.one
        )
        state.tokens = lax.all_gather(grad_own, "tensor", axis=0, tiled=True)

    def gathered():
        state.tokens = chain.wait(state.tokens)

    def ring_start():
        state.ring = RingSum(plan, chain, chain.after(*state.out))

    def ring_end():
        got, mine = chain.wait(*state.ring.finish())
        state.out = chain.run(add_last, got, mine)

    def ring_step():
        state.ring.step()

    down.away()
    gate.away()
    Chain.weight = 0.3
    down.keep()
    Chain.weight = 1.0
    down.send()
    output()
    own()
    branch()
    scatter()
    out.away()
    gate.keep()
    out.keep()
    down.wait()
    heads()
    out.send()
    attend_step()
    out.wait()
    sum_far()
    out.add()
    sum_near()
    gate.send()
    down.add()
    up.away()
    arrive()
    turn()
    up.took()
    out.send()
    qkv.away()
    up.keep()
    Chain.weight = 0.3
    up.send()
    Chain.weight = 1.0
    gate.wait()
    state.out = out.finish()
    gate.add()
    qkv.keep()
    residual()
    down.send()
    up.wait()
    tokens_step()
    ring_start()
    gate.send()
    state.ring.step()
    qkv.send()
    down.wait()
    up.add()
    gate.wait()
    state.ring.step()
    state.down = down.finish()
    up.send()
    state.gate = gate.finish()
    qkv.wait()
    qkv.add()
    qkv.send()
    state.up = up.finish()
    ring_end()
    state.qkv = qkv.finish()
    grad_tokens = (
        state.tokens
        .reshape(plan.tensor, plan.groups, plan.share, plan.width)
        .transpose(1, 0, 2, 3)
        .reshape(plan.rows, plan.width)
    )
    return (
        state.output,
        grad_tokens,
        *state.qkv,
        state.out,
        state.gate,
        state.up,
        state.down,
    )


def solution(mesh):
    in_specs = (
        P("dp", None),
        P(None, "tensor"),
        P(None, "tensor"),
        P(None, "tensor"),
        P("tensor", None),
        P(None, "tensor"),
        P(None, "tensor"),
        P("tensor", None),
        P("dp", None),
        P(),
    )
    out_specs = (
        P("dp", None),
        P("dp", None),
        P("dp", "tensor"),
        P("dp", "tensor"),
        P("dp", "tensor"),
        P("tensor", "dp"),
        P("dp", "tensor"),
        P("dp", "tensor"),
        P("tensor", "dp"),
    )
    return jax.shard_map(
        functools.partial(body, mesh),
        mesh=mesh,
        in_specs=in_specs,
        out_specs=out_specs,
        check_vma=False,
    )
```
